32 devices in a mesh: seq: 16 (over z, x, core), head: 2 (over y).
Axes of the slice: x: 2, y: 2, z: 4, core: 2. Of those that a mesh axis runs over, the one named last changes fastest.
Arguments:
- span_query: bfloat16 [2048, 8192], P('seq', 'head'), may hold values from -8 to 8
- span_kv: bfloat16 [2048, 2048], P('seq', 'head'), may hold values from -6 to 6
- prefix_cache: bfloat16 [32, 64, 2048], P('seq', None, 'head'), may hold values from -6 to 6
- prefix_len: int32 [2], replicated, may hold values from 256 to 1024, as said below
- block_owner: int32 [2, 16], replicated, may hold values from 0 to 15, as said below
Outputs:
- attended: bfloat16 [2048, 8192], P(('seq', 'head'))
The draws below stay inside these ranges and needn't reach their ends.
Inputs may be any that keep to these rules, and one draw needn't show every extreme that they name: `prefix_len`: some request's prefix has exactly 1024 tokens in every draw. `block_owner`: each row is a permutation of the seq devices: every device holds one page slot for each request, used or not.
All inputs are finite; a program needn't handle non-finite values.
Results may differ from the reference program's by a relative error of at most 0.0065.
Values may be sent and summed in bfloat16 or wider, within the bound.
No kernel may reach another device: no remote copies, remote signals or barrier semaphores. Data moves between devices by JAX's collectives and lax.ppermute only.
A program may use at most 64 MiB of HBM per device.

```python
import math
import jax
import jax.numpy as jnp
from jax import lax

QH = 64
KVH = 8
HD = 128
REQS = 2
BLK = 64
TOKENS = 2048
SPAN = 1024
PREFIX_MAX = 1024
CACHE_SLOTS = 32
N_SEQ = 16


def layout(key):
    key_lengths = jax.random.fold_in(key, 101)
    key_chosen = jax.random.fold_in(key, 102)
    key_table = jax.random.fold_in(key, 103)
    lengths = jax.random.randint(key_lengths, (REQS,), PREFIX_MAX // 4, PREFIX_MAX + 1)
    chosen = jax.random.randint(key_chosen, (), 0, REQS)
    lengths = jnp.where(jnp.arange(REQS) == chosen, PREFIX_MAX, lengths).astype(jnp.int32)
    owner_table = jax.vmap(lambda subkey: jax.random.permutation(subkey, N_SEQ))(jax.random.split(key_table, REQS))
    return (lengths, owner_table.astype(jnp.int32))


def draw_prefix_len(key, part):
    shared = layout(key)
    return shared[0]


def draw_block_owner(key, part):
    shared = layout(key)
    return shared[1]


def draw_span_query(key, part):
    key = jax.random.fold_in(key, 3)
    shape = (TOKENS, KVH, QH // KVH, HD)
    values = jnp.clip(jax.random.normal(key, shape, jnp.float32), -6.0, 6.0)
    return values.reshape(TOKENS, QH * HD).astype(jnp.bfloat16)


def draw_prefix_cache(key, part):
    key = jax.random.fold_in(key, 4)
    shape = (CACHE_SLOTS, BLK, KVH, 2, HD)
    values = jnp.clip(jax.random.normal(key, shape, jnp.float32), -6.0, 6.0)
    return values.reshape(CACHE_SLOTS, BLK, KVH * 2 * HD).astype(jnp.bfloat16)


def steps_of(rng, extent, cuts, low, largest):
    factor_of, own = 1.0, jax.random.fold_in(rng, 6)
    for dim, parts in cuts:
        steps = jnp.exp(jax.random.uniform(jax.random.fold_in(own, dim), (parts,), jnp.float32, low / len(cuts), largest / len(cuts)))
        factor_of = factor_of * jnp.repeat(steps, extent[dim] // parts).reshape([-1 if axis == dim else 1 for axis in range(len(extent))])
    return factor_of


def scatter_about(own_key, dims, deviation, reach, cuts=(), held_as=jnp.bfloat16):
    factor_of = steps_of(own_key, dims, cuts, -0.22, 0.18) if cuts else 1.0
    values = jax.random.normal(own_key, dims, jnp.float32) * deviation * factor_of
    return jnp.minimum(jnp.maximum(values, -reach), reach).astype(held_as)


def setup_inputs(seed: int = 0) -> dict:
    seeds = jax.random.split(jax.random.key(seed), 6)
    return {
        "span_query": draw_span_query(jax.random.fold_in(seeds[5], 71), 0),
        "span_kv": scatter_about(seeds[1], (TOKENS, KVH * 2 * HD), 1.0, 6.0, ((0, 16), (1, 2))),
        "prefix_cache": draw_prefix_cache(jax.random.fold_in(seeds[5], 71), 0),
        "prefix_len": draw_prefix_len(jax.random.fold_in(seeds[5], 71), 0),
        "block_owner": draw_block_owner(jax.random.fold_in(seeds[5], 71), 0),
    }


def reference(span_query, span_kv, prefix_cache, prefix_len, block_owner):
    score_scale = HD ** -0.5
    per_group = QH // KVH
    query_block = math.gcd(SPAN, 256)
    block_total = SPAN // query_block
    prefix_tokens = N_SEQ * BLK
    cache = prefix_cache.reshape(CACHE_SLOTS, BLK, KVH, 2, HD)
    span_rows = span_kv.reshape(TOKENS, KVH, 2, HD)
    all_queries = span_query.reshape(TOKENS, KVH, per_group, HD)
    results = []
    for request in range(REQS):
        page_rows = (block_owner[request] * REQS + request).astype(jnp.int32)
        prefix_rows = cache[page_rows].reshape(prefix_tokens, KVH, 2, HD)
        own_span = span_rows[request * SPAN:(request + 1) * SPAN]
        key_rows = jnp.concatenate([prefix_rows, own_span], axis=0)
        queries = all_queries[request * SPAN:(request + 1) * SPAN]
        queries = queries.reshape(block_total, query_block, KVH, per_group, HD)
        prefix_limit = prefix_len[request]

        def per_head(pair_args):
            head_queries, head_rows = pair_args
            key_float = head_rows[:, 0].astype(jnp.float32)
            value_float = head_rows[:, 1].astype(jnp.float32)

            def per_block(block_args):
                block_queries, block_id = block_args
                query_ids = block_id * query_block + jnp.arange(query_block, dtype=jnp.int32)
                prefix_seen = jnp.arange(prefix_tokens, dtype=jnp.int32) < prefix_limit
                span_seen = jnp.arange(SPAN, dtype=jnp.int32)[None, :] <= query_ids[:, None]
                visible = jnp.concatenate([jnp.broadcast_to(prefix_seen[None, :], (query_block, prefix_tokens)), span_seen], axis=1)
                scores = jnp.einsum('qgd,kd->qgk', block_queries.astype(jnp.float32), key_float) * score_scale
                live = visible[:, None, :]
                scores = jnp.where(live, scores, jnp.float32(-1e30))
                row_max = jnp.max(scores, axis=-1, keepdims=True)
                weights = jnp.where(live, jnp.exp(scores - row_max), jnp.float32(0.0))
                total = jnp.sum(weights, axis=-1)
                rounded = weights.astype(jnp.bfloat16)
                numerator = jnp.einsum('qgk,kd->qgd', rounded.astype(jnp.float32), value_float)
                return (numerator / total[:, :, None]).astype(jnp.bfloat16)

            return lax.map(per_block, (head_queries, jnp.arange(block_total, dtype=jnp.int32)))

        per_heads = lax.map(per_head, (queries.transpose(2, 0, 1, 3, 4), key_rows.transpose(1, 0, 2, 3)))
        results.append(per_heads.transpose(1, 2, 0, 3, 4).reshape(SPAN, QH * HD))
    return jnp.concatenate(results, axis=0)
```

```python
import functools
import math

import jax
import jax.numpy as jnp
from jax import lax
from jax.experimental import pallas as pl
from jax.experimental.pallas import tpu as pltpu
from jax.sharding import PartitionSpec as P

QH = 64
KVH = 8
HD = 128
REQS = 2
PER_GROUP = QH // KVH
EXP2_SCALE = HD ** (-0.5) * math.log2(math.e)
MASKED = -1e30


def swap(value, bit):
    count = lax.axis_size("seq")
    return lax.ppermute(value, "seq", [(source, source ^ bit) for source in range(count)])


def hypercube_order(bits):
    order = [0]
    for bit in bits:
        order = order + [offset ^ bit for offset in order]
    return order


def gather_half(own, bits):
    pieces = [own]
    for bit in bits:
        pieces.append(swap(pieces[0] if len(pieces) == 1 else jnp.concatenate(pieces, axis=0), bit))
    return pieces


def attend_kernel(spec, place_ref, limit_ref, owner_ref, q_ref, *refs):
    tokens, page, chunk, groups, piece_sizes, orders, group_size = spec
    piece_count = len(piece_sizes)
    halves = [refs[:piece_count], refs[piece_count : 2 * piece_count]]
    out_ref = refs[2 * piece_count]
    page_seen, keys, values, scores, weights = refs[2 * piece_count + 1 :]
    half_cols = groups * HD
    chunks = len(orders[0])
    total_keys = chunks * chunk
    me = place_ref[0]
    request = me // group_size

    def note_page(index, carry):
        page_seen[owner_ref[request, index]] = jnp.clip(limit_ref[request] - index * page, 0, page)
        return carry

    lax.fori_loop(0, owner_ref.shape[1], note_page, 0)

    row = lax.broadcasted_iota(jnp.int32, (chunk, HD), 0)
    lane = lax.broadcasted_iota(jnp.int32, (chunk, HD), 1)
    for at, offset in enumerate(orders[0]):
        source = me ^ offset
        span_seen = jnp.where(source <= me, tokens, 0)
        seen = row < span_seen
        for which in range((chunk - tokens) // page):
            start = tokens + which * page
            count = page_seen[source ^ (which * group_size)]
            seen = seen | ((row >= start) & (row < start + count))
        bias = jnp.where(seen | (lane > 0), jnp.float32(0.0), jnp.float32(MASKED))
        keys[pl.ds(at * chunk, chunk), HD:] = bias.astype(jnp.bfloat16)
    values[:, HD:] = jnp.ones((total_keys, HD), jnp.bfloat16)

    pair = 2 * tokens
    ones = (lax.broadcasted_iota(jnp.int32, (pair, HD), 1) == 0).astype(jnp.bfloat16)
    causal = lax.broadcasted_iota(jnp.int32, (pair, tokens), 1) <= (
        lax.broadcasted_iota(jnp.int32, (pair, tokens), 0) % tokens
    )

    def fill(target, column):
        half, start = divmod(column, half_cols)
        order = orders[half]
        at = 0
        for piece, size in zip(halves[half], piece_sizes):
            for inner in range(size):
                slot = orders[0].index(order[at])
                target[pl.ds(slot * chunk, chunk), :HD] = piece[
                    pl.ds(inner * chunk, chunk), pl.ds(start, HD)
                ]
                at += 1

    for group in range(groups):
        fill(keys, group * 2 * HD)
        fill(values, group * 2 * HD + HD)

        def one_pair(index, carry):
            first = pl.multiple_of((group * PER_GROUP + index * 2) * HD, HD)
            second = pl.multiple_of(first + HD, HD)
            both = jnp.concatenate([q_ref[:, pl.ds(first, HD)], q_ref[:, pl.ds(second, HD)]], axis=0)
            query = jnp.concatenate([both, ones], axis=1)
            top = jnp.full((pair, HD), MASKED, jnp.float32)
            for at in range(chunks):
                part = lax.dot_general(
                    query,
                    keys[pl.ds(at * chunk, chunk), :],
                    (((1,), (1,)), ((), ())),
                    preferred_element_type=jnp.float32,
                )
                if at == 0:
                    part = jnp.concatenate(
                        [jnp.where(causal, part[:, :tokens], MASKED), part[:, tokens:]], axis=1
                    )
                scores[:, pl.ds(at * chunk, chunk)] = part
                for lane_at in range(0, chunk, HD):
                    top = jnp.maximum(top, part[:, lane_at : lane_at + HD])
            top = jnp.max(top, axis=1, keepdims=True)
            for at in range(chunks):
                part = scores[:, pl.ds(at * chunk, chunk)]
                weights[:, pl.ds(at * chunk, chunk)] = jnp.exp2((part - top) * EXP2_SCALE).astype(
                    jnp.bfloat16
                )
            summed = jnp.dot(weights[...], values[...], preferred_element_type=jnp.float32)
            result = (summed[:, :HD] / summed[:, HD:]).astype(jnp.bfloat16)
            out_ref[:, pl.ds(first, HD)] = result[:tokens]
            out_ref[:, pl.ds(second, HD)] = result[tokens:]
            return carry

        lax.fori_loop(0, PER_GROUP // 2, one_pair, 0)


def attend(place, limits, owners, queries, halves, orders, tokens, page, group_size):
    columns = queries.shape[1]
    groups = columns // (PER_GROUP * HD)
    chunk = halves[0][0].shape[0]
    sizes = tuple(piece.shape[0] // chunk for piece in halves[0])
    total_keys = sum(sizes) * chunk
    spec = (tokens, page, chunk, groups, sizes, orders, group_size)
    whole = pl.BlockSpec(memory_space=pltpu.VMEM)
    scalars = pl.BlockSpec(memory_space=pltpu.SMEM)
    flops = 2 * tokens * columns * total_keys * 3
    return pl.pallas_call(
        functools.partial(attend_kernel, spec),
        out_shape=jax.ShapeDtypeStruct(queries.shape, jnp.bfloat16),
        in_specs=[scalars] * 3 + [whole] * (1 + 2 * len(sizes)),
        out_specs=whole,
        scratch_shapes=[
            pltpu.SMEM((owners.shape[1],), jnp.int32),
            pltpu.VMEM((total_keys, 2 * HD), jnp.bfloat16),
            pltpu.VMEM((total_keys, 2 * HD), jnp.bfloat16),
            pltpu.VMEM((2 * tokens, total_keys), jnp.float32),
            pltpu.VMEM((2 * tokens, total_keys), jnp.bfloat16),
        ],
        compiler_params=pltpu.CompilerParams(vmem_limit_bytes=48 * 1024 * 1024),
        cost_estimate=pl.CostEstimate(flops=flops, bytes_accessed=8 << 20, transcendentals=0),
    )(place, limits, owners, queries, *halves[0], *halves[1])


def body(span_query, span_kv, prefix_cache, prefix_len, block_owner):
    tokens = span_query.shape[0]
    seq_size = lax.axis_size("seq")
    group_size = seq_size // REQS
    me = lax.axis_index("seq").astype(jnp.int32)
    request = me // group_size
    page = prefix_cache.shape[1]
    own_page = lax.dynamic_index_in_dim(prefix_cache, request, 0, keepdims=False)
    other_page = lax.dynamic_index_in_dim(prefix_cache, 1 - request, 0, keepdims=False)
    crossed = swap(other_page, group_size)
    rows = jnp.concatenate([span_kv, own_page, crossed], axis=0)
    half_cols = rows.shape[1] // 2
    bits = [1 << at for at in range(group_size.bit_length() - 1)]
    bit_orders = (bits[1:] + bits[:1], bits[:0:-1] + bits[:1])
    halves = [
        gather_half(rows[:, :half_cols], bit_orders[0]),
        gather_half(rows[:, half_cols:], bit_orders[1]),
    ]
    orders = tuple(tuple(hypercube_order(order)) for order in bit_orders)
    result = attend(
        me.reshape(1), prefix_len, block_owner, span_query, halves, orders, tokens, page, group_size
    )
    return lax.all_to_all(result, "head", split_axis=0, concat_axis=1, tiled=True)


def solution(mesh):
    placed = (P("seq", "head"), P("seq", "head"), P("seq", None, "head"), P(), P())
    return jax.shard_map(
        body, mesh=mesh, in_specs=placed, out_specs=P(("seq", "head"), None), check_vma=False
    )
```

```python
import functools
import math

import jax
import jax.numpy as jnp
from jax import lax
from jax.experimental import pallas as pl
from jax.experimental.pallas import tpu as pltpu
from jax.sharding import PartitionSpec as P

QH = 64
KVH = 8
HD = 128
REQS = 2
PER_GROUP = QH // KVH
EXP2_SCALE = HD ** (-0.5) * math.log2(math.e)
MASKED = -1e30
SCORE_BYTES = 8 * 1024 * 1024


def swap(value, axis, bit):
    count = lax.axis_size(axis)
    return lax.ppermute(value, axis, [(source, source ^ bit) for source in range(count)])


def gather_strip(own, bits):
    pieces, offsets = [own], [0]
    places = [[0]]
    for bit in bits:
        sent = pieces[0] if len(pieces) == 1 else jnp.concatenate(pieces, axis=0)
        pieces.append(swap(sent, "seq", bit))
        places.append([offset ^ bit for offset in offsets])
        offsets = offsets + places[-1]
    return list(zip(pieces, places))


def attend_kernel(spec, place_ref, limit_ref, owner_ref, q_ref, *refs):
    tokens, page, chunk, groups, block_heads, group_size, head_size, strips, sources = spec
    piece_refs = refs[: sum(len(strip) for strip in strips)]
    refs = refs[len(piece_refs) :]
    outs, refs = refs[:2], refs[2:]
    page_seen, keys, values, scores_a, scores_b, top_a, top_b = refs
    chunks = group_size
    me = place_ref[0]
    my_head = place_ref[1]
    request = me // group_size

    def note_page(index, carry):
        page_seen[owner_ref[request, index]] = jnp.clip(limit_ref[request] - index * page, 0, page)
        return carry

    lax.fori_loop(0, owner_ref.shape[1], note_page, 0)

    row = lax.broadcasted_iota(jnp.int32, (chunk, HD), 0)
    lane = lax.broadcasted_iota(jnp.int32, (chunk, HD), 1)
    for offset in range(chunks):
        source = me ^ offset
        seen = row < jnp.where(source <= me, tokens, 0)
        for which in range((chunk - tokens) // page):
            start = tokens + which * page
            count = page_seen[source ^ (which * group_size)]
            seen = seen | ((row >= start) & (row < start + count))
        bias = jnp.where(seen | (lane > 0), jnp.float32(0.0), jnp.float32(MASKED))
        for group in range(groups):
            keys[group, pl.ds(offset * chunk, chunk), HD:] = bias.astype(jnp.bfloat16)
    values[:, :, HD:] = jnp.ones((groups, chunks * chunk, HD), jnp.bfloat16)

    def fill(target, group, strip_at, column):
        first = sum(len(strip) for strip in strips[:strip_at])
        for ref, places in zip(piece_refs[first:], strips[strip_at]):
            for inner, offset in enumerate(places):
                target[group, pl.ds(offset * chunk, chunk), :HD] = ref[
                    pl.ds(inner * chunk, chunk), pl.ds(column, HD)
                ]

    for group in range(groups):
        fill(keys, group, *sources[2 * group])
        fill(values, group, *sources[2 * group + 1])

    block = block_heads * tokens
    blocks_a_group = PER_GROUP // block_heads
    blocks = groups * blocks_a_group
    ones = (lax.broadcasted_iota(jnp.int32, (block, HD), 1) == 0).astype(jnp.bfloat16)
    causal = lax.broadcasted_iota(jnp.int32, (block, tokens), 1) <= (
        lax.broadcasted_iota(jnp.int32, (block, tokens), 0) % tokens
    )

    def columns(index):
        return [
            pl.ds(pl.multiple_of((index * block_heads + head) * HD, HD), HD)
            for head in range(block_heads)
        ]

    def score_steps(index, scores, top):
        group = index // blocks_a_group
        query = jnp.concatenate([q_ref[:, column] for column in columns(index)], axis=0)
        query = jnp.concatenate([query, ones], axis=1)
        best = jnp.full((block, HD), MASKED, jnp.float32)
        for at in range(chunks):
            part = lax.dot_general(
                query,
                keys[group, pl.ds(at * chunk, chunk), :],
                (((1,), (1,)), ((), ())),
                preferred_element_type=jnp.float32,
            )
            if at == 0:
                own = jnp.where(causal, part[:, :tokens], MASKED)
                part = jnp.concatenate([own, part[:, tokens:]], axis=1)
            scores[:, pl.ds(at * chunk, chunk)] = part
            for lane_at in range(0, chunk, HD):
                best = jnp.maximum(best, part[:, lane_at : lane_at + HD])
            yield
        top[...] = jnp.broadcast_to(jnp.max(best, axis=1, keepdims=True), (block, HD))

    def value_steps(index, scores, top):
        group = index // blocks_a_group
        summed = jnp.zeros((block, 2 * HD), jnp.float32)
        for at in range(chunks):
            weights = []
            for lane_at in range(at * chunk, (at + 1) * chunk, HD):
                shifted = scores[:, pl.ds(lane_at, HD)] - top[...]
                weights.append(jnp.exp2(shifted * EXP2_SCALE).astype(jnp.bfloat16))
            summed = summed + jnp.dot(
                jnp.concatenate(weights, axis=1),
                values[group, pl.ds(at * chunk, chunk), :],
                preferred_element_type=jnp.float32,
            )
            yield
        result = (summed[:, :HD] / summed[:, HD:]).astype(jnp.bfloat16)
        kept = tokens // head_size
        for head, column in enumerate(columns(index)):
            one = result[head * tokens : (head + 1) * tokens]
            if head_size == 2:
                low, high = one[:kept], one[kept:]
                outs[0][:, column] = jnp.where(my_head == 0, low, high)
                outs[1][:, column] = jnp.where(my_head == 0, high, low)
            else:
                outs[0][:, column] = one[:kept]
                outs[1][:, column] = one[kept:]

    def run(*steps):
        live = list(steps)
        while live:
            for step in list(live):
                if next(step, live) is live:
                    live.remove(step)

    run(score_steps(0, scores_a, top_a))

    def two_blocks(index, carry):
        run(score_steps(2 * index + 1, scores_b, top_b), value_steps(2 * index, scores_a, top_a))
        ahead = jnp.minimum(2 * index + 2, blocks - 1)
        run(score_steps(ahead, scores_a, top_a), value_steps(2 * index + 1, scores_b, top_b))
        return carry

    lax.fori_loop(0, blocks // 2, two_blocks, 0)


def attend(place, limits, owners, queries, part, strips, sources, page, group_size, head_size):
    tokens = queries.shape[0]
    columns = len(sources) // 2 * PER_GROUP * HD
    groups = columns // (PER_GROUP * HD)
    chunk = strips[0][0][0].shape[0]
    total_keys = group_size * chunk
    block_heads = 4
    while block_heads > 1 and block_heads * tokens * total_keys * 4 > SCORE_BYTES:
        block_heads //= 2
    block = block_heads * tokens
    offsets = tuple(tuple(tuple(places) for _, places in strip) for strip in strips)
    pieces = [piece for strip in strips for piece, _ in strip]
    spec = (tokens, page, chunk, groups, block_heads, group_size, head_size, offsets, sources)
    whole = pl.BlockSpec(memory_space=pltpu.VMEM)
    scalars = pl.BlockSpec(memory_space=pltpu.SMEM)
    kept = tokens // head_size
    return pl.pallas_call(
        functools.partial(attend_kernel, spec),
        grid=(1,),
        out_shape=[
            jax.ShapeDtypeStruct((kept, columns), jnp.bfloat16),
            jax.ShapeDtypeStruct((tokens - kept, columns), jnp.bfloat16),
        ],
        in_specs=[scalars] * 3
        + [pl.BlockSpec((tokens, columns), lambda step: (0, part))]
        + [whole] * len(pieces),
        out_specs=[whole] * 2,
        scratch_shapes=[
            pltpu.SMEM((owners.shape[1],), jnp.int32),
            pltpu.VMEM((groups, total_keys, 2 * HD), jnp.bfloat16),
            pltpu.VMEM((groups, total_keys, 2 * HD), jnp.bfloat16),
            pltpu.VMEM((block, total_keys), jnp.float32),
            pltpu.VMEM((block, total_keys), jnp.float32),
            pltpu.VMEM((block, HD), jnp.float32),
            pltpu.VMEM((block, HD), jnp.float32),
        ],
        compiler_params=pltpu.CompilerParams(vmem_limit_bytes=48 * 1024 * 1024),
        cost_estimate=pl.CostEstimate(
            flops=8 * tokens * columns * total_keys,
            bytes_accessed=4 * tokens * columns + 2 * total_keys * columns // PER_GROUP,
            transcendentals=0,
        ),
    )(place, limits, owners, queries, *pieces)


def body(span_query, span_kv, prefix_cache, prefix_len, block_owner):
    seq_size = lax.axis_size("seq")
    head_size = lax.axis_size("head")
    group_size = seq_size // REQS
    me = lax.axis_index("seq").astype(jnp.int32)
    my_head = lax.axis_index("head").astype(jnp.int32)
    request = me // group_size
    page = prefix_cache.shape[1]
    own_page = lax.dynamic_index_in_dim(prefix_cache, request, 0, keepdims=False)
    other_page = lax.dynamic_index_in_dim(prefix_cache, 1 - request, 0, keepdims=False)
    crossed = swap(other_page, "seq", group_size)
    rows = jnp.concatenate([span_kv, own_page, crossed], axis=0)
    half_cols = rows.shape[1] // 2
    bits = [1 << at for at in range(group_size.bit_length() - 1)]
    bit_orders = (bits[1:] + bits[:1], bits[:0:-1] + bits[:1])
    strips = [
        gather_strip(rows[:, :half_cols], bit_orders[0]),
        gather_strip(rows[:, half_cols:], bit_orders[1]),
    ]
    groups = rows.shape[1] // (2 * HD)
    place = jnp.stack([me, my_head])
    common = (page, group_size, head_size)
    if groups % 2 or head_size != 2:
        sources = tuple(divmod(column, half_cols) for column in range(0, 2 * half_cols, HD))
        results = [
            attend(place, prefix_len, block_owner, span_query, 0, strips, sources, *common)
        ]
    else:
        sources = tuple((0, column) for column in range(0, half_cols, HD))
        results = [
            attend(
                place,
                prefix_len,
                block_owner,
                span_query,
                at,
                [strips[at]],
                sources,
                *common,
            )
            for at in range(2)
        ]
    if head_size != 2:
        joined = jnp.concatenate([jnp.concatenate(pair, axis=0) for pair in results], axis=1)
        return lax.all_to_all(joined, "head", split_axis=0, concat_axis=1, tiled=True)
    kept = [pair[0] for pair in results]
    received = [swap(pair[1], "head", 1) for pair in results]
    joined = jnp.concatenate(kept + kept, axis=1)
    start = (1 - my_head) * span_query.shape[1]
    for one in received:
        joined = lax.dynamic_update_slice(joined, one, (0, start))
        start = start + one.shape[1]
    return joined


def solution(mesh):
    placed = (P("seq", "head"), P("seq", "head"), P("seq", None, "head"), P(), P())
    return jax.shard_map(
        body, mesh=mesh, in_specs=placed, out_specs=P(("seq", "head"), None), check_vma=False
    )
```

```python
import functools
import math

import jax
import jax.numpy as jnp
from jax import lax
from jax.experimental import pallas as pl
from jax.experimental.pallas import tpu as pltpu
from jax.sharding import PartitionSpec as P

QH = 64
KVH = 8
HD = 128
REQS = 2
PER_GROUP = QH // KVH
EXP2_SCALE = HD ** (-0.5) * math.log2(math.e)
MASKED = -1e30
SCORE_BYTES = 8 * 1024 * 1024
KEY_CHUNK = 256
SPAN_ROWS, OWN_PAGE, CROSSED_PAGE = range(3)


def hop(value, bit_of_core):
    count = lax.axis_size("seq")
    return lax.ppermute(
        value, "seq", [(source, source ^ bit_of_core[source % 2]) for source in range(count)]
    )


def shifted(layout, slots):
    return [(slot + slots, kind, rows) for slot, kind, rows in layout]


def hypercube_order(bits):
    order = [0]
    for bit in bits:
        order = order + [offset ^ bit for offset in order]
    return order


def attend_kernel(spec, block_heads, groups, place_ref, limit_ref, owner_ref, q_ref, *refs):
    tokens, page, group_size, head_size, orders, layout = spec
    halves, outs, refs = refs[:2], refs[2:4], refs[4:]
    page_seen, keys, values, scores_a, scores_b, top_a, top_b = refs
    half_keys = halves[0].shape[0]
    chunk = min(KEY_CHUNK, 2 * half_keys)
    chunks = 2 * half_keys // chunk
    me = place_ref[0]
    my_head = place_ref[1]
    request = me // group_size

    def note_page(index, carry):
        page_seen[owner_ref[request, index]] = jnp.clip(limit_ref[request] - index * page, 0, page)
        return carry

    lax.fori_loop(0, owner_ref.shape[1], note_page, 0)

    offsets = [hypercube_order(order) for order in orders]
    for half in range(2):
        holder = me ^ half
        start = half * half_keys
        for slot, kind, rows in layout:
            source = holder ^ jnp.where(holder % 2 == 0, offsets[0][slot], offsets[1][slot])
            if kind == SPAN_ROWS:
                count = jnp.where(source <= me, tokens, 0)
            elif kind == OWN_PAGE:
                count = page_seen[source]
            else:
                count = page_seen[source ^ group_size]
            row = lax.broadcasted_iota(jnp.int32, (rows, HD), 0)
            lane = lax.broadcasted_iota(jnp.int32, (rows, HD), 1)
            bias = jnp.where((row < count) | (lane > 0), jnp.float32(0.0), jnp.float32(MASKED))
            for group in range(groups):
                keys[group, pl.ds(start, rows), HD:] = bias.astype(jnp.bfloat16)
            start += rows
    values[:, :, HD:] = jnp.ones((groups, 2 * half_keys, HD), jnp.bfloat16)

    for group in range(groups):
        for half, ref in enumerate(halves):
            at = pl.ds(half * half_keys, half_keys)
            keys[group, at, :HD] = ref[:, pl.ds(2 * group * HD, HD)]
            values[group, at, :HD] = ref[:, pl.ds((2 * group + 1) * HD, HD)]

    block = block_heads * tokens
    blocks_a_group = PER_GROUP // block_heads
    blocks = groups * blocks_a_group
    ones = (lax.broadcasted_iota(jnp.int32, (block, HD), 1) == 0).astype(jnp.bfloat16)
    causal = lax.broadcasted_iota(jnp.int32, (block, tokens), 1) <= (
        lax.broadcasted_iota(jnp.int32, (block, tokens), 0) % tokens
    )

    def columns(index):
        return [
            pl.ds(pl.multiple_of((index * block_heads + head) * HD, HD), HD)
            for head in range(block_heads)
        ]

    def score_steps(index, scores, top):
        group = index // blocks_a_group
        query = jnp.concatenate([q_ref[:, column] for column in columns(index)], axis=0)
        query = jnp.concatenate([query, ones], axis=1)
        best = jnp.full((block, HD), MASKED, jnp.float32)
        for at in range(chunks):
            part = lax.dot_general(
                query,
                keys[group, pl.ds(at * chunk, chunk), :],
                (((1,), (1,)), ((), ())),
                preferred_element_type=jnp.float32,
            )
            if at == 0:
                own = jnp.where(causal, part[:, :tokens], MASKED)
                part = jnp.concatenate([own, part[:, tokens:]], axis=1)
            scores[:, pl.ds(at * chunk, chunk)] = part
            for lane_at in range(0, chunk, HD):
                best = jnp.maximum(best, part[:, lane_at : lane_at + HD])
            yield
        top[...] = jnp.broadcast_to(jnp.max(best, axis=1, keepdims=True), (block, HD))

    def value_steps(index, scores, top):
        group = index // blocks_a_group
        summed = jnp.zeros((block, 2 * HD), jnp.float32)
        for at in range(chunks):
            weights = []
            for lane_at in range(at * chunk, (at + 1) * chunk, HD):
                shifted = scores[:, pl.ds(lane_at, HD)] - top[...]
                weights.append(jnp.exp2(shifted * EXP2_SCALE).astype(jnp.bfloat16))
            summed = summed + jnp.dot(
                jnp.concatenate(weights, axis=1),
                values[group, pl.ds(at * chunk, chunk), :],
                preferred_element_type=jnp.float32,
            )
            yield
        result = (summed[:, :HD] / summed[:, HD:]).astype(jnp.bfloat16)
        kept = tokens // head_size
        for head, column in enumerate(columns(index)):
            one = result[head * tokens : (head + 1) * tokens]
            if head_size == 2:
                low, high = one[:kept], one[kept:]
                outs[0][:, column] = jnp.where(my_head == 0, low, high)
                outs[1][:, column] = jnp.where(my_head == 0, high, low)
            else:
                outs[0][:, column] = one[:kept]
                outs[1][:, column] = one[kept:]

    def run(*steps):
        live = list(steps)
        while live:
            for step in list(live):
                if next(step, live) is live:
                    live.remove(step)

    run(score_steps(0, scores_a, top_a))

    def two_blocks(index, carry):
        run(score_steps(2 * index + 1, scores_b, top_b), value_steps(2 * index, scores_a, top_a))
        ahead = jnp.minimum(2 * index + 2, blocks - 1)
        run(score_steps(ahead, scores_a, top_a), value_steps(2 * index + 1, scores_b, top_b))
        return carry

    lax.fori_loop(0, blocks // 2, two_blocks, 0)


def attend(place, limits, owners, queries, part, mine, theirs, spec):
    tokens, _, _, head_size = spec[:4]
    total_keys, columns = 2 * mine.shape[0], mine.shape[1] // 2 * PER_GROUP
    groups = columns // (PER_GROUP * HD)
    block_heads = 4
    while block_heads > 1 and block_heads * tokens * total_keys * 4 > SCORE_BYTES:
        block_heads //= 2
    block = block_heads * tokens
    whole = pl.BlockSpec(memory_space=pltpu.VMEM)
    scalars = pl.BlockSpec(memory_space=pltpu.SMEM)
    kept = tokens // head_size
    return pl.pallas_call(
        functools.partial(attend_kernel, spec, block_heads, groups),
        grid=(1,),
        out_shape=[
            jax.ShapeDtypeStruct((kept, columns), jnp.bfloat16),
            jax.ShapeDtypeStruct((tokens - kept, columns), jnp.bfloat16),
        ],
        in_specs=[scalars] * 3
        + [pl.BlockSpec((tokens, columns), lambda step: (0, part))]
        + [whole] * 2,
        out_specs=[whole] * 2,
        scratch_shapes=[
            pltpu.SMEM((owners.shape[1],), jnp.int32),
            pltpu.VMEM((groups, total_keys, 2 * HD), jnp.bfloat16),
            pltpu.VMEM((groups, total_keys, 2 * HD), jnp.bfloat16),
            pltpu.VMEM((block, total_keys), jnp.float32),
            pltpu.VMEM((block, total_keys), jnp.float32),
            pltpu.VMEM((block, HD), jnp.float32),
            pltpu.VMEM((block, HD), jnp.float32),
        ],
        compiler_params=pltpu.CompilerParams(vmem_limit_bytes=48 * 1024 * 1024),
        cost_estimate=pl.CostEstimate(
            flops=8 * tokens * columns * total_keys,
            bytes_accessed=4 * tokens * columns + 2 * total_keys * columns // PER_GROUP,
            transcendentals=0,
        ),
    )(place, limits, owners, queries, mine, theirs)


def body(span_query, span_kv, prefix_cache, prefix_len, block_owner):
    seq_size = lax.axis_size("seq")
    head_size = lax.axis_size("head")
    group_size = seq_size // REQS
    me = lax.axis_index("seq").astype(jnp.int32)
    my_head = lax.axis_index("head").astype(jnp.int32)
    request = me // group_size
    tokens = span_kv.shape[0]
    page = prefix_cache.shape[1]
    columns = span_kv.shape[1]
    groups = columns // (2 * HD)
    parts = 2 if groups % 2 == 0 else 1
    part_columns = columns // parts
    bits = [1 << at for at in range(1, group_size.bit_length() - 1)]
    orders = (bits, bits[::-1])

    other_page = lax.dynamic_index_in_dim(prefix_cache, 1 - request, 0, keepdims=False)
    own_page = lax.dynamic_index_in_dim(prefix_cache, request, 0, keepdims=False)
    early = [jnp.concatenate([span_kv, own_page], axis=0)]
    early_rows = [[(0, SPAN_ROWS, tokens), (0, OWN_PAGE, page)]]
    late = [hop(other_page, (group_size, group_size))]
    late_rows = [[(0, CROSSED_PAGE, page)]]
    slots = 1
    first = (orders[0][0], orders[1][0])
    early.append(hop(early[0], first))
    late.append(hop(late[0], first))
    early_rows.append(shifted(early_rows[0], slots))
    late_rows.append(shifted(late_rows[0], slots))
    slots *= 2
    layout = sum(early_rows + late_rows, [])

    held = []
    for part in range(parts):
        cut = slice(part * part_columns, (part + 1) * part_columns)
        held.append(jnp.concatenate([piece[:, cut] for piece in early + late], axis=0))
    for pair in list(zip(*orders))[1:]:
        held = [jnp.concatenate([rows, hop(rows, pair)], axis=0) for rows in held]
        layout = layout + shifted(layout, slots)
        slots *= 2
    swapped = [hop(rows, (1, 1)) for rows in held]

    place = jnp.stack([me, my_head])
    spec = (tokens, page, group_size, head_size, orders, tuple(layout))
    results = [
        attend(place, prefix_len, block_owner, span_query, part, held[part], swapped[part], spec)
        for part in range(parts)
    ]
    if head_size != 2:
        joined = jnp.concatenate([jnp.concatenate(pair, axis=0) for pair in results], axis=1)
        return lax.all_to_all(joined, "head", split_axis=0, concat_axis=1, tiled=True)
    kept = [pair[0] for pair in results]
    received = [
        lax.ppermute(pair[1], "head", [(0, 1), (1, 0)]) for pair in results
    ]
    joined = jnp.concatenate(kept + kept, axis=1)
    start = (1 - my_head) * span_query.shape[1]
    for one in received:
        joined = lax.dynamic_update_slice(joined, one, (0, start))
        start = start + one.shape[1]
    return joined


def solution(mesh):
    placed = (P("seq", "head"), P("seq", "head"), P("seq", None, "head"), P(), P())
    return jax.shard_map(
        body, mesh=mesh, in_specs=placed, out_specs=P(("seq", "head"), None), check_vma=False
    )
```

```python
import functools
import math

import jax
import jax.numpy as jnp
from jax import lax
from jax.experimental import pallas as pl
from jax.experimental.pallas import tpu as pltpu
from jax.sharding import PartitionSpec as P

QH = 64
KVH = 8
HD = 128
REQS = 2
PER_GROUP = QH // KVH
EXP2_SCALE = HD ** (-0.5) * math.log2(math.e)
MASKED = -1e30
SCORE_BYTES = 8 * 1024 * 1024
KEY_CHUNK = 256
SPAN_ROWS, OWN_PAGE, CROSSED_PAGE = range(3)


def hop(value, bit_of_core):
    count = lax.axis_size("seq")
    return lax.ppermute(
        value, "seq", [(source, source ^ bit_of_core[source % 2]) for source in range(count)]
    )


def after(first, value):
    return lax.optimization_barrier((first, value))[1]


def shifted(layout, slots):
    return [(slot + slots, kind, rows) for slot, kind, rows in layout]


def hypercube_order(bits):
    order = [0]
    for bit in bits:
        order = order + [offset ^ bit for offset in order]
    return order


def attend_kernel(spec, layout, part, block_heads, groups, place_ref, limit_ref, owner_ref, q_ref, *refs):
    tokens, page, group_size, head_size, orders = spec
    first_phase = layout[0][1] == SPAN_ROWS
    halves, refs = refs[:2], refs[2:]
    if first_phase:
        (state_sum, state_top), refs = refs[:2], refs[2:]
    else:
        (state_sum, state_top), outs, refs = refs[:2], refs[2:4], refs[4:]
    page_seen, keys, values, scores_a, scores_b, top_a, top_b = refs
    half_keys = halves[0].shape[0]
    chunk = min(KEY_CHUNK, 2 * half_keys)
    chunks = 2 * half_keys // chunk
    me = place_ref[0]
    my_head = place_ref[1]
    request = me // group_size

    def note_page(index, carry):
        page_seen[owner_ref[request, index]] = jnp.clip(limit_ref[request] - index * page, 0, page)
        return carry

    if not first_phase:
        lax.fori_loop(0, owner_ref.shape[1], note_page, 0)

    offsets = [hypercube_order(order) for order in orders]
    for half in range(2):
        holder = me ^ half
        start = half * half_keys
        for slot, kind, rows in layout:
            source = holder ^ jnp.where(holder % 2 == 0, offsets[0][slot], offsets[1][slot])
            if kind == SPAN_ROWS:
                count = jnp.where(source <= me, tokens, 0)
            elif kind == OWN_PAGE:
                count = page_seen[source]
            else:
                count = page_seen[source ^ group_size]
            row = lax.broadcasted_iota(jnp.int32, (rows, HD), 0)
            lane = lax.broadcasted_iota(jnp.int32, (rows, HD), 1)
            bias = jnp.where((row < count) | (lane > 0), jnp.float32(0.0), jnp.float32(MASKED))
            for group in range(groups):
                keys[group, pl.ds(start, rows), HD:] = bias.astype(jnp.bfloat16)
            start += rows
    values[:, :, HD:] = jnp.ones((groups, 2 * half_keys, HD), jnp.bfloat16)

    for group in range(groups):
        for half, ref in enumerate(halves):
            at = pl.ds(half * half_keys, half_keys)
            column = (part * groups + group) * 2 * HD
            keys[group, at, :HD] = ref[:, pl.ds(column, HD)]
            values[group, at, :HD] = ref[:, pl.ds(column + HD, HD)]

    block = block_heads * tokens
    blocks_a_group = PER_GROUP // block_heads
    blocks = groups * blocks_a_group
    ones = (lax.broadcasted_iota(jnp.int32, (block, HD), 1) == 0).astype(jnp.bfloat16)
    causal = lax.broadcasted_iota(jnp.int32, (block, tokens), 1) <= (
        lax.broadcasted_iota(jnp.int32, (block, tokens), 0) % tokens
    )

    def columns(index, first):
        return [
            pl.ds(pl.multiple_of(first + (index * block_heads + head) * HD, HD), HD)
            for head in range(block_heads)
        ]

    def block_rows(index):
        return pl.ds(pl.multiple_of(index * block, block), block)

    def score_steps(index, scores, top):
        group = index // blocks_a_group
        first = part * groups * PER_GROUP * HD
        query = jnp.concatenate([q_ref[:, column] for column in columns(index, first)], axis=0)
        query = jnp.concatenate([query, ones], axis=1)
        if first_phase:
            best = jnp.full((block, HD), MASKED, jnp.float32)
        else:
            best = state_top[block_rows(index), :]
        for at in range(chunks):
            made = lax.dot_general(
                query,
                keys[group, pl.ds(at * chunk, chunk), :],
                (((1,), (1,)), ((), ())),
                preferred_element_type=jnp.float32,
            )
            if at == 0 and first_phase:
                own = jnp.where(causal, made[:, :tokens], MASKED)
                made = jnp.concatenate([own, made[:, tokens:]], axis=1)
            scores[:, pl.ds(at * chunk, chunk)] = made
            for lane_at in range(0, chunk, HD):
                best = jnp.maximum(best, made[:, lane_at : lane_at + HD])
            yield
        top[...] = jnp.broadcast_to(jnp.max(best, axis=1, keepdims=True), (block, HD))

    def value_steps(index, scores, top):
        group = index // blocks_a_group
        if first_phase:
            summed = jnp.zeros((block, 2 * HD), jnp.float32)
        else:
            fade = jnp.exp2((state_top[block_rows(index), :] - top[...]) * EXP2_SCALE)
            summed = state_sum[block_rows(index), :] * jnp.concatenate([fade, fade], axis=1)
        for at in range(chunks):
            weights = []
            for lane_at in range(at * chunk, (at + 1) * chunk, HD):
                shifted = scores[:, pl.ds(lane_at, HD)] - top[...]
                weights.append(jnp.exp2(shifted * EXP2_SCALE).astype(jnp.bfloat16))
            summed = summed + jnp.dot(
                jnp.concatenate(weights, axis=1),
                values[group, pl.ds(at * chunk, chunk), :],
                preferred_element_type=jnp.float32,
            )
            yield
        if first_phase:
            state_sum[block_rows(index), :] = summed
            state_top[block_rows(index), :] = top[...]
            return
        result = (summed[:, :HD] / summed[:, HD:]).astype(jnp.bfloat16)
        kept = tokens // head_size
        for head, column in enumerate(columns(index, 0)):
            one = result[head * tokens : (head + 1) * tokens]
            if head_size == 2:
                low, high = one[:kept], one[kept:]
                outs[0][:, column] = jnp.where(my_head == 0, low, high)
                outs[1][:, column] = jnp.where(my_head == 0, high, low)
            else:
                outs[0][:, column] = one[:kept]
                outs[1][:, column] = one[kept:]

    def run(*steps):
        live = list(steps)
        while live:
            for step in list(live):
                if next(step, live) is live:
                    live.remove(step)

    run(score_steps(0, scores_a, top_a))

    def two_blocks(index, carry):
        run(score_steps(2 * index + 1, scores_b, top_b), value_steps(2 * index, scores_a, top_a))
        ahead = jnp.minimum(2 * index + 2, blocks - 1)
        run(score_steps(ahead, scores_a, top_a), value_steps(2 * index + 1, scores_b, top_b))
        return carry

    lax.fori_loop(0, blocks // 2, two_blocks, 0)


def attend(place, limits, owners, queries, part, parts, mine, theirs, layout, spec, state):
    tokens, _, _, head_size = spec[:4]
    total_keys = 2 * mine.shape[0]
    columns = queries.shape[1] // parts
    groups = columns // (PER_GROUP * HD)
    block_heads = 4
    while block_heads > 1 and block_heads * tokens * total_keys * 4 > SCORE_BYTES:
        block_heads //= 2
    block = block_heads * tokens
    rows = PER_GROUP * groups * tokens
    whole = pl.BlockSpec(memory_space=pltpu.VMEM)
    scalars = pl.BlockSpec(memory_space=pltpu.SMEM)
    kept = tokens // head_size
    if state is None:
        state = ()
        out_shape = [
            jax.ShapeDtypeStruct((rows, 2 * HD), jnp.float32),
            jax.ShapeDtypeStruct((rows, HD), jnp.float32),
        ]
    else:
        out_shape = [
            jax.ShapeDtypeStruct((kept, columns), jnp.bfloat16),
            jax.ShapeDtypeStruct((tokens - kept, columns), jnp.bfloat16),
        ]
    return pl.pallas_call(
        functools.partial(attend_kernel, spec, tuple(layout), part, block_heads, groups),
        out_shape=out_shape,
        in_specs=[scalars] * 3 + [whole] * (3 + len(state)),
        out_specs=[whole] * 2,
        scratch_shapes=[
            pltpu.SMEM((owners.shape[1],), jnp.int32),
            pltpu.VMEM((groups, total_keys, 2 * HD), jnp.bfloat16),
            pltpu.VMEM((groups, total_keys, 2 * HD), jnp.bfloat16),
            pltpu.VMEM((block, total_keys), jnp.float32),
            pltpu.VMEM((block, total_keys), jnp.float32),
            pltpu.VMEM((block, HD), jnp.float32),
            pltpu.VMEM((block, HD), jnp.float32),
        ],
        compiler_params=pltpu.CompilerParams(vmem_limit_bytes=40 * 1024 * 1024),
        cost_estimate=pl.CostEstimate(
            flops=8 * tokens * columns * total_keys,
            bytes_accessed=4 * tokens * columns + 2 * total_keys * columns // PER_GROUP,
            transcendentals=0,
        ),
    )(place, limits, owners, queries, mine, theirs, *state)


def body(span_query, span_kv, prefix_cache, prefix_len, block_owner):
    seq_size = lax.axis_size("seq")
    head_size = lax.axis_size("head")
    group_size = seq_size // REQS
    me = lax.axis_index("seq").astype(jnp.int32)
    my_head = lax.axis_index("head").astype(jnp.int32)
    request = me // group_size
    tokens = span_kv.shape[0]
    page = prefix_cache.shape[1]
    groups = span_kv.shape[1] // (2 * HD)
    parts = 2 if groups % 2 == 0 else 1
    bits = [1 << at for at in range(1, group_size.bit_length() - 1)]
    orders = (bits, bits[::-1])

    def send(rows, stage):
        return hop(rows, tuple(order[stage] for order in orders))

    def grown(layout, stage):
        return layout + shifted(layout, 1 << stage)

    stages = len(bits)
    other_page = lax.dynamic_index_in_dim(prefix_cache, 1 - request, 0, keepdims=False)
    crossed = hop(other_page, (group_size, group_size))
    own_page = lax.dynamic_index_in_dim(prefix_cache, request, 0, keepdims=False)
    span, span_layout = span_kv, [(0, SPAN_ROWS, tokens)]
    for stage in range(stages):
        received = send(span, stage)
        if stage == 0:
            crossed = after(received, crossed)
            pages = jnp.concatenate([own_page, crossed], axis=0)
            pages = jnp.concatenate([pages, send(pages, 0)], axis=0)
        elif stage == 1:
            received = after(pages, received)
        span, span_layout = jnp.concatenate([span, received], axis=0), grown(span_layout, stage)
    span_swapped = hop(span, (1, 1))

    place = jnp.stack([me, my_head])
    spec = (tokens, page, group_size, head_size, orders)
    common = (place, prefix_len, block_owner, span_query)
    states = [
        attend(*common, part, parts, span, span_swapped, span_layout, spec, None)
        for part in range(parts)
    ]

    page_layout = [(0, OWN_PAGE, page), (0, CROSSED_PAGE, page)]
    page_layout = grown(page_layout, 0)
    for stage in range(1, stages):
        received = send(pages, stage)
        if stage == stages - 1:
            received = after(states[0], received)
        pages, page_layout = jnp.concatenate([pages, received], axis=0), grown(page_layout, stage)
    pages_swapped = hop(pages, (1, 1))
    results = [
        attend(*common, part, parts, pages, pages_swapped, page_layout, spec, states[part])
        for part in range(parts)
    ]
    if head_size != 2:
        joined = jnp.concatenate([jnp.concatenate(pair, axis=0) for pair in results], axis=1)
        return lax.all_to_all(joined, "head", split_axis=0, concat_axis=1, tiled=True)
    kept = [pair[0] for pair in results]
    received = [lax.ppermute(pair[1], "head", [(0, 1), (1, 0)]) for pair in results]
    joined = jnp.concatenate(kept + kept, axis=1)
    start = (1 - my_head) * span_query.shape[1]
    for one in received:
        joined = lax.dynamic_update_slice(joined, one, (0, start))
        start = start + one.shape[1]
    return joined


def solution(mesh):
    placed = (P("seq", "head"), P("seq", "head"), P("seq", None, "head"), P(), P())
    return jax.shard_map(
        body, mesh=mesh, in_specs=placed, out_specs=P(("seq", "head"), None), check_vma=False
    )
```

```python
import functools
import math

import jax
import jax.numpy as jnp
from jax import lax
from jax.experimental import pallas as pl
from jax.experimental.pallas import tpu as pltpu
from jax.sharding import PartitionSpec as P

QH = 64
KVH = 8
HD = 128
REQS = 2
PER_GROUP = QH // KVH
EXP2_SCALE = HD ** (-0.5) * math.log2(math.e)
MASKED = -1e30
SCORE_BYTES = 8 * 1024 * 1024
KEY_CHUNK = 256
SPAN_ROWS, OWN_PAGE, CROSSED_PAGE = range(3)


def hop(value, bit_of_core):
    count = lax.axis_size("seq")
    return lax.ppermute(
        value, "seq", [(source, source ^ bit_of_core[source % 2]) for source in range(count)]
    )


def after(first, value):
    return lax.optimization_barrier((first, value))[1]


def shifted(layout, slots):
    return [(slot + slots, kind, rows) for slot, kind, rows in layout]


def hypercube_order(bits):
    order = [0]
    for bit in bits:
        order = order + [offset ^ bit for offset in order]
    return order


def attend_kernel(spec, layout, part, block_heads, groups, place_ref, limit_ref, owner_ref, q_ref, *refs):
    tokens, page, group_size, head_size, orders = spec
    first_phase = layout[0][1] == SPAN_ROWS
    halves, refs = refs[:2], refs[2:]
    if first_phase:
        (state_sum, state_top), refs = refs[:2], refs[2:]
    else:
        (state_sum, state_top), outs, refs = refs[:2], refs[2:4], refs[4:]
    page_seen, keys, values = refs[:3]
    scores, weights, tops = refs[3:5], refs[5:7], refs[7:10]
    half_keys = halves[0].shape[0]
    chunk = min(KEY_CHUNK, 2 * half_keys)
    chunks = 2 * half_keys // chunk
    me = place_ref[0]
    my_head = place_ref[1]
    request = me // group_size

    def note_page(index, carry):
        page_seen[owner_ref[request, index]] = jnp.clip(limit_ref[request] - index * page, 0, page)
        return carry

    if not first_phase:
        lax.fori_loop(0, owner_ref.shape[1], note_page, 0)

    offsets = [hypercube_order(order) for order in orders]
    for half in range(2):
        holder = me ^ half
        start = half * half_keys
        for slot, kind, rows in layout:
            source = holder ^ jnp.where(holder % 2 == 0, offsets[0][slot], offsets[1][slot])
            if kind == SPAN_ROWS:
                count = jnp.where(source <= me, tokens, 0)
            elif kind == OWN_PAGE:
                count = page_seen[source]
            else:
                count = page_seen[source ^ group_size]
            row = lax.broadcasted_iota(jnp.int32, (rows, HD), 0)
            lane = lax.broadcasted_iota(jnp.int32, (rows, HD), 1)
            bias = jnp.where((row < count) | (lane > 0), jnp.float32(0.0), jnp.float32(MASKED))
            for group in range(groups):
                keys[group, pl.ds(start, rows), HD:] = bias.astype(jnp.bfloat16)
            start += rows
    values[:, :, HD:] = jnp.ones((groups, 2 * half_keys, HD), jnp.bfloat16)

    for group in range(groups):
        for half, ref in enumerate(halves):
            at = pl.ds(half * half_keys, half_keys)
            column = (part * groups + group) * 2 * HD
            keys[group, at, :HD] = ref[:, pl.ds(column, HD)]
            values[group, at, :HD] = ref[:, pl.ds(column + HD, HD)]

    block = block_heads * tokens
    blocks_a_group = PER_GROUP // block_heads
    blocks = groups * blocks_a_group
    ones = (lax.broadcasted_iota(jnp.int32, (block, HD), 1) == 0).astype(jnp.bfloat16)
    causal = lax.broadcasted_iota(jnp.int32, (block, tokens), 1) <= (
        lax.broadcasted_iota(jnp.int32, (block, tokens), 0) % tokens
    )

    def columns(index, first):
        return [
            pl.ds(first + (index * block_heads + head) * HD, HD)
            for head in range(block_heads)
        ]

    def score_steps(index, scores, top):
        group = index // blocks_a_group
        first = part * groups * PER_GROUP * HD
        query = jnp.concatenate([q_ref[:, column] for column in columns(index, first)], axis=0)
        query = jnp.concatenate([query, ones], axis=1)
        if first_phase:
            best = jnp.full((block, HD), MASKED, jnp.float32)
        else:
            best = state_top[pl.ds(index * block, block), :]
        for at in range(chunks):
            made = lax.dot_general(
                query,
                keys[group, pl.ds(at * chunk, chunk), :],
                (((1,), (1,)), ((), ())),
                preferred_element_type=jnp.float32,
            )
            if at == 0 and first_phase:
                own = jnp.where(causal, made[:, :tokens], MASKED)
                made = jnp.concatenate([own, made[:, tokens:]], axis=1)
            scores[:, pl.ds(at * chunk, chunk)] = made
            for lane_at in range(0, chunk, HD):
                best = jnp.maximum(best, made[:, lane_at : lane_at + HD])
            yield
        top[...] = jnp.broadcast_to(jnp.max(best, axis=1, keepdims=True), (block, HD))

    def weight_steps(index, scores, top, weights):
        for at in range(chunks):
            for lane_at in range(at * chunk, (at + 1) * chunk, HD):
                shifted_score = scores[:, pl.ds(lane_at, HD)] - top[...]
                weights[:, pl.ds(lane_at, HD)] = jnp.exp2(shifted_score * EXP2_SCALE).astype(
                    jnp.bfloat16
                )
            yield

    def finish(index, top, weights):
        group = index // blocks_a_group
        summed = jnp.dot(weights[...], values[group], preferred_element_type=jnp.float32)
        rows = pl.ds(index * block, block)
        if first_phase:
            state_sum[rows, :] = summed
            state_top[rows, :] = top[...]
            return
        fade = jnp.exp2((state_top[rows, :] - top[...]) * EXP2_SCALE)
        total = state_sum[rows, HD:] * fade + summed[:, HD:]
        result = ((state_sum[rows, :HD] * fade + summed[:, :HD]) / total).astype(jnp.bfloat16)
        kept = tokens // head_size
        for head, column in enumerate(columns(index, 0)):
            one = result[head * tokens : (head + 1) * tokens]
            if head_size == 2:
                low, high = one[:kept], one[kept:]
                outs[0][:, column] = jnp.where(my_head == 0, low, high)
                outs[1][:, column] = jnp.where(my_head == 0, high, low)
            else:
                outs[0][:, column] = one[:kept]
                outs[1][:, column] = one[kept:]

    def run(*steps):
        live = list(steps)
        while live:
            for step in list(live):
                if next(step, live) is live:
                    live.remove(step)

    for index in range(blocks + 2):
        if index >= 2:
            at = (index - 2) % 2
            finish(index - 2, tops[(index - 2) % 3], weights[at])
        steps = []
        if index < blocks:
            steps.append(score_steps(index, scores[index % 2], tops[index % 3]))
        if 1 <= index <= blocks:
            at = (index - 1) % 2
            steps.append(weight_steps(index - 1, scores[at], tops[(index - 1) % 3], weights[at]))
        run(*steps)


def attend(place, limits, owners, queries, part, parts, mine, theirs, layout, spec, state):
    tokens, _, _, head_size = spec[:4]
    total_keys = 2 * mine.shape[0]
    columns = queries.shape[1] // parts
    groups = columns // (PER_GROUP * HD)
    block_heads = 4
    while block_heads > 1 and block_heads * tokens * total_keys * 4 > SCORE_BYTES:
        block_heads //= 2
    block = block_heads * tokens
    rows = PER_GROUP * groups * tokens
    operands = queries.size * 2 + mine.size * 4 + rows * HD * 12
    scratch = groups * total_keys * HD * 8 + block * total_keys * 12 + block * HD * 12
    limit = operands + scratch + (6 << 20)
    whole = pl.BlockSpec(memory_space=pltpu.VMEM)
    scalars = pl.BlockSpec(memory_space=pltpu.SMEM)
    kept = tokens // head_size
    if state is None:
        state = ()
        out_shape = [
            jax.ShapeDtypeStruct((rows, 2 * HD), jnp.float32),
            jax.ShapeDtypeStruct((rows, HD), jnp.float32),
        ]
    else:
        out_shape = [
            jax.ShapeDtypeStruct((kept, columns), jnp.bfloat16),
            jax.ShapeDtypeStruct((tokens - kept, columns), jnp.bfloat16),
        ]
    return pl.pallas_call(
        functools.partial(attend_kernel, spec, tuple(layout), part, block_heads, groups),
        out_shape=out_shape,
        in_specs=[scalars] * 3 + [whole] * (3 + len(state)),
        out_specs=[whole] * 2,
        scratch_shapes=[
            pltpu.SMEM((owners.shape[1],), jnp.int32),
            pltpu.VMEM((groups, total_keys, 2 * HD), jnp.bfloat16),
            pltpu.VMEM((groups, total_keys, 2 * HD), jnp.bfloat16),
        ]
        + [pltpu.VMEM((block, total_keys), jnp.float32)] * 2
        + [pltpu.VMEM((block, total_keys), jnp.bfloat16)] * 2
        + [pltpu.VMEM((block, HD), jnp.float32)] * 3,
        compiler_params=pltpu.CompilerParams(vmem_limit_bytes=limit),
        cost_estimate=pl.CostEstimate(
            flops=8 * tokens * columns * total_keys,
            bytes_accessed=4 * tokens * columns + 2 * total_keys * columns // PER_GROUP,
            transcendentals=0,
        ),
    )(place, limits, owners, queries, mine, theirs, *state)


def body(span_query, span_kv, prefix_cache, prefix_len, block_owner):
    seq_size = lax.axis_size("seq")
    head_size = lax.axis_size("head")
    group_size = seq_size // REQS
    me = lax.axis_index("seq").astype(jnp.int32)
    my_head = lax.axis_index("head").astype(jnp.int32)
    request = me // group_size
    tokens = span_kv.shape[0]
    page = prefix_cache.shape[1]
    groups = span_kv.shape[1] // (2 * HD)
    parts = 2 if groups % 2 == 0 else 1
    bits = [1 << at for at in range(1, group_size.bit_length() - 1)]
    orders = (bits, bits[::-1])

    def send(rows, stage):
        return hop(rows, tuple(order[stage] for order in orders))

    def grown(layout, stage):
        return layout + shifted(layout, 1 << stage)

    stages = len(bits)
    other_page = lax.dynamic_index_in_dim(prefix_cache, 1 - request, 0, keepdims=False)
    crossed = hop(other_page, (group_size, group_size))
    own_page = lax.dynamic_index_in_dim(prefix_cache, request, 0, keepdims=False)
    span, span_layout = span_kv, [(0, SPAN_ROWS, tokens)]
    for stage in range(stages):
        received = send(span, stage)
        if stage == 0:
            crossed = after(received, crossed)
            pages = jnp.concatenate([own_page, crossed], axis=0)
            pages = jnp.concatenate([pages, send(pages, 0)], axis=0)
        elif stage == 1:
            received = after(pages, received)
        span, span_layout = jnp.concatenate([span, received], axis=0), grown(span_layout, stage)
    span_swapped = hop(span, (1, 1))

    place = jnp.stack([me, my_head])
    spec = (tokens, page, group_size, head_size, orders)
    common = (place, prefix_len, block_owner, span_query)
    states = [
        attend(*common, part, parts, span, span_swapped, span_layout, spec, None)
        for part in range(parts)
    ]

    page_layout = [(0, OWN_PAGE, page), (0, CROSSED_PAGE, page)]
    page_layout = grown(page_layout, 0)
    for stage in range(1, stages):
        received = send(pages, stage)
        if stage == stages - 1:
            received = after(states[0], received)
        pages, page_layout = jnp.concatenate([pages, received], axis=0), grown(page_layout, stage)
    pages_swapped = hop(pages, (1, 1))
    results = [
        attend(*common, part, parts, pages, pages_swapped, page_layout, spec, states[part])
        for part in range(parts)
    ]
    if head_size != 2:
        joined = jnp.concatenate([jnp.concatenate(pair, axis=0) for pair in results], axis=1)
        return lax.all_to_all(joined, "head", split_axis=0, concat_axis=1, tiled=True)
    kept = [pair[0] for pair in results]
    received = [lax.ppermute(pair[1], "head", [(0, 1), (1, 0)]) for pair in results]
    joined = jnp.concatenate(kept + kept, axis=1)
    start = (1 - my_head) * span_query.shape[1]
    for one in received:
        joined = lax.dynamic_update_slice(joined, one, (0, start))
        start = start + one.shape[1]
    return joined


def solution(mesh):
    placed = (P("seq", "head"), P("seq", "head"), P("seq", None, "head"), P(), P())
    return jax.shard_map(
        body, mesh=mesh, in_specs=placed, out_specs=P(("seq", "head"), None), check_vma=False
    )
```

```python
import functools
import math

import jax
import jax.numpy as jnp
from jax import lax
from jax.experimental import pallas as pl
from jax.experimental.pallas import tpu as pltpu
from jax.sharding import PartitionSpec as P

QH = 64
KVH = 8
HD = 128
REQS = 2
PER_GROUP = QH // KVH
EXP2_SCALE = HD ** (-0.5) * math.log2(math.e)
MASKED = -1e30
SCORE_BYTES = 8 * 1024 * 1024
KEY_CHUNK = 512
SPAN_ROWS, OWN_PAGE, CROSSED_PAGE = range(3)


def hop(value, bit_of_core):
    count = lax.axis_size("seq")
    return lax.ppermute(
        value, "seq", [(source, source ^ bit_of_core[source % 2]) for source in range(count)]
    )


def after(first, value):
    return lax.optimization_barrier((first, value))[1]


def shifted(layout, slots):
    return [(slot + slots, kind, rows) for slot, kind, rows in layout]


def hypercube_order(bits):
    order = [0]
    for bit in bits:
        order = order + [offset ^ bit for offset in order]
    return order


def attend_kernel(spec, layout, part, block_heads, groups, limit_ref, owner_ref, q_ref, *refs):
    tokens, page, group_size, head_size, orders = spec
    first_phase = layout[0][1] == SPAN_ROWS
    halves, refs = refs[:2], refs[2:]
    if first_phase:
        (state_sum, state_top), refs = refs[:2], refs[2:]
    else:
        (state_sum, state_top), outs, refs = refs[:2], refs[2:4], refs[4:]
    page_seen, keys, values = refs[:3]
    scores, weights, tops = refs[3:5], refs[5:7], refs[7:10]
    half_keys = halves[0].shape[0]
    chunk = min(KEY_CHUNK, 2 * half_keys)
    chunks = 2 * half_keys // chunk
    me = lax.axis_index("seq")
    my_head = lax.axis_index("head")
    request = me // group_size

    def note_page(index, carry):
        page_seen[owner_ref[request, index]] = jnp.clip(limit_ref[request] - index * page, 0, page)
        return carry

    if not first_phase:
        lax.fori_loop(0, owner_ref.shape[1], note_page, 0)

    offsets = [hypercube_order(order) for order in orders]
    for half in range(2):
        holder = me ^ half
        start = half * half_keys
        for slot, kind, rows in layout:
            source = holder ^ jnp.where(holder % 2 == 0, offsets[0][slot], offsets[1][slot])
            if kind == SPAN_ROWS:
                count = jnp.where(source <= me, tokens, 0)
            elif kind == OWN_PAGE:
                count = page_seen[source]
            else:
                count = page_seen[source ^ group_size]
            row = lax.broadcasted_iota(jnp.int32, (rows, HD), 0)
            lane = lax.broadcasted_iota(jnp.int32, (rows, HD), 1)
            bias = jnp.where((row < count) | (lane > 0), jnp.float32(0.0), jnp.float32(MASKED))
            for group in range(groups):
                keys[group, pl.ds(start, rows), HD:] = bias.astype(jnp.bfloat16)
            start += rows
    values[:, :, HD:] = jnp.ones((groups, 2 * half_keys, HD), jnp.bfloat16)

    for group in range(groups):
        for half, ref in enumerate(halves):
            at = pl.ds(half * half_keys, half_keys)
            column = (part * groups + group) * 2 * HD
            keys[group, at, :HD] = ref[:, pl.ds(column, HD)]
            values[group, at, :HD] = ref[:, pl.ds(column + HD, HD)]

    block = block_heads * tokens
    blocks_a_group = PER_GROUP // block_heads
    blocks = groups * blocks_a_group
    ones = (lax.broadcasted_iota(jnp.int32, (block, HD), 1) == 0).astype(jnp.bfloat16)
    causal = lax.broadcasted_iota(jnp.int32, (block, tokens), 1) <= (
        lax.broadcasted_iota(jnp.int32, (block, tokens), 0) % tokens
    )

    def columns(index, first):
        return [
            pl.ds(first + (index * block_heads + head) * HD, HD)
            for head in range(block_heads)
        ]

    def score_steps(index, scores, top):
        group = index // blocks_a_group
        first = part * groups * PER_GROUP * HD
        query = jnp.concatenate([q_ref[:, column] for column in columns(index, first)], axis=0)
        query = jnp.concatenate([query, ones], axis=1)
        if first_phase:
            best = jnp.full((block, HD), MASKED, jnp.float32)
        else:
            best = state_top[pl.ds(index * block, block), :]
        for at in range(chunks):
            made = lax.dot_general(
                query,
                keys[group, pl.ds(at * chunk, chunk), :],
                (((1,), (1,)), ((), ())),
                preferred_element_type=jnp.float32,
            )
            if at == 0 and first_phase:
                own = jnp.where(causal, made[:, :tokens], MASKED)
                made = jnp.concatenate([own, made[:, tokens:]], axis=1)
            scores[:, pl.ds(at * chunk, chunk)] = made
            for lane_at in range(0, chunk, HD):
                best = jnp.maximum(best, made[:, lane_at : lane_at + HD])
            yield
        top[...] = jnp.broadcast_to(jnp.max(best, axis=1, keepdims=True), (block, HD))

    def weight_steps(index, scores, top, weights):
        for at in range(chunks):
            for lane_at in range(at * chunk, (at + 1) * chunk, HD):
                shifted_score = scores[:, pl.ds(lane_at, HD)] - top[...]
                weights[:, pl.ds(lane_at, HD)] = jnp.exp2(shifted_score * EXP2_SCALE).astype(
                    jnp.bfloat16
                )
            yield

    def finish(index, top, weights):
        group = index // blocks_a_group
        summed = jnp.dot(weights[...], values[group], preferred_element_type=jnp.float32)
        rows = pl.ds(index * block, block)
        if first_phase:
            state_sum[rows, :] = summed
            state_top[rows, :] = top[...]
            return
        fade = jnp.exp2((state_top[rows, :] - top[...]) * EXP2_SCALE)
        total = state_sum[rows, HD:] * fade + summed[:, HD:]
        result = ((state_sum[rows, :HD] * fade + summed[:, :HD]) / total).astype(jnp.bfloat16)
        kept = tokens // head_size
        for head, column in enumerate(columns(index, 0)):
            one = result[head * tokens : (head + 1) * tokens]
            if head_size == 2:
                low, high = one[:kept], one[kept:]
                outs[0][:, column] = jnp.where(my_head == 0, low, high)
                outs[1][:, column] = jnp.where(my_head == 0, high, low)
            else:
                outs[0][:, column] = one[:kept]
                outs[1][:, column] = one[kept:]

    def run(*steps):
        live = list(steps)
        while live:
            for step in list(live):
                if next(step, live) is live:
                    live.remove(step)

    for index in range(blocks + 2):
        if index >= 2:
            at = (index - 2) % 2
            finish(index - 2, tops[(index - 2) % 3], weights[at])
        steps = []
        if index < blocks:
            steps.append(score_steps(index, scores[index % 2], tops[index % 3]))
        if 1 <= index <= blocks:
            at = (index - 1) % 2
            steps.append(weight_steps(index - 1, scores[at], tops[(index - 1) % 3], weights[at]))
        run(*steps)


def attend(limits, owners, queries, part, parts, mine, theirs, layout, spec, state):
    tokens, _, _, head_size = spec[:4]
    total_keys = 2 * mine.shape[0]
    columns = queries.shape[1] // parts
    groups = columns // (PER_GROUP * HD)
    block_heads = 4
    while block_heads > 1 and block_heads * tokens * total_keys * 4 > SCORE_BYTES:
        block_heads //= 2
    block = block_heads * tokens
    rows = PER_GROUP * groups * tokens
    operands = queries.size * 2 + mine.size * 4 + rows * HD * 12
    scratch = groups * total_keys * HD * 8 + block * total_keys * 12 + block * HD * 12
    limit = operands + scratch + (6 << 20)
    whole = pl.BlockSpec(memory_space=pltpu.VMEM)
    scalars = pl.BlockSpec(memory_space=pltpu.SMEM)
    kept = tokens // head_size
    if state is None:
        state = ()
        out_shape = [
            jax.ShapeDtypeStruct((rows, 2 * HD), jnp.float32),
            jax.ShapeDtypeStruct((rows, HD), jnp.float32),
        ]
    else:
        out_shape = [
            jax.ShapeDtypeStruct((kept, columns), jnp.bfloat16),
            jax.ShapeDtypeStruct((tokens - kept, columns), jnp.bfloat16),
        ]
    return pl.pallas_call(
        functools.partial(attend_kernel, spec, tuple(layout), part, block_heads, groups),
        out_shape=out_shape,
        in_specs=[scalars] * 2 + [whole] * (3 + len(state)),
        out_specs=[whole] * 2,
        scratch_shapes=[
            pltpu.SMEM((owners.shape[1],), jnp.int32),
            pltpu.VMEM((groups, total_keys, 2 * HD), jnp.bfloat16),
            pltpu.VMEM((groups, total_keys, 2 * HD), jnp.bfloat16),
        ]
        + [pltpu.VMEM((block, total_keys), jnp.float32)] * 2
        + [pltpu.VMEM((block, total_keys), jnp.bfloat16)] * 2
        + [pltpu.VMEM((block, HD), jnp.float32)] * 3,
        compiler_params=pltpu.CompilerParams(vmem_limit_bytes=limit),
        cost_estimate=pl.CostEstimate(
            flops=8 * tokens * columns * total_keys,
            bytes_accessed=4 * tokens * columns + 2 * total_keys * columns // PER_GROUP,
            transcendentals=0,
        ),
    )(limits, owners, queries, mine, theirs, *state)


def pick_kernel(group_size, cache_ref, span_ref, other_ref, own_ref, copied_ref):
    request = lax.axis_index("seq") // group_size
    other_ref[...] = cache_ref[1 - request]
    own_ref[...] = cache_ref[request]
    copied_ref[...] = span_ref[...]


def pick(cache, span, group_size):
    whole = pl.BlockSpec(memory_space=pltpu.VMEM)
    return pl.pallas_call(
        functools.partial(pick_kernel, group_size),
        out_shape=[
            jax.ShapeDtypeStruct(cache.shape[1:], cache.dtype),
            jax.ShapeDtypeStruct(cache.shape[1:], cache.dtype),
            jax.ShapeDtypeStruct(span.shape, span.dtype),
        ],
        in_specs=[whole] * 2,
        out_specs=[whole] * 3,
        compiler_params=pltpu.CompilerParams(vmem_limit_bytes=8 << 20),
    )(cache, span)


def join_kernel(pieces, *refs):
    parts, (out_ref, done) = refs[:pieces], refs[pieces:]
    columns = [ref.shape[1] for ref in parts[: pieces // 2]]
    side = out_ref.shape[1] // 2
    my_head = lax.axis_index("head")
    copies = []
    for at, ref in enumerate(parts):
        owner = my_head if at < pieces // 2 else 1 - my_head
        first = pl.multiple_of(owner * side + sum(columns[: at % (pieces // 2)]), HD)
        copies.append(
            pltpu.make_async_copy(ref, out_ref.at[:, pl.ds(first, ref.shape[1])], done.at[at])
        )
    for copy in copies:
        copy.start()
    for copy in copies:
        copy.wait()


def put_together(kept, received):
    pieces = len(kept) + len(received)
    rows = kept[0].shape[0]
    columns = sum(one.shape[1] for one in kept + received)
    return pl.pallas_call(
        functools.partial(join_kernel, pieces),
        out_shape=jax.ShapeDtypeStruct((rows, columns), kept[0].dtype),
        in_specs=[pl.BlockSpec(memory_space=pltpu.VMEM)] * pieces,
        out_specs=pl.BlockSpec(memory_space=pl.ANY),
        scratch_shapes=[pltpu.SemaphoreType.DMA((pieces,))],
        compiler_params=pltpu.CompilerParams(vmem_limit_bytes=8 << 20),
    )(*kept, *received)


def body(span_query, span_kv, prefix_cache, prefix_len, block_owner):
    seq_size = lax.axis_size("seq")
    head_size = lax.axis_size("head")
    group_size = seq_size // REQS
    tokens = span_kv.shape[0]
    page = prefix_cache.shape[1]
    groups = span_kv.shape[1] // (2 * HD)
    parts = 2 if groups % 2 == 0 else 1
    bits = [1 << at for at in range(1, group_size.bit_length() - 1)]
    orders = (bits, bits[::-1])

    def send(rows, stage):
        return hop(rows, tuple(order[stage] for order in orders))

    def grown(layout, stage):
        return layout + shifted(layout, 1 << stage)

    stages = len(bits)
    other_page, own_page, span = pick(prefix_cache, span_kv, group_size)
    crossed = hop(other_page, (group_size, group_size))
    span_layout = [(0, SPAN_ROWS, tokens)]
    for stage in range(stages):
        received = send(span if stage else span_kv, stage)
        if stage == 0:
            crossed = after(received, crossed)
            pages = jnp.concatenate([own_page, crossed], axis=0)
            pages = jnp.concatenate([pages, send(pages, 0)], axis=0)
        elif stage == 1:
            received = after(pages, received)
        span, span_layout = jnp.concatenate([span, received], axis=0), grown(span_layout, stage)
    span_swapped = hop(span, (1, 1))

    spec = (tokens, page, group_size, head_size, orders)
    common = (prefix_len, block_owner, span_query)
    states = [
        attend(*common, part, parts, span, span_swapped, span_layout, spec, None)
        for part in range(parts)
    ]

    page_layout = [(0, OWN_PAGE, page), (0, CROSSED_PAGE, page)]
    page_layout = grown(page_layout, 0)
    for stage in range(1, stages):
        received = send(pages, stage)
        if stage == stages - 1:
            received = after(states[0], received)
        pages, page_layout = jnp.concatenate([pages, received], axis=0), grown(page_layout, stage)
    pages_swapped = hop(pages, (1, 1))
    results = [
        attend(*common, part, parts, pages, pages_swapped, page_layout, spec, states[part])
        for part in range(parts)
    ]
    if head_size != 2:
        joined = jnp.concatenate([jnp.concatenate(pair, axis=0) for pair in results], axis=1)
        return lax.all_to_all(joined, "head", split_axis=0, concat_axis=1, tiled=True)
    kept = [pair[0] for pair in results]
    received = [lax.ppermute(pair[1], "head", [(0, 1), (1, 0)]) for pair in results]
    return put_together(kept, received)


def solution(mesh):
    placed = (P("seq", "head"), P("seq", "head"), P("seq", None, "head"), P(), P())
    return jax.shard_map(
        body, mesh=mesh, in_specs=placed, out_specs=P(("seq", "head"), None), check_vma=False
    )
```

```python
import functools
import math

import jax
import jax.numpy as jnp
from jax import lax
from jax.experimental import pallas as pl
from jax.experimental.pallas import tpu as pltpu
from jax.sharding import PartitionSpec as P

QH = 64
KVH = 8
HD = 128
REQS = 2
PER_GROUP = QH // KVH
EXP2_SCALE = HD ** (-0.5) * math.log2(math.e)
MASKED = -1e30
SCORE_BYTES = 8 * 1024 * 1024
KEY_CHUNK = 512
BIAS_ROWS = 16
SPAN_ROWS, OWN_PAGE, CROSSED_PAGE = range(3)


def hop(value, bit_of_core):
    count = lax.axis_size("seq")
    return lax.ppermute(
        value, "seq", [(source, source ^ bit_of_core[source % 2]) for source in range(count)]
    )


def after(first, value):
    return lax.optimization_barrier((first, value))[1]


def shifted(layout, slots):
    return [(slot + slots, kind, rows) for slot, kind, rows in layout]


def hypercube_order(bits):
    order = [0]
    for bit in bits:
        order = order + [offset ^ bit for offset in order]
    return order


def attend_kernel(spec, layout, part, block_heads, groups, limit_ref, owner_ref, q_ref, *refs):
    tokens, page, group_size, head_size, orders = spec
    first_phase = layout[0][1] == SPAN_ROWS
    halves, refs = refs[:2], refs[2:]
    if first_phase:
        (state_sum, state_top), refs = refs[:2], refs[2:]
    else:
        (state_sum, state_top), outs, refs = refs[:2], refs[2:4], refs[4:]
    page_seen, keys, values = refs[:3]
    scores, weights, tops = refs[3:5], refs[5:7], refs[7:10]
    half_keys = halves[0].shape[0]
    chunk = min(KEY_CHUNK, 2 * half_keys)
    chunks = 2 * half_keys // chunk
    me = lax.axis_index("seq")
    my_head = lax.axis_index("head")
    request = me // group_size

    def note_page(index, carry):
        page_seen[owner_ref[request, index]] = jnp.clip(limit_ref[request] - index * page, 0, page)
        return carry

    if not first_phase:
        lax.fori_loop(0, owner_ref.shape[1], note_page, 0)

    offsets = [hypercube_order(order) for order in orders]
    row = lax.broadcasted_iota(jnp.int32, (BIAS_ROWS, half_keys), 0)
    key = lax.broadcasted_iota(jnp.int32, (BIAS_ROWS, half_keys), 1)
    for half in range(2):
        holder = me ^ half
        start = 0
        seen = row > 0
        for slot, kind, rows in layout:
            source = holder ^ jnp.where(holder % 2 == 0, offsets[0][slot], offsets[1][slot])
            if kind == SPAN_ROWS:
                count = jnp.where(source <= me, tokens, 0)
            elif kind == OWN_PAGE:
                count = page_seen[source]
            else:
                count = page_seen[source ^ group_size]
            seen = seen | ((key >= start) & (key < start + count))
            start += rows
        bias = jnp.where(seen, jnp.float32(0.0), jnp.float32(MASKED)).astype(jnp.bfloat16)
        at = pl.ds(half * half_keys, half_keys)
        for group in range(groups):
            column = (part * groups + group) * 2 * HD
            keys[group, :HD, at] = halves[half][:, pl.ds(column, HD)].T
            keys[group, pl.ds(HD, BIAS_ROWS), at] = bias
            values[group, at, :HD] = halves[half][:, pl.ds(column + HD, HD)]
    rest = HD - BIAS_ROWS
    keys[:, HD + BIAS_ROWS :, :] = jnp.zeros((groups, rest, 2 * half_keys), jnp.bfloat16)
    values[:, :, HD:] = jnp.ones((groups, 2 * half_keys, HD), jnp.bfloat16)

    block = block_heads * tokens
    blocks_a_group = PER_GROUP // block_heads
    blocks = groups * blocks_a_group
    ones = (lax.broadcasted_iota(jnp.int32, (block, HD), 1) == 0).astype(jnp.bfloat16)
    causal = lax.broadcasted_iota(jnp.int32, (block, tokens), 1) <= (
        lax.broadcasted_iota(jnp.int32, (block, tokens), 0) % tokens
    )

    def columns(index, first):
        return [
            pl.ds(first + (index * block_heads + head) * HD, HD)
            for head in range(block_heads)
        ]

    def score_steps(index, scores, top):
        group = index // blocks_a_group
        first = part * groups * PER_GROUP * HD
        query = jnp.concatenate([q_ref[:, column] for column in columns(index, first)], axis=0)
        query = jnp.concatenate([query, ones], axis=1)
        if first_phase:
            best = jnp.full((block, HD), MASKED, jnp.float32)
        else:
            best = state_top[pl.ds(index * block, block), :]
        for at in range(chunks):
            made = jnp.dot(
                query, keys[group, :, pl.ds(at * chunk, chunk)], preferred_element_type=jnp.float32
            )
            if at == 0 and first_phase:
                own = jnp.where(causal, made[:, :tokens], MASKED)
                made = jnp.concatenate([own, made[:, tokens:]], axis=1)
            scores[:, pl.ds(at * chunk, chunk)] = made
            for lane_at in range(0, chunk, 2 * HD):
                left, right = made[:, lane_at : lane_at + HD], made[:, lane_at + HD : lane_at + 2 * HD]
                best = jnp.maximum(best, jnp.maximum(left, right))
            yield
        top[...] = jnp.broadcast_to(jnp.max(best, axis=1, keepdims=True), (block, HD))

    def weight_steps(index, scores, top, weights):
        for at in range(chunks):
            for lane_at in range(at * chunk, (at + 1) * chunk, HD):
                shifted_score = scores[:, pl.ds(lane_at, HD)] - top[...]
                weights[:, pl.ds(lane_at, HD)] = jnp.exp2(shifted_score * EXP2_SCALE).astype(
                    jnp.bfloat16
                )
            yield

    def finish(index, top, weights):
        group = index // blocks_a_group
        summed = jnp.dot(weights[...], values[group], preferred_element_type=jnp.float32)
        rows = pl.ds(index * block, block)
        if first_phase:
            state_sum[rows, :] = summed
            state_top[rows, :] = top[...]
            return
        fade = jnp.exp2((state_top[rows, :] - top[...]) * EXP2_SCALE)
        total = state_sum[rows, HD:] * fade + summed[:, HD:]
        result = ((state_sum[rows, :HD] * fade + summed[:, :HD]) / total).astype(jnp.bfloat16)
        kept = tokens // head_size
        for head, column in enumerate(columns(index, 0)):
            one = result[head * tokens : (head + 1) * tokens]
            if head_size == 2:
                low, high = one[:kept], one[kept:]
                outs[0][:, column] = jnp.where(my_head == 0, low, high)
                outs[1][:, column] = jnp.where(my_head == 0, high, low)
            else:
                outs[0][:, column] = one[:kept]
                outs[1][:, column] = one[kept:]

    def run(*steps):
        live = list(steps)
        while live:
            for step in list(live):
                if next(step, live) is live:
                    live.remove(step)

    for index in range(blocks + 2):
        if index >= 2:
            at = (index - 2) % 2
            finish(index - 2, tops[(index - 2) % 3], weights[at])
        steps = []
        if index < blocks:
            steps.append(score_steps(index, scores[index % 2], tops[index % 3]))
        if 1 <= index <= blocks:
            at = (index - 1) % 2
            steps.append(weight_steps(index - 1, scores[at], tops[(index - 1) % 3], weights[at]))
        run(*steps)


def attend(limits, owners, queries, part, parts, mine, theirs, layout, spec, state):
    tokens, _, _, head_size = spec[:4]
    total_keys = 2 * mine.shape[0]
    columns = queries.shape[1] // parts
    groups = columns // (PER_GROUP * HD)
    block_heads = 4
    while block_heads > 1 and block_heads * tokens * total_keys * 4 > SCORE_BYTES:
        block_heads //= 2
    block = block_heads * tokens
    rows = PER_GROUP * groups * tokens
    operands = queries.size * 2 + mine.size * 4 + rows * HD * 12
    scratch = groups * total_keys * HD * 8 + block * total_keys * 12 + block * HD * 12
    limit = operands + scratch + (6 << 20)
    whole = pl.BlockSpec(memory_space=pltpu.VMEM)
    scalars = pl.BlockSpec(memory_space=pltpu.SMEM)
    kept = tokens // head_size
    if state is None:
        state = ()
        out_shape = [
            jax.ShapeDtypeStruct((rows, 2 * HD), jnp.float32),
            jax.ShapeDtypeStruct((rows, HD), jnp.float32),
        ]
    else:
        out_shape = [
            jax.ShapeDtypeStruct((kept, columns), jnp.bfloat16),
            jax.ShapeDtypeStruct((tokens - kept, columns), jnp.bfloat16),
        ]
    return pl.pallas_call(
        functools.partial(attend_kernel, spec, tuple(layout), part, block_heads, groups),
        out_shape=out_shape,
        in_specs=[scalars] * 2 + [whole] * (3 + len(state)),
        out_specs=[whole] * 2,
        scratch_shapes=[
            pltpu.SMEM((owners.shape[1],), jnp.int32),
            pltpu.VMEM((groups, 2 * HD, total_keys), jnp.bfloat16),
            pltpu.VMEM((groups, total_keys, 2 * HD), jnp.bfloat16),
        ]
        + [pltpu.VMEM((block, total_keys), jnp.float32)] * 2
        + [pltpu.VMEM((block, total_keys), jnp.bfloat16)] * 2
        + [pltpu.VMEM((block, HD), jnp.float32)] * 3,
        compiler_params=pltpu.CompilerParams(vmem_limit_bytes=limit),
        cost_estimate=pl.CostEstimate(
            flops=8 * tokens * columns * total_keys,
            bytes_accessed=4 * tokens * columns + 2 * total_keys * columns // PER_GROUP,
            transcendentals=0,
        ),
    )(limits, owners, queries, mine, theirs, *state)


def pick_kernel(group_size, cache_ref, span_ref, other_ref, own_ref, copied_ref, done):
    request = lax.axis_index("seq") // group_size
    copies = [
        pltpu.make_async_copy(cache_ref.at[1 - request], other_ref, done.at[0]),
        pltpu.make_async_copy(cache_ref.at[request], own_ref, done.at[1]),
        pltpu.make_async_copy(span_ref, copied_ref, done.at[2]),
    ]
    for copy in copies:
        copy.start()
    for copy in copies:
        copy.wait()


def pick(cache, span, group_size):
    return pl.pallas_call(
        functools.partial(pick_kernel, group_size),
        out_shape=[
            jax.ShapeDtypeStruct(cache.shape[1:], cache.dtype),
            jax.ShapeDtypeStruct(cache.shape[1:], cache.dtype),
            jax.ShapeDtypeStruct(span.shape, span.dtype),
        ],
        in_specs=[pl.BlockSpec(memory_space=pl.ANY)] * 2,
        out_specs=[pl.BlockSpec(memory_space=pltpu.VMEM)] * 3,
        scratch_shapes=[pltpu.SemaphoreType.DMA((3,))],
        compiler_params=pltpu.CompilerParams(vmem_limit_bytes=8 << 20),
    )(cache, span)


def join_kernel(pieces, *refs):
    parts, (out_ref, done) = refs[:pieces], refs[pieces:]
    columns = [ref.shape[1] for ref in parts[: pieces // 2]]
    side = out_ref.shape[1] // 2
    my_head = lax.axis_index("head")
    copies = []
    for at, ref in enumerate(parts):
        owner = my_head if at < pieces // 2 else 1 - my_head
        first = pl.multiple_of(owner * side + sum(columns[: at % (pieces // 2)]), HD)
        copies.append(
            pltpu.make_async_copy(ref, out_ref.at[:, pl.ds(first, ref.shape[1])], done.at[at])
        )
    for copy in copies:
        copy.start()
    for copy in copies:
        copy.wait()


def put_together(kept, received):
    pieces = len(kept) + len(received)
    rows = kept[0].shape[0]
    columns = sum(one.shape[1] for one in kept + received)
    return pl.pallas_call(
        functools.partial(join_kernel, pieces),
        out_shape=jax.ShapeDtypeStruct((rows, columns), kept[0].dtype),
        in_specs=[pl.BlockSpec(memory_space=pltpu.VMEM)] * pieces,
        out_specs=pl.BlockSpec(memory_space=pl.ANY),
        scratch_shapes=[pltpu.SemaphoreType.DMA((pieces,))],
        compiler_params=pltpu.CompilerParams(vmem_limit_bytes=8 << 20),
    )(*kept, *received)


def body(span_query, span_kv, prefix_cache, prefix_len, block_owner):
    seq_size = lax.axis_size("seq")
    head_size = lax.axis_size("head")
    group_size = seq_size // REQS
    tokens = span_kv.shape[0]
    page = prefix_cache.shape[1]
    groups = span_kv.shape[1] // (2 * HD)
    parts = 2 if groups % 2 == 0 else 1
    bits = [1 << at for at in range(1, group_size.bit_length() - 1)]
    orders = (bits, bits[::-1])

    def send(rows, stage):
        return hop(rows, tuple(order[stage] for order in orders))

    def grown(layout, stage):
        return layout + shifted(layout, 1 << stage)

    stages = len(bits)
    other_page, own_page, span = pick(prefix_cache, span_kv, group_size)
    crossed = hop(other_page, (group_size, group_size))
    span_layout = [(0, SPAN_ROWS, tokens)]
    for stage in range(stages):
        received = send(span if stage else span_kv, stage)
        if stage == 1:
            received = after(pages, received)
        span, span_layout = jnp.concatenate([span, received], axis=0), grown(span_layout, stage)
        if stage == 0:
            crossed = after(span, crossed)
            pages = jnp.concatenate([own_page, crossed], axis=0)
            pages = jnp.concatenate([pages, send(pages, 0)], axis=0)
    span_swapped = hop(span, (1, 1))

    spec = (tokens, page, group_size, head_size, orders)
    common = (prefix_len, block_owner, span_query)
    states = [
        attend(*common, part, parts, span, span_swapped, span_layout, spec, None)
        for part in range(parts)
    ]

    page_layout = [(0, OWN_PAGE, page), (0, CROSSED_PAGE, page)]
    page_layout = grown(page_layout, 0)
    for stage in range(1, stages):
        received = send(pages, stage)
        if stage == stages - 1:
            received = after(states[0], received)
        pages, page_layout = jnp.concatenate([pages, received], axis=0), grown(page_layout, stage)
    pages_swapped = hop(pages, (1, 1))
    results = [
        attend(*common, part, parts, pages, pages_swapped, page_layout, spec, states[part])
        for part in range(parts)
    ]
    if head_size != 2:
        joined = jnp.concatenate([jnp.concatenate(pair, axis=0) for pair in results], axis=1)
        return lax.all_to_all(joined, "head", split_axis=0, concat_axis=1, tiled=True)
    kept = [pair[0] for pair in results]
    received = [lax.ppermute(pair[1], "head", [(0, 1), (1, 0)]) for pair in results]
    return put_together(kept, received)


def solution(mesh):
    placed = (P("seq", "head"), P("seq", "head"), P("seq", None, "head"), P(), P())
    return jax.shard_map(
        body, mesh=mesh, in_specs=placed, out_specs=P(("seq", "head"), None), check_vma=False
    )
```

```python
import functools
import math

import jax
import jax.numpy as jnp
from jax import lax
from jax.experimental import pallas as pl
from jax.experimental.pallas import tpu as pltpu
from jax.sharding import PartitionSpec as P

QH = 64
KVH = 8
HD = 128
REQS = 2
PER_GROUP = QH // KVH
EXP2_SCALE = HD ** (-0.5) * math.log2(math.e)
MASKED = -1e30
KEY_CHUNK = 512
EXTRA_ROWS = 16
SHIFT_STEP = 32.0
LOWEST_TOTAL = 1e-20
SPAN_ROWS, OWN_PAGE, CROSSED_PAGE = range(3)


def hop(value, bit_of_core):
    count = lax.axis_size("seq")
    return lax.ppermute(
        value, "seq", [(source, source ^ bit_of_core[source % 2]) for source in range(count)]
    )


def after(first, value):
    return lax.optimization_barrier((first, value))[1]


def shifted(layout, slots):
    return [(slot + slots, kind, rows) for slot, kind, rows in layout]


def hypercube_order(bits):
    order = [0]
    for bit in bits:
        order = order + [offset ^ bit for offset in order]
    return order


def attend_kernel(spec, layouts, part, block_heads, groups, limit_ref, owner_ref, q_ref, *refs):
    tokens, page, group_size, head_size, orders = spec
    first_phase = len(layouts) == 1
    key_sets, refs = [(refs[2 * at : 2 * at + 2], layout) for at, layout in enumerate(layouts)], refs[
        2 * len(layouts) :
    ]
    (state_sum, state_shift), refs = refs[:2], refs[2:]
    if first_phase:
        page_seen, keys, values = refs[:3]
        weights = refs[3:5]
    else:
        outs = refs[:2]
        page_seen, keys, values = refs[2:5]
        weights, shifts, slow_sum, slow_top = refs[5:7], refs[7:9], refs[9], refs[10]
    half_keys = key_sets[0][0][0].shape[0]
    total_keys = 2 * half_keys
    chunk = min(KEY_CHUNK, total_keys)
    me = lax.axis_index("seq")
    my_head = lax.axis_index("head")
    request = me // group_size
    offsets = [hypercube_order(order) for order in orders]

    def note_page(index, carry):
        page_seen[owner_ref[request, index]] = jnp.clip(limit_ref[request] - index * page, 0, page)
        return carry

    if not first_phase:
        lax.fori_loop(0, owner_ref.shape[1], note_page, 0)

    def fill(halves, layout):
        row = lax.broadcasted_iota(jnp.int32, (EXTRA_ROWS, half_keys), 0)
        key = lax.broadcasted_iota(jnp.int32, (EXTRA_ROWS, half_keys), 1)
        for half in range(2):
            holder = me ^ half
            start = 0
            seen = key < 0
            for slot, kind, rows in layout:
                source = holder ^ jnp.where(holder % 2 == 0, offsets[0][slot], offsets[1][slot])
                if kind == SPAN_ROWS:
                    count = jnp.where(source <= me, tokens, 0)
                elif kind == OWN_PAGE:
                    count = page_seen[source]
                else:
                    count = page_seen[source ^ group_size]
                seen = seen | ((key >= start) & (key < start + count))
                start += rows
            mask = jnp.where(seen, jnp.float32(0.0), jnp.float32(MASKED))
            extra = jnp.where(row == 0, mask, jnp.where(row == 1, jnp.float32(1.0), jnp.float32(0.0)))
            at = pl.ds(half * half_keys, half_keys)
            for group in range(groups):
                column = (part * groups + group) * 2 * HD
                keys[group, :HD, at] = halves[half][:, pl.ds(column, HD)].T
                keys[group, pl.ds(HD, EXTRA_ROWS), at] = extra.astype(jnp.bfloat16)
                values[group, at, :HD] = halves[half][:, pl.ds(column + HD, HD)]
        rest = HD - EXTRA_ROWS
        keys[:, HD + EXTRA_ROWS :, :] = jnp.zeros((groups, rest, total_keys), jnp.bfloat16)
        values[:, :, HD:] = jnp.ones((groups, total_keys, HD), jnp.bfloat16)

    block = block_heads * tokens
    blocks_a_group = PER_GROUP // block_heads
    blocks = groups * blocks_a_group
    lane = lax.broadcasted_iota(jnp.int32, (block, HD), 1)
    causal = lax.broadcasted_iota(jnp.int32, (block, tokens), 1) <= (
        lax.broadcasted_iota(jnp.int32, (block, tokens), 0) % tokens
    )

    def query_rows(index):
        first = (part * blocks + index) * block_heads * HD
        columns = [
            pl.ds(pl.multiple_of(first + head * HD, HD), HD) for head in range(block_heads)
        ]
        return jnp.concatenate([q_ref[:, column] for column in columns], axis=0)

    def scores_of(query, group, start, is_span):
        made = jnp.dot(
            query, keys[group, :, pl.ds(start, chunk)], preferred_element_type=jnp.float32
        )
        if start == 0 and is_span:
            own = jnp.where(causal, made[:, :tokens], MASKED)
            made = jnp.concatenate([own, made[:, tokens:]], axis=1)
        return made

    def give(index, result):
        kept = tokens // head_size
        for head in range(block_heads):
            column = pl.ds((index * block_heads + head) * HD, HD)
            one = result[head * tokens : (head + 1) * tokens]
            if head_size == 2:
                low, high = one[:kept], one[kept:]
                outs[0][:, column] = jnp.where(my_head == 0, low, high)
                outs[1][:, column] = jnp.where(my_head == 0, high, low)
            else:
                outs[0][:, column] = one[:kept]
                outs[1][:, column] = one[kept:]

    fill(*key_sets[-1])
    longest = []
    for group in range(groups):
        key = keys[group, :HD, :].astype(jnp.float32)
        longest.append(jnp.max(jnp.sum(key * key, axis=0, keepdims=True), axis=1, keepdims=True))

    def weigh(index):
        group = index // blocks_a_group
        query = query_rows(index)
        wide = query.astype(jnp.float32)
        bound = jnp.sqrt(jnp.sum(wide * wide, axis=1, keepdims=True) * longest[group])
        shift = jnp.ceil(bound * (1.0 / SHIFT_STEP)) * SHIFT_STEP
        extra = jnp.where(lane == 0, 1.0, jnp.where(lane == 1, -shift, 0.0))
        query = jnp.concatenate([query, extra.astype(jnp.bfloat16)], axis=1)
        shift = jnp.broadcast_to(shift, (block, HD))
        if first_phase:
            state_shift[pl.ds(index * block, block), :] = shift
        else:
            shifts[index % 2][...] = shift
        for start in range(0, total_keys, chunk):
            made = scores_of(query, group, start, first_phase)
            weights[index % 2][:, pl.ds(start, chunk)] = jnp.exp2(made * EXP2_SCALE).astype(
                jnp.bfloat16
            )

    def finish(index, lowest):
        group = index // blocks_a_group
        summed = jnp.dot(
            weights[index % 2][...], values[group], preferred_element_type=jnp.float32
        )
        rows = pl.ds(index * block, block)
        if first_phase:
            state_sum[rows, :] = summed
            return lowest
        before, shift = state_shift[rows, :], shifts[index % 2][...]
        both = jnp.maximum(before, shift)
        fade_before = jnp.exp2((before - both) * EXP2_SCALE)
        fade = jnp.exp2((shift - both) * EXP2_SCALE)
        total = state_sum[rows, HD:] * fade_before + summed[:, HD:] * fade
        result = (state_sum[rows, :HD] * fade_before + summed[:, :HD] * fade) / total
        give(index, result.astype(jnp.bfloat16))
        return jnp.minimum(lowest, total)

    lowest = jnp.ones((block, HD), jnp.float32)
    for index in range(blocks + 1):
        if index >= 1:
            lowest = finish(index - 1, lowest)
        if index < blocks:
            weigh(index)
    if first_phase:
        return

    @pl.when(jnp.min(lowest) < LOWEST_TOTAL)
    def exact():
        for number, (halves, layout) in enumerate(key_sets):
            fill(halves, layout)

            def one_block(index, carry):
                group = index // blocks_a_group
                extra = (lane == 0).astype(jnp.float32).astype(jnp.bfloat16)
                query = jnp.concatenate([query_rows(index), extra], axis=1)
                rows = pl.ds(pl.multiple_of(index * block, block), block)
                if number == 0:
                    top = jnp.full((block, HD), MASKED, jnp.float32)
                    summed = jnp.zeros((block, 2 * HD), jnp.float32)
                else:
                    top = slow_top[rows, :]
                    summed = slow_sum[rows, :]
                best = top
                for start in range(0, total_keys, chunk):
                    made = scores_of(query, group, start, number == 0)
                    for at in range(0, chunk, HD):
                        best = jnp.maximum(best, made[:, at : at + HD])
                best = jnp.broadcast_to(jnp.max(best, axis=1, keepdims=True), (block, HD))
                fade = jnp.exp2((top - best) * EXP2_SCALE)
                summed = summed * jnp.concatenate([fade, fade], axis=1)
                for start in range(0, total_keys, chunk):
                    made = scores_of(query, group, start, number == 0)
                    parts = [
                        jnp.exp2((made[:, at : at + HD] - best) * EXP2_SCALE)
                        for at in range(0, chunk, HD)
                    ]
                    summed = summed + jnp.dot(
                        jnp.concatenate(parts, axis=1).astype(jnp.bfloat16),
                        values[group, pl.ds(start, chunk), :],
                        preferred_element_type=jnp.float32,
                    )
                slow_top[rows, :] = best
                slow_sum[rows, :] = summed
                return carry

            lax.fori_loop(0, blocks, one_block, 0)
        for index in range(blocks):
            rows = pl.ds(index * block, block)
            give(index, (slow_sum[rows, :HD] / slow_sum[rows, HD:]).astype(jnp.bfloat16))


def attend(limits, owners, queries, part, parts, key_sets, spec, state):
    tokens, _, _, head_size = spec[:4]
    half_keys = key_sets[0][0].shape[0]
    total_keys = 2 * half_keys
    columns = queries.shape[1] // parts
    groups = columns // (PER_GROUP * HD)
    block_heads = 4
    block = block_heads * tokens
    rows = PER_GROUP * groups * tokens
    pieces = [piece for mine, theirs, _ in key_sets for piece in (mine, theirs)]
    layouts = tuple(tuple(layout) for _, _, layout in key_sets)
    operands = queries.size * 2 + sum(piece.size for piece in pieces) * 2 + rows * HD * 12
    scratch = groups * total_keys * HD * 8 + block * total_keys * 4 + rows * HD * 12
    whole = pl.BlockSpec(memory_space=pltpu.VMEM)
    scalars = pl.BlockSpec(memory_space=pltpu.SMEM)
    kept = tokens // head_size
    scratch_shapes = [
        pltpu.SMEM((owners.shape[1],), jnp.int32),
        pltpu.VMEM((groups, 2 * HD, total_keys), jnp.bfloat16),
        pltpu.VMEM((groups, total_keys, 2 * HD), jnp.bfloat16),
    ] + [pltpu.VMEM((block, total_keys), jnp.bfloat16)] * 2
    if state is None:
        state = ()
        out_shape = [
            jax.ShapeDtypeStruct((rows, 2 * HD), jnp.float32),
            jax.ShapeDtypeStruct((rows, HD), jnp.float32),
        ]
    else:
        out_shape = [
            jax.ShapeDtypeStruct((kept, columns), jnp.bfloat16),
            jax.ShapeDtypeStruct((tokens - kept, columns), jnp.bfloat16),
        ]
        scratch_shapes += [pltpu.VMEM((block, HD), jnp.float32)] * 2
        scratch_shapes += [
            pltpu.VMEM((rows, 2 * HD), jnp.float32),
            pltpu.VMEM((rows, HD), jnp.float32),
        ]
    return pl.pallas_call(
        functools.partial(attend_kernel, spec, layouts, part, block_heads, groups),
        out_shape=out_shape,
        in_specs=[scalars] * 2 + [whole] * (1 + len(pieces) + len(state)),
        out_specs=[whole] * 2,
        scratch_shapes=scratch_shapes,
        compiler_params=pltpu.CompilerParams(vmem_limit_bytes=operands + scratch + (6 << 20)),
        cost_estimate=pl.CostEstimate(
            flops=8 * tokens * columns * total_keys,
            bytes_accessed=4 * tokens * columns + 2 * total_keys * columns // PER_GROUP,
            transcendentals=0,
        ),
    )(limits, owners, queries, *pieces, *state)


def pick_kernel(group_size, cache_ref, span_ref, other_ref, own_ref, copied_ref, done):
    request = lax.axis_index("seq") // group_size
    copies = [
        pltpu.make_async_copy(cache_ref.at[1 - request], other_ref, done.at[0]),
        pltpu.make_async_copy(cache_ref.at[request], own_ref, done.at[1]),
        pltpu.make_async_copy(span_ref, copied_ref, done.at[2]),
    ]
    for copy in copies:
        copy.start()
    for copy in copies:
        copy.wait()


def pick(cache, span, group_size):
    return pl.pallas_call(
        functools.partial(pick_kernel, group_size),
        out_shape=[
            jax.ShapeDtypeStruct(cache.shape[1:], cache.dtype),
            jax.ShapeDtypeStruct(cache.shape[1:], cache.dtype),
            jax.ShapeDtypeStruct(span.shape, span.dtype),
        ],
        in_specs=[pl.BlockSpec(memory_space=pltpu.HBM)] * 2,
        out_specs=[pl.BlockSpec(memory_space=pltpu.VMEM)] * 3,
        scratch_shapes=[pltpu.SemaphoreType.DMA((3,))],
        compiler_params=pltpu.CompilerParams(vmem_limit_bytes=8 << 20),
    )(cache, span)


def join_kernel(pieces, *refs):
    parts, (out_ref, done) = refs[:pieces], refs[pieces:]
    columns = [ref.shape[1] for ref in parts[: pieces // 2]]
    side = out_ref.shape[1] // 2
    my_head = lax.axis_index("head")
    copies = []
    for at, ref in enumerate(parts):
        owner = my_head if at < pieces // 2 else 1 - my_head
        first = pl.multiple_of(owner * side + sum(columns[: at % (pieces // 2)]), HD)
        copies.append(
            pltpu.make_async_copy(ref, out_ref.at[:, pl.ds(first, ref.shape[1])], done.at[at])
        )
    for copy in copies:
        copy.start()
    for copy in copies:
        copy.wait()


def put_together(kept, received):
    pieces = len(kept) + len(received)
    rows = kept[0].shape[0]
    columns = sum(one.shape[1] for one in kept + received)
    return pl.pallas_call(
        functools.partial(join_kernel, pieces),
        out_shape=jax.ShapeDtypeStruct((rows, columns), kept[0].dtype),
        in_specs=[pl.BlockSpec(memory_space=pltpu.VMEM)] * pieces,
        out_specs=pl.BlockSpec(memory_space=pl.ANY),
        scratch_shapes=[pltpu.SemaphoreType.DMA((pieces,))],
        compiler_params=pltpu.CompilerParams(vmem_limit_bytes=8 << 20),
    )(*kept, *received)


def body(span_query, span_kv, prefix_cache, prefix_len, block_owner):
    seq_size = lax.axis_size("seq")
    head_size = lax.axis_size("head")
    group_size = seq_size // REQS
    tokens = span_kv.shape[0]
    page = prefix_cache.shape[1]
    groups = span_kv.shape[1] // (2 * HD)
    parts = 2 if groups % 2 == 0 else 1
    bits = [1 << at for at in range(1, group_size.bit_length() - 1)]
    orders = (bits, bits[::-1])

    def send(rows, stage):
        return hop(rows, tuple(order[stage] for order in orders))

    def grown(layout, stage):
        return layout + shifted(layout, 1 << stage)

    stages = len(bits)
    other_page, own_page, span = pick(prefix_cache, span_kv, group_size)
    crossed = hop(other_page, (group_size, group_size))
    span_layout = [(0, SPAN_ROWS, tokens)]
    for stage in range(stages):
        received = send(span if stage else span_kv, stage)
        if stage == 1:
            received = after(pages, received)
        span, span_layout = jnp.concatenate([span, received], axis=0), grown(span_layout, stage)
        if stage == 0:
            crossed = after(span, crossed)
            pages = jnp.concatenate([own_page, crossed], axis=0)
            pages = jnp.concatenate([pages, send(pages, 0)], axis=0)
    span_swapped = hop(span, (1, 1))

    spec = (tokens, page, group_size, head_size, orders)
    common = (prefix_len, block_owner, span_query)
    span_set = (span, span_swapped, span_layout)
    states = [attend(*common, part, parts, [span_set], spec, None) for part in range(parts)]

    page_layout = [(0, OWN_PAGE, page), (0, CROSSED_PAGE, page)]
    page_layout = grown(page_layout, 0)
    for stage in range(1, stages):
        received = send(pages, stage)
        if stage == stages - 1:
            received = after(states[0], received)
        pages, page_layout = jnp.concatenate([pages, received], axis=0), grown(page_layout, stage)
    pages_swapped = hop(pages, (1, 1))
    page_set = (pages, pages_swapped, page_layout)
    results = [
        attend(*common, part, parts, [span_set, page_set], spec, states[part])
        for part in range(parts)
    ]
    if head_size != 2:
        joined = jnp.concatenate([jnp.concatenate(pair, axis=0) for pair in results], axis=1)
        return lax.all_to_all(joined, "head", split_axis=0, concat_axis=1, tiled=True)
    kept = [pair[0] for pair in results]
    received = [lax.ppermute(pair[1], "head", [(0, 1), (1, 0)]) for pair in results]
    return put_together(kept, received)


def solution(mesh):
    placed = (P("seq", "head"), P("seq", "head"), P("seq", None, "head"), P(), P())
    return jax.shard_map(
        body, mesh=mesh, in_specs=placed, out_specs=P(("seq", "head"), None), check_vma=False
    )
```

```python
import functools
import math

import jax
import jax.numpy as jnp
from jax import lax
from jax.experimental import pallas as pl
from jax.experimental.pallas import tpu as pltpu
from jax.sharding import PartitionSpec as P

QH = 64
KVH = 8
HD = 128
REQS = 2
PER_GROUP = QH // KVH
EXP2_SCALE = HD ** (-0.5) * math.log2(math.e)
MASKED = -1e30
KEY_CHUNK = 512
EXTRA_ROWS = 16
SHIFT_STEP = 32.0
LOWEST_TOTAL = 1e-20
SPAN_ROWS, OWN_PAGE, CROSSED_PAGE = range(3)


def hop(value, bit_of_core):
    count = lax.axis_size("seq")
    return lax.ppermute(
        value, "seq", [(source, source ^ bit_of_core[source % 2]) for source in range(count)]
    )


def after(first, value):
    return lax.optimization_barrier((first, value))[1]


def shifted(layout, slots):
    return [(slot + slots, kind, rows) for slot, kind, rows in layout]


def hypercube_order(bits):
    order = [0]
    for bit in bits:
        order = order + [offset ^ bit for offset in order]
    return order


def attend_kernel(spec, layouts, part, block_heads, groups, limit_ref, owner_ref, q_ref, *refs):
    tokens, page, group_size, head_size, orders = spec
    first_phase = len(layouts) == 1
    key_sets, refs = [(refs[2 * at : 2 * at + 2], layout) for at, layout in enumerate(layouts)], refs[
        2 * len(layouts) :
    ]
    (state_sum, state_shift), refs = refs[:2], refs[2:]
    if first_phase:
        page_seen, keys, values = refs[:3]
        weights = refs[3:5]
    else:
        outs = refs[:2]
        page_seen, keys, values = refs[2:5]
        weights, shifts, slow_sum, slow_top = refs[5:7], refs[7:9], refs[9], refs[10]
    half_keys = key_sets[0][0][0].shape[0]
    total_keys = 2 * half_keys
    chunk = min(KEY_CHUNK, total_keys)
    me = lax.axis_index("seq")
    my_head = lax.axis_index("head")
    request = me // group_size
    offsets = [hypercube_order(order) for order in orders]

    def note_page(index, carry):
        page_seen[owner_ref[request, index]] = jnp.clip(limit_ref[request] - index * page, 0, page)
        return carry

    if not first_phase:
        lax.fori_loop(0, owner_ref.shape[1], note_page, 0)

    def extra_rows(layout, half):
        row = lax.broadcasted_iota(jnp.int32, (EXTRA_ROWS, half_keys), 0)
        key = lax.broadcasted_iota(jnp.int32, (EXTRA_ROWS, half_keys), 1)
        holder = me ^ half
        start = 0
        seen = key < 0
        for slot, kind, rows in layout:
            source = holder ^ jnp.where(holder % 2 == 0, offsets[0][slot], offsets[1][slot])
            if kind == SPAN_ROWS:
                count = jnp.where(source <= me, tokens, 0)
            elif kind == OWN_PAGE:
                count = page_seen[source]
            else:
                count = page_seen[source ^ group_size]
            seen = seen | ((key >= start) & (key < start + count))
            start += rows
        mask = jnp.where(seen, jnp.float32(0.0), jnp.float32(MASKED))
        extra = jnp.where(row == 0, mask, jnp.where(row == 1, jnp.float32(1.0), jnp.float32(0.0)))
        return extra.astype(jnp.bfloat16)

    def fill(group, halves, extras):
        for half in range(2):
            column = (part * groups + group) * 2 * HD
            at = pl.ds(half * half_keys, half_keys)
            keys[group, :HD, at] = halves[half][:, pl.ds(column, HD)].T
            keys[group, pl.ds(HD, EXTRA_ROWS), at] = extras[half]
            values[group, at, :HD] = halves[half][:, pl.ds(column + HD, HD)]
        rest = HD - EXTRA_ROWS
        keys[group, HD + EXTRA_ROWS :, :] = jnp.zeros((rest, total_keys), jnp.bfloat16)
        values[group, :, HD:] = jnp.ones((total_keys, HD), jnp.bfloat16)

    block = block_heads * tokens
    blocks_a_group = PER_GROUP // block_heads
    blocks = groups * blocks_a_group
    lane = lax.broadcasted_iota(jnp.int32, (block, HD), 1)
    causal = lax.broadcasted_iota(jnp.int32, (block, tokens), 1) <= (
        lax.broadcasted_iota(jnp.int32, (block, tokens), 0) % tokens
    )

    def query_rows(index):
        first = (part * blocks + index) * block_heads * HD
        columns = [
            pl.ds(pl.multiple_of(first + head * HD, HD), HD) for head in range(block_heads)
        ]
        return jnp.concatenate([q_ref[:, column] for column in columns], axis=0)

    def scores_of(query, group, start, is_span):
        made = jnp.dot(
            query, keys[group, :, pl.ds(start, chunk)], preferred_element_type=jnp.float32
        )
        if start == 0 and is_span:
            own = jnp.where(causal, made[:, :tokens], MASKED)
            made = jnp.concatenate([own, made[:, tokens:]], axis=1)
        return made

    def give(index, result):
        kept = tokens // head_size
        for head in range(block_heads):
            column = pl.ds((index * block_heads + head) * HD, HD)
            one = result[head * tokens : (head + 1) * tokens]
            if head_size == 2:
                low, high = one[:kept], one[kept:]
                outs[0][:, column] = jnp.where(my_head == 0, low, high)
                outs[1][:, column] = jnp.where(my_head == 0, high, low)
            else:
                outs[0][:, column] = one[:kept]
                outs[1][:, column] = one[kept:]

    halves, layout = key_sets[-1]
    extras = [extra_rows(layout, half) for half in range(2)]
    longest = [None] * groups

    def begin(group):
        fill(group, halves, extras)
        key = keys[group, :HD, :].astype(jnp.float32)
        squares = jnp.sum(key * key, axis=0, keepdims=True)
        longest[group] = jnp.max(squares, axis=1, keepdims=True)

    def weigh(index):
        group = index // blocks_a_group
        query = query_rows(index)
        wide = query.astype(jnp.float32)
        bound = jnp.sqrt(jnp.sum(wide * wide, axis=1, keepdims=True) * longest[group])
        shift = jnp.ceil(bound * (1.0 / SHIFT_STEP)) * SHIFT_STEP
        extra = jnp.where(lane == 0, 1.0, jnp.where(lane == 1, -shift, 0.0))
        query = jnp.concatenate([query, extra.astype(jnp.bfloat16)], axis=1)
        shift = jnp.broadcast_to(shift, (block, HD))
        if first_phase:
            state_shift[pl.ds(index * block, block), :] = shift
        else:
            shifts[index % 2][...] = shift
        for start in range(0, total_keys, chunk):
            made = scores_of(query, group, start, first_phase)
            weights[index % 2][:, pl.ds(start, chunk)] = jnp.exp2(made * EXP2_SCALE).astype(
                jnp.bfloat16
            )

    def finish(index, lowest):
        group = index // blocks_a_group
        summed = jnp.dot(
            weights[index % 2][...], values[group], preferred_element_type=jnp.float32
        )
        rows = pl.ds(index * block, block)
        if first_phase:
            state_sum[rows, :] = summed
            return lowest
        old = pl.ds((part * blocks + index) * block, block)
        before, shift = state_shift[old, :], shifts[index % 2][...]
        both = jnp.maximum(before, shift)
        fade_before = jnp.exp2((before - both) * EXP2_SCALE)
        fade = jnp.exp2((shift - both) * EXP2_SCALE)
        total = state_sum[old, HD:] * fade_before + summed[:, HD:] * fade
        result = (state_sum[old, :HD] * fade_before + summed[:, :HD] * fade) / total
        give(index, result.astype(jnp.bfloat16))
        return jnp.minimum(lowest, total)

    begin(0)
    lowest = jnp.ones((block, HD), jnp.float32)
    for index in range(blocks + 1):
        if index >= 1:
            lowest = finish(index - 1, lowest)
        if index < blocks:
            weigh(index)
            if (index + 1) % blocks_a_group == 0 and index + 1 < blocks:
                begin((index + 1) // blocks_a_group)
    if first_phase:
        return

    @pl.when(jnp.min(lowest) < LOWEST_TOTAL)
    def exact():
        for number, (halves, layout) in enumerate(key_sets):
            extras = [extra_rows(layout, half) for half in range(2)]
            for group in range(groups):
                fill(group, halves, extras)

            def one_block(index, carry):
                group = index // blocks_a_group
                extra = (lane == 0).astype(jnp.float32).astype(jnp.bfloat16)
                query = jnp.concatenate([query_rows(index), extra], axis=1)
                rows = pl.ds(pl.multiple_of(index * block, block), block)
                if number == 0:
                    top = jnp.full((block, HD), MASKED, jnp.float32)
                    summed = jnp.zeros((block, 2 * HD), jnp.float32)
                else:
                    top = slow_top[rows, :]
                    summed = slow_sum[rows, :]
                best = top
                for start in range(0, total_keys, chunk):
                    made = scores_of(query, group, start, number == 0)
                    for at in range(0, chunk, HD):
                        best = jnp.maximum(best, made[:, at : at + HD])
                best = jnp.broadcast_to(jnp.max(best, axis=1, keepdims=True), (block, HD))
                fade = jnp.exp2((top - best) * EXP2_SCALE)
                summed = summed * jnp.concatenate([fade, fade], axis=1)
                for start in range(0, total_keys, chunk):
                    made = scores_of(query, group, start, number == 0)
                    parts = [
                        jnp.exp2((made[:, at : at + HD] - best) * EXP2_SCALE)
                        for at in range(0, chunk, HD)
                    ]
                    summed = summed + jnp.dot(
                        jnp.concatenate(parts, axis=1).astype(jnp.bfloat16),
                        values[group, pl.ds(start, chunk), :],
                        preferred_element_type=jnp.float32,
                    )
                slow_top[rows, :] = best
                slow_sum[rows, :] = summed
                return carry

            lax.fori_loop(0, blocks, one_block, 0)
        for index in range(blocks):
            rows = pl.ds(index * block, block)
            give(index, (slow_sum[rows, :HD] / slow_sum[rows, HD:]).astype(jnp.bfloat16))


def attend(limits, owners, queries, part, parts, key_sets, spec, state):
    tokens, _, _, head_size = spec[:4]
    half_keys = key_sets[0][0].shape[0]
    total_keys = 2 * half_keys
    columns = queries.shape[1] // parts
    groups = columns // (PER_GROUP * HD)
    block_heads = 4
    block = block_heads * tokens
    rows = PER_GROUP * groups * tokens
    pieces = [piece for mine, theirs, _ in key_sets for piece in (mine, theirs)]
    layouts = tuple(tuple(layout) for _, _, layout in key_sets)
    operands = queries.size * 2 + sum(piece.size for piece in pieces) * 2 + rows * HD * 12
    scratch = groups * total_keys * HD * 8 + block * total_keys * 4 + rows * HD * 12
    whole = pl.BlockSpec(memory_space=pltpu.VMEM)
    scalars = pl.BlockSpec(memory_space=pltpu.SMEM)
    kept = tokens // head_size
    scratch_shapes = [
        pltpu.SMEM((owners.shape[1],), jnp.int32),
        pltpu.VMEM((groups, 2 * HD, total_keys), jnp.bfloat16),
        pltpu.VMEM((groups, total_keys, 2 * HD), jnp.bfloat16),
    ] + [pltpu.VMEM((block, total_keys), jnp.bfloat16)] * 2
    if state is None:
        state = ()
        out_shape = [
            jax.ShapeDtypeStruct((rows, 2 * HD), jnp.float32),
            jax.ShapeDtypeStruct((rows, HD), jnp.float32),
        ]
    else:
        out_shape = [
            jax.ShapeDtypeStruct((kept, columns), jnp.bfloat16),
            jax.ShapeDtypeStruct((tokens - kept, columns), jnp.bfloat16),
        ]
        scratch_shapes += [pltpu.VMEM((block, HD), jnp.float32)] * 2
        scratch_shapes += [
            pltpu.VMEM((rows, 2 * HD), jnp.float32),
            pltpu.VMEM((rows, HD), jnp.float32),
        ]
    return pl.pallas_call(
        functools.partial(attend_kernel, spec, layouts, part, block_heads, groups),
        out_shape=out_shape,
        in_specs=[scalars] * 2 + [whole] * (1 + len(pieces) + len(state)),
        out_specs=[whole] * 2,
        scratch_shapes=scratch_shapes,
        compiler_params=pltpu.CompilerParams(vmem_limit_bytes=operands + scratch + (6 << 20)),
        cost_estimate=pl.CostEstimate(
            flops=8 * tokens * columns * total_keys,
            bytes_accessed=4 * tokens * columns + 2 * total_keys * columns // PER_GROUP,
            transcendentals=0,
        ),
    )(limits, owners, queries, *pieces, *state)


def pick_kernel(group_size, cache_ref, other_ref, own_ref):
    request = lax.axis_index("seq") // group_size
    other_ref[...] = cache_ref[1 - request]
    own_ref[...] = cache_ref[request]


def pick(cache, group_size):
    whole = pl.BlockSpec(memory_space=pltpu.VMEM)
    return pl.pallas_call(
        functools.partial(pick_kernel, group_size),
        out_shape=[jax.ShapeDtypeStruct(cache.shape[1:], cache.dtype)] * 2,
        in_specs=[whole],
        out_specs=[whole] * 2,
        compiler_params=pltpu.CompilerParams(vmem_limit_bytes=8 << 20),
    )(cache)


def join_kernel(pieces, *refs):
    parts, (out_ref, done) = refs[:pieces], refs[pieces:]
    columns = [ref.shape[1] for ref in parts[: pieces // 2]]
    side = out_ref.shape[1] // 2
    my_head = lax.axis_index("head")
    copies = []
    for at, ref in enumerate(parts):
        owner = my_head if at < pieces // 2 else 1 - my_head
        first = pl.multiple_of(owner * side + sum(columns[: at % (pieces // 2)]), HD)
        copies.append(
            pltpu.make_async_copy(ref, out_ref.at[:, pl.ds(first, ref.shape[1])], done.at[at])
        )
    for copy in copies:
        copy.start()
    for copy in copies:
        copy.wait()


def put_together(kept, received):
    pieces = len(kept) + len(received)
    rows = kept[0].shape[0]
    columns = sum(one.shape[1] for one in kept + received)
    return pl.pallas_call(
        functools.partial(join_kernel, pieces),
        out_shape=jax.ShapeDtypeStruct((rows, columns), kept[0].dtype),
        in_specs=[pl.BlockSpec(memory_space=pltpu.VMEM)] * pieces,
        out_specs=pl.BlockSpec(memory_space=pl.ANY),
        scratch_shapes=[pltpu.SemaphoreType.DMA((pieces,))],
        compiler_params=pltpu.CompilerParams(vmem_limit_bytes=8 << 20),
    )(*kept, *received)


def body(span_query, span_kv, prefix_cache, prefix_len, block_owner):
    seq_size = lax.axis_size("seq")
    head_size = lax.axis_size("head")
    group_size = seq_size // REQS
    tokens = span_kv.shape[0]
    page = prefix_cache.shape[1]
    groups = span_kv.shape[1] // (2 * HD)
    parts = 2 if groups % 2 == 0 else 1
    bits = [1 << at for at in range(1, group_size.bit_length() - 1)]
    orders = (bits, bits[::-1])

    stages = len(bits)

    def send(rows, stage):
        return hop(rows, tuple(order[stage] for order in orders))

    def whole_layout(layout):
        for stage in range(stages):
            layout = layout + shifted(layout, 1 << stage)
        return layout

    span_layout = whole_layout([(0, SPAN_ROWS, tokens)])
    page_layout = whole_layout([(0, OWN_PAGE, page), (0, CROSSED_PAGE, page)])

    other_page, own_page = pick(prefix_cache, group_size)
    crossed = hop(other_page, (group_size, group_size))

    span_early = send(span_kv, stages - 1)
    span_forward = send(span_kv, 0)
    for stage in range(1, stages - 1):
        seen = jnp.concatenate([span_kv, span_forward], axis=0)
        span_forward = jnp.concatenate([span_forward, send(seen, stage)], axis=0)
    span = jnp.concatenate([span_kv, span_forward], axis=0)
    span_late = send(span_forward, stages - 1)
    crossed = after(span, crossed)
    pages = jnp.concatenate([own_page, crossed], axis=0)
    pages = jnp.concatenate([pages, send(pages, 0)], axis=0)
    span_late = after(pages, span_late)
    span = jnp.concatenate([span, span_early, span_late], axis=0)
    span_swapped = hop(span, (1, 1))

    spec = (tokens, page, group_size, head_size, orders)
    common = (prefix_len, block_owner, span_query)
    span_set = (span, span_swapped, span_layout)
    state = attend(*common, 0, 1, [span_set], spec, None)

    for stage in range(1, stages):
        received = send(pages, stage)
        if stage == stages - 1:
            received = after(state, received)
        pages = jnp.concatenate([pages, received], axis=0)
    page_set = (pages, hop(pages, (1, 1)), page_layout)
    results = [
        attend(*common, part, parts, [span_set, page_set], spec, state) for part in range(parts)
    ]
    if head_size != 2:
        rows = jnp.concatenate([jnp.concatenate(pair, axis=0) for pair in results], axis=1)
        return lax.all_to_all(rows, "head", split_axis=0, concat_axis=1, tiled=True)
    kept = [pair[0] for pair in results]
    received = [lax.ppermute(pair[1], "head", [(0, 1), (1, 0)]) for pair in results]
    return put_together(kept, received)


def solution(mesh):
    placed = (P("seq", "head"), P("seq", "head"), P("seq", None, "head"), P(), P())
    return jax.shard_map(
        body, mesh=mesh, in_specs=placed, out_specs=P(("seq", "head"), None), check_vma=False
    )
```

```python
import functools
import math

import jax
import jax.numpy as jnp
from jax import lax
from jax.experimental import pallas as pl
from jax.experimental.pallas import tpu as pltpu
from jax.sharding import PartitionSpec as P

QH = 64
KVH = 8
HD = 128
REQS = 2
PER_GROUP = QH // KVH
EXP2_SCALE = HD ** (-0.5) * math.log2(math.e)
MASKED = -1e30
KEY_CHUNK = 512
EXTRA_ROWS = 16
SHIFT_STEP = 32.0
LOWEST_TOTAL = 1e-20
HIGHEST_TOTAL = 1e30
SPAN_ROWS, OWN_PAGE, CROSSED_PAGE = range(3)


def hop(value, bit_of_core):
    count = lax.axis_size("seq")
    return lax.ppermute(
        value, "seq", [(source, source ^ bit_of_core[source % 2]) for source in range(count)]
    )


def after(first, value):
    return lax.optimization_barrier((first, value))[1]


def shifted(layout, slots):
    return [(slot + slots, kind, rows) for slot, kind, rows in layout]


def hypercube_order(bits):
    order = [0]
    for bit in bits:
        order = order + [offset ^ bit for offset in order]
    return order


def attend_kernel(spec, layouts, part, block_heads, groups, limit_ref, owner_ref, q_ref, *refs):
    tokens, page, group_size, head_size, orders = spec
    first_phase = len(layouts) == 1
    key_sets, refs = [(refs[2 * at : 2 * at + 2], layout) for at, layout in enumerate(layouts)], refs[
        2 * len(layouts) :
    ]
    (state_sum, state_extra), refs = refs[:2], refs[2:]
    if first_phase:
        page_seen, keys, values = refs[:3]
        weights = refs[3:5]
    else:
        outs = refs[:2]
        page_seen, keys, values = refs[2:5]
        weights, slow_sum, slow_top = refs[5:7], refs[7], refs[8]
    half_keys = key_sets[0][0][0].shape[0]
    total_keys = 2 * half_keys
    chunk = min(KEY_CHUNK, total_keys)
    me = lax.axis_index("seq")
    my_head = lax.axis_index("head")
    request = me // group_size
    offsets = [hypercube_order(order) for order in orders]

    def note_page(index, carry):
        page_seen[owner_ref[request, index]] = jnp.clip(limit_ref[request] - index * page, 0, page)
        return carry

    if not first_phase:
        lax.fori_loop(0, owner_ref.shape[1], note_page, 0)

    def extra_rows(layout, half):
        row = lax.broadcasted_iota(jnp.int32, (EXTRA_ROWS, half_keys), 0)
        key = lax.broadcasted_iota(jnp.int32, (EXTRA_ROWS, half_keys), 1)
        holder = me ^ half
        start = 0
        seen = key < 0
        for slot, kind, rows in layout:
            source = holder ^ jnp.where(holder % 2 == 0, offsets[0][slot], offsets[1][slot])
            if kind == SPAN_ROWS:
                count = jnp.where(source <= me, tokens, 0)
            elif kind == OWN_PAGE:
                count = page_seen[source]
            else:
                count = page_seen[source ^ group_size]
            seen = seen | ((key >= start) & (key < start + count))
            start += rows
        mask = jnp.where(seen, jnp.float32(0.0), jnp.float32(MASKED))
        extra = jnp.where(row == 0, mask, jnp.where(row == 1, jnp.float32(1.0), jnp.float32(0.0)))
        return extra.astype(jnp.bfloat16)

    def fill(group, halves, extras):
        for half in range(2):
            column = (part * groups + group) * 2 * HD % halves[half].shape[1]
            at = pl.ds(half * half_keys, half_keys)
            keys[group, :HD, at] = halves[half][:, pl.ds(column, HD)].T
            keys[group, pl.ds(HD, EXTRA_ROWS), at] = extras[half]
            values[group, at, :HD] = halves[half][:, pl.ds(column + HD, HD)]
        rest = HD - EXTRA_ROWS
        keys[group, HD + EXTRA_ROWS :, :] = jnp.zeros((rest, total_keys), jnp.bfloat16)
        values[group, :, HD:] = jnp.ones((total_keys, HD), jnp.bfloat16)

    block = block_heads * tokens
    blocks_a_group = PER_GROUP // block_heads
    blocks = groups * blocks_a_group
    lane = lax.broadcasted_iota(jnp.int32, (block, HD), 1)
    causal = lax.broadcasted_iota(jnp.int32, (block, tokens), 1) <= (
        lax.broadcasted_iota(jnp.int32, (block, tokens), 0) % tokens
    )

    def query_rows(index):
        first = (part * blocks + index) * block_heads * HD
        columns = [
            pl.ds(pl.multiple_of(first + head * HD, HD), HD) for head in range(block_heads)
        ]
        return jnp.concatenate([q_ref[:, column] for column in columns], axis=0)

    def scores_of(query, group, start, is_span):
        made = jnp.dot(
            query, keys[group, :, pl.ds(start, chunk)], preferred_element_type=jnp.float32
        )
        if start == 0 and is_span:
            own = jnp.where(causal, made[:, :tokens], MASKED)
            made = jnp.concatenate([own, made[:, tokens:]], axis=1)
        return made

    def give(index, result):
        kept = tokens // head_size
        for head in range(block_heads):
            column = pl.ds((index * block_heads + head) * HD, HD)
            one = result[head * tokens : (head + 1) * tokens]
            if head_size == 2:
                low, high = one[:kept], one[kept:]
                outs[0][:, column] = jnp.where(my_head == 0, low, high)
                outs[1][:, column] = jnp.where(my_head == 0, high, low)
            else:
                outs[0][:, column] = one[:kept]
                outs[1][:, column] = one[kept:]

    halves, layout = key_sets[-1]
    extras = [extra_rows(layout, half) for half in range(2)]
    longest = [None] * groups

    def begin(group):
        fill(group, halves, extras)
        if first_phase:
            key = keys[group, :HD, :].astype(jnp.float32)
            squares = jnp.sum(key * key, axis=0, keepdims=True)
            longest[group] = jnp.max(squares, axis=1, keepdims=True)

    def weigh(index):
        group = index // blocks_a_group
        query = query_rows(index)
        if first_phase:
            wide = query.astype(jnp.float32)
            bound = jnp.sqrt(jnp.sum(wide * wide, axis=1, keepdims=True) * longest[group])
            shift = jnp.ceil(bound * (1.0 / SHIFT_STEP)) * SHIFT_STEP
            extra = jnp.where(lane == 0, 1.0, jnp.where(lane == 1, -shift, 0.0))
            extra = extra.astype(jnp.bfloat16)
            state_extra[pl.ds(index * block, block), :] = extra
        else:
            extra = state_extra[pl.ds((part * blocks + index) * block, block), :]
        query = jnp.concatenate([query, extra], axis=1)
        for start in range(0, total_keys, chunk):
            made = scores_of(query, group, start, first_phase)
            weights[index % 2][:, pl.ds(start, chunk)] = jnp.exp2(made * EXP2_SCALE).astype(
                jnp.bfloat16
            )

    def finish(index, extremes):
        group = index // blocks_a_group
        summed = jnp.dot(
            weights[index % 2][...], values[group], preferred_element_type=jnp.float32
        )
        rows = pl.ds(index * block, block)
        if first_phase:
            state_sum[rows, :] = summed
            return extremes
        old = pl.ds((part * blocks + index) * block, block)
        summed = summed + state_sum[old, :]
        total = summed[:, HD:]
        give(index, (summed[:, :HD] / total).astype(jnp.bfloat16))
        return jnp.minimum(extremes[0], total), jnp.maximum(extremes[1], total)

    begin(0)
    extremes = (jnp.ones((block, HD), jnp.float32),) * 2
    for index in range(blocks + 1):
        if index >= 1:
            extremes = finish(index - 1, extremes)
        if index < blocks:
            weigh(index)
            if (index + 1) % blocks_a_group == 0 and index + 1 < blocks:
                begin((index + 1) // blocks_a_group)
    if first_phase:
        return

    @pl.when((jnp.min(extremes[0]) < LOWEST_TOTAL) | (jnp.max(extremes[1]) > HIGHEST_TOTAL))
    def exact():
        for number, (halves, layout) in enumerate(key_sets):
            extras = [extra_rows(layout, half) for half in range(2)]
            for group in range(groups):
                fill(group, halves, extras)

            def one_block(index, carry):
                group = index // blocks_a_group
                extra = (lane == 0).astype(jnp.float32).astype(jnp.bfloat16)
                query = jnp.concatenate([query_rows(index), extra], axis=1)
                rows = pl.ds(pl.multiple_of(index * block, block), block)
                if number == 0:
                    top = jnp.full((block, HD), MASKED, jnp.float32)
                    summed = jnp.zeros((block, 2 * HD), jnp.float32)
                else:
                    top = slow_top[rows, :]
                    summed = slow_sum[rows, :]
                best = top
                for start in range(0, total_keys, chunk):
                    made = scores_of(query, group, start, number == 0)
                    for at in range(0, chunk, HD):
                        best = jnp.maximum(best, made[:, at : at + HD])
                best = jnp.broadcast_to(jnp.max(best, axis=1, keepdims=True), (block, HD))
                fade = jnp.exp2((top - best) * EXP2_SCALE)
                summed = summed * jnp.concatenate([fade, fade], axis=1)
                for start in range(0, total_keys, chunk):
                    made = scores_of(query, group, start, number == 0)
                    parts = [
                        jnp.exp2((made[:, at : at + HD] - best) * EXP2_SCALE)
                        for at in range(0, chunk, HD)
                    ]
                    summed = summed + jnp.dot(
                        jnp.concatenate(parts, axis=1).astype(jnp.bfloat16),
                        values[group, pl.ds(start, chunk), :],
                        preferred_element_type=jnp.float32,
                    )
                slow_top[rows, :] = best
                slow_sum[rows, :] = summed
                return carry

            lax.fori_loop(0, blocks, one_block, 0)
        for index in range(blocks):
            rows = pl.ds(index * block, block)
            give(index, (slow_sum[rows, :HD] / slow_sum[rows, HD:]).astype(jnp.bfloat16))


def attend(limits, owners, queries, part, parts, key_sets, spec, state):
    tokens, _, _, head_size = spec[:4]
    half_keys = key_sets[0][0].shape[0]
    total_keys = 2 * half_keys
    columns = queries.shape[1] // parts
    groups = columns // (PER_GROUP * HD)
    block_heads = 4
    block = block_heads * tokens
    rows = PER_GROUP * groups * tokens
    pieces = [piece for mine, theirs, _ in key_sets for piece in (mine, theirs)]
    layouts = tuple(tuple(layout) for _, _, layout in key_sets)
    operands = queries.size * 2 + sum(piece.size for piece in pieces) * 2 + rows * HD * 12
    scratch = groups * total_keys * HD * 8 + block * total_keys * 4 + rows * HD * 12
    whole = pl.BlockSpec(memory_space=pltpu.VMEM)
    scalars = pl.BlockSpec(memory_space=pltpu.SMEM)
    kept = tokens // head_size
    scratch_shapes = [
        pltpu.SMEM((owners.shape[1],), jnp.int32),
        pltpu.VMEM((groups, 2 * HD, total_keys), jnp.bfloat16),
        pltpu.VMEM((groups, total_keys, 2 * HD), jnp.bfloat16),
    ] + [pltpu.VMEM((block, total_keys), jnp.bfloat16)] * 2
    if state is None:
        state = ()
        out_shape = [
            jax.ShapeDtypeStruct((rows, 2 * HD), jnp.float32),
            jax.ShapeDtypeStruct((rows, HD), jnp.bfloat16),
        ]
    else:
        out_shape = [
            jax.ShapeDtypeStruct((kept, columns), jnp.bfloat16),
            jax.ShapeDtypeStruct((tokens - kept, columns), jnp.bfloat16),
        ]
        scratch_shapes += [
            pltpu.VMEM((rows, 2 * HD), jnp.float32),
            pltpu.VMEM((rows, HD), jnp.float32),
        ]
    return pl.pallas_call(
        functools.partial(attend_kernel, spec, layouts, part, block_heads, groups),
        out_shape=out_shape,
        in_specs=[scalars] * 2 + [whole] * (1 + len(pieces) + len(state)),
        out_specs=[whole] * 2,
        scratch_shapes=scratch_shapes,
        compiler_params=pltpu.CompilerParams(vmem_limit_bytes=operands + scratch + (6 << 20)),
        cost_estimate=pl.CostEstimate(
            flops=8 * tokens * columns * total_keys,
            bytes_accessed=4 * tokens * columns + 2 * total_keys * columns // PER_GROUP,
            transcendentals=0,
        ),
    )(limits, owners, queries, *pieces, *state)


def pick_kernel(group_size, cache_ref, other_ref, own_ref):
    request = lax.axis_index("seq") // group_size
    other_ref[...] = cache_ref[1 - request]
    own_ref[...] = cache_ref[request]


def pick(cache, group_size):
    whole = pl.BlockSpec(memory_space=pltpu.VMEM)
    return pl.pallas_call(
        functools.partial(pick_kernel, group_size),
        out_shape=[jax.ShapeDtypeStruct(cache.shape[1:], cache.dtype)] * 2,
        in_specs=[whole],
        out_specs=[whole] * 2,
        compiler_params=pltpu.CompilerParams(vmem_limit_bytes=8 << 20),
    )(cache)


def join_kernel(spots, count, *refs):
    parts, (out_ref, done) = refs[len(refs) - 2 - count : -2], refs[-2:]
    side = out_ref.shape[1] // 2
    my_head = lax.axis_index("head")
    copies = []
    for at, (ref, (received, start)) in enumerate(zip(parts, spots)):
        owner = 1 - my_head if received else my_head
        first = pl.multiple_of(owner * side + start, HD)
        copies.append(
            pltpu.make_async_copy(ref, out_ref.at[:, pl.ds(first, ref.shape[1])], done.at[at])
        )
    for copy in copies:
        copy.start()
    for copy in copies:
        copy.wait()


def join(pieces, spots, columns, partial):
    earlier = [] if partial is None else [partial]
    return pl.pallas_call(
        functools.partial(join_kernel, spots, len(pieces)),
        out_shape=jax.ShapeDtypeStruct((pieces[0].shape[0], columns), pieces[0].dtype),
        in_specs=[pl.BlockSpec(memory_space=pl.ANY)] * len(earlier)
        + [pl.BlockSpec(memory_space=pltpu.VMEM)] * len(pieces),
        out_specs=pl.BlockSpec(memory_space=pl.ANY),
        scratch_shapes=[pltpu.SemaphoreType.DMA((len(pieces),))],
        input_output_aliases={0: 0} if earlier else {},
        compiler_params=pltpu.CompilerParams(vmem_limit_bytes=8 << 20),
    )(*earlier, *pieces)


def put_together(kept, received):
    columns = kept[0].shape[1]
    pieces = kept + received
    spots = [(at >= len(kept), at % len(kept) * columns) for at in range(len(pieces))]
    out = join(pieces[:-1], spots[:-1], columns * len(pieces), None)
    return join(pieces[-1:], spots[-1:], columns * len(pieces), out)


def body(span_query, span_kv, prefix_cache, prefix_len, block_owner):
    seq_size = lax.axis_size("seq")
    head_size = lax.axis_size("head")
    group_size = seq_size // REQS
    tokens = span_kv.shape[0]
    page = prefix_cache.shape[1]
    groups = span_kv.shape[1] // (2 * HD)
    parts = 2 if groups % 2 == 0 else 1
    bits = [1 << at for at in range(1, group_size.bit_length() - 1)]
    orders = (bits, bits[::-1])

    stages = len(bits)

    def send(rows, stage):
        return hop(rows, tuple(order[stage] for order in orders))

    def whole_layout(layout):
        for stage in range(stages):
            layout = layout + shifted(layout, 1 << stage)
        return layout

    span_layout = whole_layout([(0, SPAN_ROWS, tokens)])
    page_layout = whole_layout([(0, OWN_PAGE, page), (0, CROSSED_PAGE, page)])

    other_page, own_page = pick(prefix_cache, group_size)
    crossed = hop(other_page, (group_size, group_size))

    span_forward = send(span_kv, 0)
    span_early = send(span_kv, stages - 1)
    if stages == 2:
        across = sum(bits)
        span_late = hop(span_kv, (across, across))
    for stage in range(1, stages - 1):
        seen = jnp.concatenate([span_kv, span_forward], axis=0)
        span_forward = jnp.concatenate([span_forward, send(seen, stage)], axis=0)
    if stages != 2:
        span_late = send(span_forward, stages - 1)
    span = jnp.concatenate([span_kv, span_forward], axis=0)
    crossed = after(span, crossed)
    pages = jnp.concatenate([own_page, crossed], axis=0)
    pages = jnp.concatenate([pages, send(pages, 0)], axis=0)
    span_late = after(pages, span_late)
    span = jnp.concatenate([span, span_early, span_late], axis=0)
    span_swapped = hop(span, (1, 1))

    spec = (tokens, page, group_size, head_size, orders)
    common = (prefix_len, block_owner, span_query)
    span_set = (span, span_swapped, span_layout)
    state = attend(*common, 0, 1, [span_set], spec, None)

    for stage in range(1, stages):
        received = send(pages, stage)
        if stage == stages - 1:
            received = after(state, received)
        pages = jnp.concatenate([pages, received], axis=0)
    columns = pages.shape[1] // parts
    results = []
    for part in range(parts):
        theirs = hop(pages[:, part * columns : (part + 1) * columns], (1, 1))
        page_set = (pages, theirs, page_layout)
        results.append(attend(*common, part, parts, [span_set, page_set], spec, state))
    if head_size != 2:
        rows = jnp.concatenate([jnp.concatenate(pair, axis=0) for pair in results], axis=1)
        return lax.all_to_all(rows, "head", split_axis=0, concat_axis=1, tiled=True)
    kept = [pair[0] for pair in results]
    received = [lax.ppermute(pair[1], "head", [(0, 1), (1, 0)]) for pair in results]
    return put_together(kept, received)


def solution(mesh):
    placed = (P("seq", "head"), P("seq", "head"), P("seq", None, "head"), P(), P())
    return jax.shard_map(
        body, mesh=mesh, in_specs=placed, out_specs=P(("seq", "head"), None), check_vma=False
    )
```

```python
import functools
import math

import jax
import jax.numpy as jnp
from jax import lax
from jax.experimental import pallas as pl
from jax.experimental.pallas import tpu as pltpu
from jax.sharding import PartitionSpec as P

QH = 64
KVH = 8
HD = 128
REQS = 2
PER_GROUP = QH // KVH
EXP2_SCALE = HD ** (-0.5) * math.log2(math.e)
MASKED = -1e30
KEY_CHUNK = 512
EXTRA_ROWS = 16
SHIFT_STEP = 32.0
LOWEST_TOTAL = 1e-20
HIGHEST_TOTAL = 1e30
SPAN_ROWS, OWN_PAGE, CROSSED_PAGE = range(3)


def hop(value, bit_of_core):
    count = lax.axis_size("seq")
    return lax.ppermute(
        value, "seq", [(source, source ^ bit_of_core[source % 2]) for source in range(count)]
    )


def together(*values):
    return lax.optimization_barrier(values)


def shifted(layout, slots):
    return [(slot + slots, kind, rows) for slot, kind, rows in layout]


def hypercube_order(bits):
    order = [0]
    for bit in bits:
        order = order + [offset ^ bit for offset in order]
    return order


def attend_kernel(spec, layouts, part, block_heads, groups, limit_ref, owner_ref, q_ref, *refs):
    tokens, page, group_size, head_size, orders = spec
    first_phase = len(layouts) == 1
    key_sets = []
    for layout, counts in layouts:
        halves = []
        for count in counts:
            halves.append(refs[:count])
            refs = refs[count:]
        key_sets.append((halves, layout))
    (state_sum, state_extra), refs = refs[:2], refs[2:]
    if first_phase:
        page_seen, keys, values = refs[:3]
        weights = refs[3:5]
    else:
        outs = refs[:2]
        page_seen, keys, values = refs[2:5]
        weights, slow_sum, slow_top = refs[5:7], refs[7], refs[8]
    half_keys = sum(ref.shape[0] for ref in key_sets[0][0][0])
    total_keys = 2 * half_keys
    chunk = min(KEY_CHUNK, total_keys)
    me = lax.axis_index("seq")
    my_head = lax.axis_index("head")
    request = me // group_size
    offsets = [hypercube_order(order) for order in orders]

    def note_page(index, carry):
        page_seen[owner_ref[request, index]] = jnp.clip(limit_ref[request] - index * page, 0, page)
        return carry

    if not first_phase:
        lax.fori_loop(0, owner_ref.shape[1], note_page, 0)

    def extra_rows(layout, half):
        row = lax.broadcasted_iota(jnp.int32, (EXTRA_ROWS, half_keys), 0)
        key = lax.broadcasted_iota(jnp.int32, (EXTRA_ROWS, half_keys), 1)
        holder = me ^ half
        start = 0
        seen = key < 0
        for slot, kind, rows in layout:
            source = holder ^ jnp.where(holder % 2 == 0, offsets[0][slot], offsets[1][slot])
            if kind == SPAN_ROWS:
                count = jnp.where(source <= me, tokens, 0)
            elif kind == OWN_PAGE:
                count = page_seen[source]
            else:
                count = page_seen[source ^ group_size]
            seen = seen | ((key >= start) & (key < start + count))
            start += rows
        mask = jnp.where(seen, jnp.float32(0.0), jnp.float32(MASKED))
        extra = jnp.where(row == 0, mask, jnp.where(row == 1, jnp.float32(1.0), jnp.float32(0.0)))
        return extra.astype(jnp.bfloat16)

    def fill(group, halves, extras):
        for half in range(2):
            start = half * half_keys
            keys[group, pl.ds(HD, EXTRA_ROWS), pl.ds(start, half_keys)] = extras[half]
            for ref in halves[half]:
                column = (part * groups + group) * 2 * HD % ref.shape[1]
                at = pl.ds(start, ref.shape[0])
                keys[group, :HD, at] = ref[:, pl.ds(column, HD)].T
                values[group, at, :HD] = ref[:, pl.ds(column + HD, HD)]
                start += ref.shape[0]
        rest = HD - EXTRA_ROWS
        keys[group, HD + EXTRA_ROWS :, :] = jnp.zeros((rest, total_keys), jnp.bfloat16)
        values[group, :, HD:] = jnp.ones((total_keys, HD), jnp.bfloat16)

    block = block_heads * tokens
    blocks_a_group = PER_GROUP // block_heads
    blocks = groups * blocks_a_group
    lane = lax.broadcasted_iota(jnp.int32, (block, HD), 1)
    causal = lax.broadcasted_iota(jnp.int32, (block, tokens), 1) <= (
        lax.broadcasted_iota(jnp.int32, (block, tokens), 0) % tokens
    )

    def query_rows(index):
        first = (part * blocks + index) * block_heads * HD
        columns = [
            pl.ds(pl.multiple_of(first + head * HD, HD), HD) for head in range(block_heads)
        ]
        return jnp.concatenate([q_ref[:, column] for column in columns], axis=0)

    def scores_of(query, group, start, is_span):
        made = jnp.dot(
            query, keys[group, :, pl.ds(start, chunk)], preferred_element_type=jnp.float32
        )
        if start == 0 and is_span:
            own = jnp.where(causal, made[:, :tokens], MASKED)
            made = jnp.concatenate([own, made[:, tokens:]], axis=1)
        return made

    def give(index, result):
        kept = tokens // head_size
        for head in range(block_heads):
            column = pl.ds((index * block_heads + head) * HD, HD)
            one = result[head * tokens : (head + 1) * tokens]
            if head_size == 2:
                low, high = one[:kept], one[kept:]
                outs[0][:, column] = jnp.where(my_head == 0, low, high)
                outs[1][:, column] = jnp.where(my_head == 0, high, low)
            else:
                outs[0][:, column] = one[:kept]
                outs[1][:, column] = one[kept:]

    halves, layout = key_sets[-1]
    extras = [extra_rows(layout, half) for half in range(2)]
    longest = [None] * groups

    def begin(group):
        fill(group, halves, extras)
        if first_phase:
            key = keys[group, :HD, :].astype(jnp.float32)
            squares = jnp.sum(key * key, axis=0, keepdims=True)
            longest[group] = jnp.max(squares, axis=1, keepdims=True)

    def weigh(index):
        group = index // blocks_a_group
        query = query_rows(index)
        if first_phase:
            wide = query.astype(jnp.float32)
            bound = jnp.sqrt(jnp.sum(wide * wide, axis=1, keepdims=True) * longest[group])
            shift = jnp.ceil(bound * (1.0 / SHIFT_STEP)) * SHIFT_STEP
            extra = jnp.where(lane == 0, 1.0, jnp.where(lane == 1, -shift, 0.0))
            extra = extra.astype(jnp.bfloat16)
            state_extra[pl.ds(index * block, block), :] = extra
        else:
            extra = state_extra[pl.ds((part * blocks + index) * block, block), :]
        query = jnp.concatenate([query, extra], axis=1)
        for start in range(0, total_keys, chunk):
            made = scores_of(query, group, start, first_phase)
            weights[index % 2][:, pl.ds(start, chunk)] = jnp.exp2(made * EXP2_SCALE).astype(
                jnp.bfloat16
            )

    def finish(index, extremes):
        group = index // blocks_a_group
        summed = jnp.dot(
            weights[index % 2][...], values[group], preferred_element_type=jnp.float32
        )
        rows = pl.ds(index * block, block)
        if first_phase:
            state_sum[rows, :] = summed
            return extremes
        old = pl.ds((part * blocks + index) * block, block)
        summed = summed + state_sum[old, :]
        total = summed[:, HD:]
        give(index, (summed[:, :HD] / total).astype(jnp.bfloat16))
        return jnp.minimum(extremes[0], total), jnp.maximum(extremes[1], total)

    begin(0)
    extremes = (jnp.ones((block, HD), jnp.float32),) * 2
    for index in range(blocks + 1):
        if index >= 1:
            extremes = finish(index - 1, extremes)
        if index < blocks:
            weigh(index)
            if (index + 1) % blocks_a_group == 0 and index + 1 < blocks:
                begin((index + 1) // blocks_a_group)
    if first_phase:
        return

    @pl.when((jnp.min(extremes[0]) < LOWEST_TOTAL) | (jnp.max(extremes[1]) > HIGHEST_TOTAL))
    def exact():
        for number, (halves, layout) in enumerate(key_sets):
            extras = [extra_rows(layout, half) for half in range(2)]
            for group in range(groups):
                fill(group, halves, extras)

            def one_block(index, carry):
                group = index // blocks_a_group
                extra = (lane == 0).astype(jnp.float32).astype(jnp.bfloat16)
                query = jnp.concatenate([query_rows(index), extra], axis=1)
                rows = pl.ds(pl.multiple_of(index * block, block), block)
                if number == 0:
                    top = jnp.full((block, HD), MASKED, jnp.float32)
                    summed = jnp.zeros((block, 2 * HD), jnp.float32)
                else:
                    top = slow_top[rows, :]
                    summed = slow_sum[rows, :]
                best = top
                for start in range(0, total_keys, chunk):
                    made = scores_of(query, group, start, number == 0)
                    for at in range(0, chunk, HD):
                        best = jnp.maximum(best, made[:, at : at + HD])
                best = jnp.broadcast_to(jnp.max(best, axis=1, keepdims=True), (block, HD))
                fade = jnp.exp2((top - best) * EXP2_SCALE)
                summed = summed * jnp.concatenate([fade, fade], axis=1)
                for start in range(0, total_keys, chunk):
                    made = scores_of(query, group, start, number == 0)
                    parts = [
                        jnp.exp2((made[:, at : at + HD] - best) * EXP2_SCALE)
                        for at in range(0, chunk, HD)
                    ]
                    summed = summed + jnp.dot(
                        jnp.concatenate(parts, axis=1).astype(jnp.bfloat16),
                        values[group, pl.ds(start, chunk), :],
                        preferred_element_type=jnp.float32,
                    )
                slow_top[rows, :] = best
                slow_sum[rows, :] = summed
                return carry

            lax.fori_loop(0, blocks, one_block, 0)
        for index in range(blocks):
            rows = pl.ds(index * block, block)
            give(index, (slow_sum[rows, :HD] / slow_sum[rows, HD:]).astype(jnp.bfloat16))


def attend(limits, owners, queries, part, parts, key_sets, spec, state):
    tokens, _, _, head_size = spec[:4]
    half_keys = sum(piece.shape[0] for piece in key_sets[0][0])
    total_keys = 2 * half_keys
    columns = queries.shape[1] // parts
    groups = columns // (PER_GROUP * HD)
    block_heads = 4
    block = block_heads * tokens
    rows = PER_GROUP * groups * tokens
    pieces = [piece for mine, theirs, _ in key_sets for piece in mine + theirs]
    layouts = tuple(
        (tuple(layout), (len(mine), len(theirs))) for mine, theirs, layout in key_sets
    )
    operands = queries.size * 2 + sum(piece.size for piece in pieces) * 2 + rows * HD * 12
    scratch = groups * total_keys * HD * 8 + block * total_keys * 4 + rows * HD * 12
    whole = pl.BlockSpec(memory_space=pltpu.VMEM)
    scalars = pl.BlockSpec(memory_space=pltpu.SMEM)
    kept = tokens // head_size
    scratch_shapes = [
        pltpu.SMEM((owners.shape[1],), jnp.int32),
        pltpu.VMEM((groups, 2 * HD, total_keys), jnp.bfloat16),
        pltpu.VMEM((groups, total_keys, 2 * HD), jnp.bfloat16),
    ] + [pltpu.VMEM((block, total_keys), jnp.bfloat16)] * 2
    if state is None:
        state = ()
        out_shape = [
            jax.ShapeDtypeStruct((rows, 2 * HD), jnp.float32),
            jax.ShapeDtypeStruct((rows, HD), jnp.bfloat16),
        ]
    else:
        out_shape = [
            jax.ShapeDtypeStruct((kept, columns), jnp.bfloat16),
            jax.ShapeDtypeStruct((tokens - kept, columns), jnp.bfloat16),
        ]
        scratch_shapes += [
            pltpu.VMEM((rows, 2 * HD), jnp.float32),
            pltpu.VMEM((rows, HD), jnp.float32),
        ]
    return pl.pallas_call(
        functools.partial(attend_kernel, spec, layouts, part, block_heads, groups),
        out_shape=out_shape,
        in_specs=[scalars] * 2 + [whole] * (1 + len(pieces) + len(state)),
        out_specs=[whole] * 2,
        scratch_shapes=scratch_shapes,
        compiler_params=pltpu.CompilerParams(vmem_limit_bytes=operands + scratch + (6 << 20)),
        cost_estimate=pl.CostEstimate(
            flops=8 * tokens * columns * total_keys,
            bytes_accessed=4 * tokens * columns + 2 * total_keys * columns // PER_GROUP,
            transcendentals=0,
        ),
    )(limits, owners, queries, *pieces, *state)


def pick_kernel(group_size, cache_ref, other_ref, own_ref):
    request = lax.axis_index("seq") // group_size
    other_ref[...] = cache_ref[1 - request]
    own_ref[...] = cache_ref[request]


def pick(cache, group_size):
    whole = pl.BlockSpec(memory_space=pltpu.VMEM)
    return pl.pallas_call(
        functools.partial(pick_kernel, group_size),
        out_shape=[jax.ShapeDtypeStruct(cache.shape[1:], cache.dtype)] * 2,
        in_specs=[whole],
        out_specs=[whole] * 2,
        compiler_params=pltpu.CompilerParams(vmem_limit_bytes=8 << 20),
    )(cache)


def join_kernel(spots, count, *refs):
    parts, (out_ref, done) = refs[len(refs) - 2 - count : -2], refs[-2:]
    side = out_ref.shape[1] // 2
    my_head = lax.axis_index("head")
    copies = []
    for at, (ref, (received, start)) in enumerate(zip(parts, spots)):
        owner = 1 - my_head if received else my_head
        first = pl.multiple_of(owner * side + start, HD)
        copies.append(
            pltpu.make_async_copy(ref, out_ref.at[:, pl.ds(first, ref.shape[1])], done.at[at])
        )
    for copy in copies:
        copy.start()
    for copy in copies:
        copy.wait()


def join(pieces, spots, columns, partial):
    earlier = [] if partial is None else [partial]
    return pl.pallas_call(
        functools.partial(join_kernel, spots, len(pieces)),
        out_shape=jax.ShapeDtypeStruct((pieces[0].shape[0], columns), pieces[0].dtype),
        in_specs=[pl.BlockSpec(memory_space=pl.ANY)] * len(earlier)
        + [pl.BlockSpec(memory_space=pltpu.VMEM)] * len(pieces),
        out_specs=pl.BlockSpec(memory_space=pl.ANY),
        scratch_shapes=[pltpu.SemaphoreType.DMA((len(pieces),))],
        input_output_aliases={0: 0} if earlier else {},
        compiler_params=pltpu.CompilerParams(vmem_limit_bytes=8 << 20),
    )(*earlier, *pieces)


def put_together(kept, received):
    columns = kept[0].shape[1]
    pieces = kept + received
    spots = [(at >= len(kept), at % len(kept) * columns) for at in range(len(pieces))]
    out = join(pieces[:-1], spots[:-1], columns * len(pieces), None)
    return join(pieces[-1:], spots[-1:], columns * len(pieces), out)


def body(span_query, span_kv, prefix_cache, prefix_len, block_owner):
    seq_size = lax.axis_size("seq")
    head_size = lax.axis_size("head")
    group_size = seq_size // REQS
    tokens = span_kv.shape[0]
    page = prefix_cache.shape[1]
    groups = span_kv.shape[1] // (2 * HD)
    parts = 2 if groups % 2 == 0 else 1
    bits = [1 << at for at in range(1, group_size.bit_length() - 1)]
    orders = (bits, bits[::-1])

    stages = len(bits)

    def send(rows, stage):
        return hop(rows, tuple(order[stage] for order in orders))

    def swap_cores(pieces):
        return hop(pieces[0] if len(pieces) == 1 else jnp.concatenate(pieces, axis=0), (1, 1))

    def whole_layout(layout):
        for stage in range(stages):
            layout = layout + shifted(layout, 1 << stage)
        return layout

    span_layout = whole_layout([(0, SPAN_ROWS, tokens)])
    page_layout = whole_layout([(0, OWN_PAGE, page), (0, CROSSED_PAGE, page)])

    other_page, own_page = pick(prefix_cache, group_size)
    crossed = hop(other_page, (group_size, group_size))

    span_early = send(span_kv, stages - 1)
    span_forward = send(span_kv, 0)
    for stage in range(1, stages - 1):
        seen = jnp.concatenate([span_kv, span_forward], axis=0)
        span_forward = jnp.concatenate([span_forward, send(seen, stage)], axis=0)
    span_late = send(span_forward, stages - 1)
    span_forward, crossed = together(span_forward, crossed)
    pages = [jnp.concatenate([own_page, crossed], axis=0)]
    pages.append(send(pages[0], 0))
    span_early, span_late = together(span_early, span_late)
    pages[1], span_late = together(pages[1], span_late)
    span = [jnp.concatenate([span_kv, span_forward, span_early, span_late], axis=0)]
    span_swapped = [swap_cores(span)]

    spec = (tokens, page, group_size, head_size, orders)
    common = (prefix_len, block_owner, span_query)
    span_set = (span, span_swapped, span_layout)
    state = attend(*common, 0, 1, [span_set], spec, None)

    for stage in range(1, stages - 1):
        pages.append(send(jnp.concatenate(pages, axis=0), stage))
    columns = span_kv.shape[1] // parts
    cuts = [slice(part * columns, (part + 1) * columns) for part in range(parts)]
    held = [jnp.concatenate([piece[:, cut] for piece in pages], axis=0) for cut in cuts]
    arrived = [send(rows, stages - 1) for rows in held]
    results = []
    for part in range(parts):
        arrived[part], state = together(arrived[part], state)
        mine = [held[part], arrived[part]]
        page_set = (mine, [swap_cores(mine)], page_layout)
        results.append(attend(*common, part, parts, [span_set, page_set], spec, state))
    if head_size != 2:
        rows = jnp.concatenate([jnp.concatenate(pair, axis=0) for pair in results], axis=1)
        return lax.all_to_all(rows, "head", split_axis=0, concat_axis=1, tiled=True)
    kept = [pair[0] for pair in results]
    received = [lax.ppermute(pair[1], "head", [(0, 1), (1, 0)]) for pair in results]
    return put_together(kept, received)


def solution(mesh):
    placed = (P("seq", "head"), P("seq", "head"), P("seq", None, "head"), P(), P())
    return jax.shard_map(
        body, mesh=mesh, in_specs=placed, out_specs=P(("seq", "head"), None), check_vma=False
    )
```

```python
import functools
import math

import jax
import jax.numpy as jnp
from jax import lax
from jax.experimental import pallas as pl
from jax.experimental.pallas import tpu as pltpu
from jax.sharding import PartitionSpec as P

QH = 64
KVH = 8
HD = 128
REQS = 2
PER_GROUP = QH // KVH
EXP2_SCALE = HD ** (-0.5) * math.log2(math.e)
MASKED = -1e30
KEY_CHUNK = 256
SHIFT_STEP = 32.0
LOWEST_TOTAL = 1e-20
HIGHEST_TOTAL = 1e30
SPAN_ROWS, OWN_PAGE, CROSSED_PAGE = range(3)


def hop(value, bit_of_core):
    count = lax.axis_size("seq")
    return lax.ppermute(
        value, "seq", [(source, source ^ bit_of_core[source % 2]) for source in range(count)]
    )


def together(*values):
    return lax.optimization_barrier(values)


def shifted(layout, slots):
    return [(slot + slots, kind, rows) for slot, kind, rows in layout]


def hypercube_order(bits):
    order = [0]
    for bit in bits:
        order = order + [offset ^ bit for offset in order]
    return order


def attend_kernel(spec, layouts, part, block_heads, groups, limit_ref, owner_ref, q_ref, *refs):
    tokens, page, group_size, head_size, orders = spec
    first_phase = len(layouts) == 1
    key_sets = []
    for layout, counts in layouts:
        halves = []
        for count in counts:
            halves.append(refs[:count])
            refs = refs[count:]
        key_sets.append((halves, layout))
    (state_sum, state_extra), refs = refs[:2], refs[2:]
    if first_phase:
        page_seen, keys, values = refs[:3]
        weights = refs[3:5]
    else:
        outs = refs[:2]
        page_seen, keys, values = refs[2:5]
        weights, slow_sum, slow_top = refs[5:7], refs[7], refs[8]
    chunk = KEY_CHUNK
    me = lax.axis_index("seq")
    my_head = lax.axis_index("head")
    request = me // group_size
    offsets = [hypercube_order(order) for order in orders]

    def note_page(index, carry):
        page_seen[owner_ref[request, index]] = jnp.clip(limit_ref[request] - index * page, 0, page)
        return carry

    if not first_phase:
        lax.fori_loop(0, owner_ref.shape[1], note_page, 0)

    def extra_columns(layout, half):
        holder = me ^ half
        pieces = []
        for slot, kind, rows in layout:
            source = holder ^ jnp.where(holder % 2 == 0, offsets[0][slot], offsets[1][slot])
            if kind == SPAN_ROWS:
                count = jnp.where(source <= me, tokens, 0)
            elif kind == OWN_PAGE:
                count = page_seen[source]
            else:
                count = page_seen[source ^ group_size]
            row = lax.broadcasted_iota(jnp.int32, (rows, HD), 0)
            column = lax.broadcasted_iota(jnp.int32, (rows, HD), 1)
            mask = jnp.where(row < count, jnp.float32(0.0), jnp.float32(MASKED))
            one = jnp.where(column == 1, jnp.float32(1.0), jnp.float32(0.0))
            pieces.append(jnp.where(column == 0, mask, one).astype(jnp.bfloat16))
        return pieces

    def key_count(halves):
        return sum(ref.shape[0] for half in halves for ref in half)

    def fill(group, halves, extras):
        total_keys = key_count(halves)
        half_keys = total_keys // 2
        for half in range(2):
            start = half * half_keys
            for piece in extras[half]:
                keys[group, pl.ds(start, piece.shape[0]), HD:] = piece
                start += piece.shape[0]
            start = half * half_keys
            for ref in halves[half]:
                column = (part * groups + group) * 2 * HD % ref.shape[1]
                at = pl.ds(start, ref.shape[0])
                keys[group, at, :HD] = ref[:, pl.ds(column, HD)]
                values[group, at, :HD] = ref[:, pl.ds(column + HD, HD)]
                start += ref.shape[0]
        values[group, :total_keys, HD:] = jnp.ones((total_keys, HD), jnp.bfloat16)

    block = block_heads * tokens
    blocks_a_group = PER_GROUP // block_heads
    blocks = groups * blocks_a_group
    lane = lax.broadcasted_iota(jnp.int32, (block, HD), 1)
    causal = lax.broadcasted_iota(jnp.int32, (block, tokens), 1) <= (
        lax.broadcasted_iota(jnp.int32, (block, tokens), 0) % tokens
    )

    def query_rows(index):
        first = (part * blocks + index) * block_heads * HD
        columns = [
            pl.ds(pl.multiple_of(first + head * HD, HD), HD) for head in range(block_heads)
        ]
        return jnp.concatenate([q_ref[:, column] for column in columns], axis=0)

    def scores_of(query, group, start, is_span):
        made = lax.dot_general(
            query,
            keys[group, pl.ds(start, chunk), :],
            (((1,), (1,)), ((), ())),
            preferred_element_type=jnp.float32,
        )
        if start == 0 and is_span:
            own = jnp.where(causal, made[:, :tokens], MASKED)
            made = jnp.concatenate([own, made[:, tokens:]], axis=1)
        return made

    def give(index, result):
        kept = tokens // head_size
        for head in range(block_heads):
            column = pl.ds((index * block_heads + head) * HD, HD)
            one = result[head * tokens : (head + 1) * tokens]
            if head_size == 2:
                low, high = one[:kept], one[kept:]
                outs[0][:, column] = jnp.where(my_head == 0, low, high)
                outs[1][:, column] = jnp.where(my_head == 0, high, low)
            else:
                outs[0][:, column] = one[:kept]
                outs[1][:, column] = one[kept:]

    halves, layout = key_sets[-1]
    total_keys = key_count(halves)
    extras = [extra_columns(layout, half) for half in range(2)]
    longest = [None] * groups

    def begin(group):
        fill(group, halves, extras)
        if first_phase:
            key = keys[group, :total_keys, :HD].astype(jnp.float32)
            squares = jnp.sum(key * key, axis=1, keepdims=True)
            longest[group] = jnp.max(squares, axis=0, keepdims=True)

    def weigh(index):
        group = index // blocks_a_group
        query = query_rows(index)
        if first_phase:
            wide = query.astype(jnp.float32)
            bound = jnp.sqrt(jnp.sum(wide * wide, axis=1, keepdims=True) * longest[group])
            shift = jnp.ceil(bound * (1.0 / SHIFT_STEP)) * SHIFT_STEP
            extra = jnp.where(lane == 0, 1.0, jnp.where(lane == 1, -shift, 0.0))
            extra = extra.astype(jnp.bfloat16)
            state_extra[pl.ds(index * block, block), :] = extra
        else:
            extra = state_extra[pl.ds((part * blocks + index) * block, block), :]
        query = jnp.concatenate([query, extra], axis=1)
        for start in range(0, total_keys, chunk):
            made = scores_of(query, group, start, first_phase)
            weights[index % 2][:, pl.ds(start, chunk)] = jnp.exp2(made * EXP2_SCALE).astype(
                jnp.bfloat16
            )

    def finish(index, extremes):
        group = index // blocks_a_group
        summed = jnp.dot(
            weights[index % 2][:, :total_keys],
            values[group, :total_keys, :],
            preferred_element_type=jnp.float32,
        )
        rows = pl.ds(index * block, block)
        if first_phase:
            state_sum[rows, :] = summed
            return extremes
        old = pl.ds((part * blocks + index) * block, block)
        summed = summed + state_sum[old, :]
        total = summed[:, HD:]
        give(index, (summed[:, :HD] / total).astype(jnp.bfloat16))
        return jnp.minimum(extremes[0], total), jnp.maximum(extremes[1], total)

    begin(0)
    extremes = (jnp.ones((block, HD), jnp.float32),) * 2
    for index in range(blocks + 1):
        if index >= 1:
            extremes = finish(index - 1, extremes)
        if index < blocks:
            weigh(index)
            if (index + 1) % blocks_a_group == 0 and index + 1 < blocks:
                begin((index + 1) // blocks_a_group)
    if first_phase:
        return

    @pl.when((jnp.min(extremes[0]) < LOWEST_TOTAL) | (jnp.max(extremes[1]) > HIGHEST_TOTAL))
    def exact():
        for number, (halves, layout) in enumerate(key_sets):
            extras = [extra_columns(layout, half) for half in range(2)]
            for group in range(groups):
                fill(group, halves, extras)

            def one_block(index, carry):
                group = index // blocks_a_group
                extra = (lane == 0).astype(jnp.float32).astype(jnp.bfloat16)
                query = jnp.concatenate([query_rows(index), extra], axis=1)
                rows = pl.ds(pl.multiple_of(index * block, block), block)
                if number == 0:
                    top = jnp.full((block, HD), MASKED, jnp.float32)
                    summed = jnp.zeros((block, 2 * HD), jnp.float32)
                else:
                    top = slow_top[rows, :]
                    summed = slow_sum[rows, :]
                best = top
                for start in range(0, key_count(halves), chunk):
                    made = scores_of(query, group, start, number == 0)
                    for at in range(0, chunk, HD):
                        best = jnp.maximum(best, made[:, at : at + HD])
                best = jnp.broadcast_to(jnp.max(best, axis=1, keepdims=True), (block, HD))
                fade = jnp.exp2((top - best) * EXP2_SCALE)
                summed = summed * jnp.concatenate([fade, fade], axis=1)
                for start in range(0, key_count(halves), chunk):
                    made = scores_of(query, group, start, number == 0)
                    parts = [
                        jnp.exp2((made[:, at : at + HD] - best) * EXP2_SCALE)
                        for at in range(0, chunk, HD)
                    ]
                    summed = summed + jnp.dot(
                        jnp.concatenate(parts, axis=1).astype(jnp.bfloat16),
                        values[group, pl.ds(start, chunk), :],
                        preferred_element_type=jnp.float32,
                    )
                slow_top[rows, :] = best
                slow_sum[rows, :] = summed
                return carry

            lax.fori_loop(0, blocks, one_block, 0)
        for index in range(blocks):
            rows = pl.ds(index * block, block)
            give(index, (slow_sum[rows, :HD] / slow_sum[rows, HD:]).astype(jnp.bfloat16))


def attend(limits, owners, queries, part, parts, key_sets, spec, state):
    tokens, _, _, head_size = spec[:4]
    total_keys = 2 * max(sum(piece.shape[0] for piece in mine) for mine, _, _ in key_sets)
    columns = queries.shape[1] // parts
    groups = columns // (PER_GROUP * HD)
    block_heads = 4
    block = block_heads * tokens
    rows = PER_GROUP * groups * tokens
    pieces = [piece for mine, theirs, _ in key_sets for piece in mine + theirs]
    layouts = tuple(
        (tuple(layout), (len(mine), len(theirs))) for mine, theirs, layout in key_sets
    )
    operands = queries.size * 2 + sum(piece.size for piece in pieces) * 2 + rows * HD * 12
    scratch = groups * total_keys * HD * 8 + block * total_keys * 4 + rows * HD * 12
    whole = pl.BlockSpec(memory_space=pltpu.VMEM)
    scalars = pl.BlockSpec(memory_space=pltpu.SMEM)
    kept = tokens // head_size
    scratch_shapes = [
        pltpu.SMEM((owners.shape[1],), jnp.int32),
        pltpu.VMEM((groups, total_keys, 2 * HD), jnp.bfloat16),
        pltpu.VMEM((groups, total_keys, 2 * HD), jnp.bfloat16),
    ] + [pltpu.VMEM((block, total_keys), jnp.bfloat16)] * 2
    if state is None:
        state = ()
        out_shape = [
            jax.ShapeDtypeStruct((rows, 2 * HD), jnp.float32),
            jax.ShapeDtypeStruct((rows, HD), jnp.bfloat16),
        ]
    else:
        out_shape = [
            jax.ShapeDtypeStruct((kept, columns), jnp.bfloat16),
            jax.ShapeDtypeStruct((tokens - kept, columns), jnp.bfloat16),
        ]
        scratch_shapes += [
            pltpu.VMEM((rows, 2 * HD), jnp.float32),
            pltpu.VMEM((rows, HD), jnp.float32),
        ]
    return pl.pallas_call(
        functools.partial(attend_kernel, spec, layouts, part, block_heads, groups),
        out_shape=out_shape,
        in_specs=[scalars] * 2 + [whole] * (1 + len(pieces) + len(state)),
        out_specs=[whole] * 2,
        scratch_shapes=scratch_shapes,
        compiler_params=pltpu.CompilerParams(vmem_limit_bytes=operands + scratch + (6 << 20)),
        cost_estimate=pl.CostEstimate(
            flops=8 * tokens * columns * total_keys,
            bytes_accessed=4 * tokens * columns + 2 * total_keys * columns // PER_GROUP,
            transcendentals=0,
        ),
    )(limits, owners, queries, *pieces, *state)


def pick_kernel(group_size, cache_ref, other_ref, own_ref):
    request = lax.axis_index("seq") // group_size
    other_ref[...] = cache_ref[1 - request]
    own_ref[...] = cache_ref[request]


def pick(cache, group_size):
    whole = pl.BlockSpec(memory_space=pltpu.VMEM)
    return pl.pallas_call(
        functools.partial(pick_kernel, group_size),
        out_shape=[jax.ShapeDtypeStruct(cache.shape[1:], cache.dtype)] * 2,
        in_specs=[whole],
        out_specs=[whole] * 2,
        compiler_params=pltpu.CompilerParams(vmem_limit_bytes=8 << 20),
    )(cache)


def hold_kernel(from_ref, to_ref):
    to_ref[...] = from_ref[...]


def hold(value):
    whole = pl.BlockSpec(memory_space=pltpu.VMEM)
    return pl.pallas_call(
        hold_kernel,
        out_shape=jax.ShapeDtypeStruct(value.shape, value.dtype),
        in_specs=[whole],
        out_specs=whole,
        compiler_params=pltpu.CompilerParams(vmem_limit_bytes=8 << 20),
    )(value)


def join_kernel(spots, count, *refs):
    parts, (out_ref, done) = refs[len(refs) - 2 - count : -2], refs[-2:]
    side = out_ref.shape[1] // 2
    my_head = lax.axis_index("head")
    copies = []
    for at, (ref, (received, start)) in enumerate(zip(parts, spots)):
        owner = 1 - my_head if received else my_head
        first = pl.multiple_of(owner * side + start, HD)
        copies.append(
            pltpu.make_async_copy(ref, out_ref.at[:, pl.ds(first, ref.shape[1])], done.at[at])
        )
    for copy in copies:
        copy.start()
    for copy in copies:
        copy.wait()


def join(pieces, spots, columns, partial):
    earlier = [] if partial is None else [partial]
    return pl.pallas_call(
        functools.partial(join_kernel, spots, len(pieces)),
        out_shape=jax.ShapeDtypeStruct((pieces[0].shape[0], columns), pieces[0].dtype),
        in_specs=[pl.BlockSpec(memory_space=pl.ANY)] * len(earlier)
        + [pl.BlockSpec(memory_space=pltpu.VMEM)] * len(pieces),
        out_specs=pl.BlockSpec(memory_space=pl.ANY),
        scratch_shapes=[pltpu.SemaphoreType.DMA((len(pieces),))],
        input_output_aliases={0: 0} if earlier else {},
        compiler_params=pltpu.CompilerParams(vmem_limit_bytes=8 << 20),
    )(*earlier, *pieces)


def put_together(kept, received):
    columns = kept[0].shape[1]
    pieces = kept + received
    spots = [(at >= len(kept), at % len(kept) * columns) for at in range(len(pieces))]
    out = join(pieces[:-1], spots[:-1], columns * len(pieces), None)
    return join(pieces[-1:], spots[-1:], columns * len(pieces), out)


def body(span_query, span_kv, prefix_cache, prefix_len, block_owner):
    seq_size = lax.axis_size("seq")
    head_size = lax.axis_size("head")
    group_size = seq_size // REQS
    tokens = span_kv.shape[0]
    page = prefix_cache.shape[1]
    groups = span_kv.shape[1] // (2 * HD)
    parts = 2 if groups % 2 == 0 else 1
    bits = [1 << at for at in range(1, group_size.bit_length() - 1)]
    orders = (bits, bits[::-1])

    stages = len(bits)

    def send(rows, stage):
        return hop(rows, tuple(order[stage] for order in orders))

    def swap_cores(pieces):
        return hop(pieces[0] if len(pieces) == 1 else jnp.concatenate(pieces, axis=0), (1, 1))

    def whole_layout(layout):
        for stage in range(stages):
            layout = layout + shifted(layout, 1 << stage)
        return layout

    span_layout = whole_layout([(0, SPAN_ROWS, tokens)])
    page_layout = whole_layout([(0, OWN_PAGE, page), (0, CROSSED_PAGE, page)])
    near_count = (1 << (stages - 1)) + 1
    near_layout, far_layout = span_layout[:near_count], span_layout[near_count:] + page_layout

    other_page, own_page = pick(prefix_cache, group_size)
    crossed = hop(other_page, (group_size, group_size))

    span_early = send(span_kv, stages - 1)
    span_forward = send(span_kv, 0)
    for stage in range(1, stages - 1):
        seen = jnp.concatenate([span_kv, span_forward], axis=0)
        span_forward = jnp.concatenate([span_forward, send(seen, stage)], axis=0)
    span_late = send(span_forward, stages - 1)
    span_forward, span_own, crossed = together(span_forward, hold(span_kv), crossed)
    pages = [jnp.concatenate([own_page, crossed], axis=0)]
    pages.append(send(pages[0], 0))

    spec = (tokens, page, group_size, head_size, orders)
    common = (prefix_len, block_owner, span_query)
    near = [span_own, span_forward, span_early]
    near_set = (near, [swap_cores(near)], near_layout)
    state = attend(*common, 0, 1, [near_set], spec, None)

    pages[1], span_late, state = together(pages[1], span_late, state)
    for stage in range(1, stages - 1):
        pages.append(send(jnp.concatenate(pages, axis=0), stage))
    columns = span_kv.shape[1] // parts
    cuts = [slice(part * columns, (part + 1) * columns) for part in range(parts)]
    held = [jnp.concatenate([piece[:, cut] for piece in pages], axis=0) for cut in cuts]
    arrived = [send(rows, stages - 1) for rows in held]
    results = []
    for part in range(parts):
        mine = [span_late[:, cuts[part]], held[part], arrived[part]]
        far_set = (mine, [swap_cores(mine)], far_layout)
        results.append(attend(*common, part, parts, [near_set, far_set], spec, state))
    if head_size != 2:
        rows = jnp.concatenate([jnp.concatenate(pair, axis=0) for pair in results], axis=1)
        return lax.all_to_all(rows, "head", split_axis=0, concat_axis=1, tiled=True)
    kept = [pair[0] for pair in results]
    received = [lax.ppermute(pair[1], "head", [(0, 1), (1, 0)]) for pair in results]
    return put_together(kept, received)


def solution(mesh):
    placed = (P("seq", "head"), P("seq", "head"), P("seq", None, "head"), P(), P())
    return jax.shard_map(
        body, mesh=mesh, in_specs=placed, out_specs=P(("seq", "head"), None), check_vma=False
    )
```

```python
import functools
import math

import jax
import jax.numpy as jnp
from jax import lax
from jax.experimental import pallas as pl
from jax.experimental.pallas import tpu as pltpu
from jax.sharding import PartitionSpec as P

QH = 64
KVH = 8
HD = 128
REQS = 2
PER_GROUP = QH // KVH
EXP2_SCALE = HD ** (-0.5) * math.log2(math.e)
MASKED = -1e30
KEY_CHUNK = 256
SHIFT_STEP = 32.0
LOWEST_TOTAL = 1e-20
HIGHEST_TOTAL = 1e30
SPAN_ROWS, OWN_PAGE, CROSSED_PAGE = range(3)


def hop(value, bit_of_core):
    count = lax.axis_size("seq")
    return lax.ppermute(
        value, "seq", [(source, source ^ bit_of_core[source % 2]) for source in range(count)]
    )


def together(*values):
    return lax.optimization_barrier(values)


def shifted(layout, slots):
    return [(slot + slots, kind, rows) for slot, kind, rows in layout]


def hypercube_order(bits):
    order = [0]
    for bit in bits:
        order = order + [offset ^ bit for offset in order]
    return order


def attend_kernel(spec, layouts, part, block_heads, groups, limit_ref, owner_ref, q_ref, *refs):
    tokens, page, group_size, head_size, orders = spec
    first_phase = len(layouts) == 1
    key_sets = []
    for layout, counts in layouts:
        halves = []
        for count in counts:
            halves.append(refs[:count])
            refs = refs[count:]
        key_sets.append((halves, layout))
    (state_sum, state_extra), refs = refs[:2], refs[2:]
    if first_phase:
        page_seen, keys, values = refs[:3]
        weights = refs[3:5]
    else:
        outs = refs[:2]
        page_seen, keys, values = refs[2:5]
        weights, slow_sum, slow_top = refs[5:7], refs[7], refs[8]
    chunk = KEY_CHUNK
    me = lax.axis_index("seq")
    my_head = lax.axis_index("head")
    request = me // group_size
    offsets = [hypercube_order(order) for order in orders]

    def note_page(index, carry):
        page_seen[owner_ref[request, index]] = jnp.clip(limit_ref[request] - index * page, 0, page)
        return carry

    if not first_phase:
        lax.fori_loop(0, owner_ref.shape[1], note_page, 0)

    def extra_columns(layout, half):
        holder = me ^ half
        pieces = []
        for slot, kind, rows in layout:
            source = holder ^ jnp.where(holder % 2 == 0, offsets[0][slot], offsets[1][slot])
            if kind == SPAN_ROWS:
                count = jnp.where(source <= me, tokens, 0)
            elif kind == OWN_PAGE:
                count = page_seen[source]
            else:
                count = page_seen[source ^ group_size]
            row = lax.broadcasted_iota(jnp.int32, (rows, HD), 0)
            column = lax.broadcasted_iota(jnp.int32, (rows, HD), 1)
            mask = jnp.where(row < count, jnp.float32(0.0), jnp.float32(MASKED))
            one = jnp.where(column == 1, jnp.float32(1.0), jnp.float32(0.0))
            pieces.append(jnp.where(column == 0, mask, one).astype(jnp.bfloat16))
        return pieces

    def key_count(halves):
        return sum(ref.shape[0] for half in halves for ref in half)

    def fill(group, halves, extras):
        total_keys = key_count(halves)
        half_keys = total_keys // 2
        for half in range(2):
            start = half * half_keys
            for piece in extras[half]:
                keys[group, pl.ds(start, piece.shape[0]), HD:] = piece
                start += piece.shape[0]
            start = half * half_keys
            for ref in halves[half]:
                column = (part * groups + group) * 2 * HD % ref.shape[1]
                at = pl.ds(start, ref.shape[0])
                keys[group, at, :HD] = ref[:, pl.ds(column, HD)]
                values[group, at, :HD] = ref[:, pl.ds(column + HD, HD)]
                start += ref.shape[0]
        values[group, :total_keys, HD:] = jnp.ones((total_keys, HD), jnp.bfloat16)

    block = block_heads * tokens
    blocks_a_group = PER_GROUP // block_heads
    blocks = groups * blocks_a_group
    lane = lax.broadcasted_iota(jnp.int32, (block, HD), 1)
    causal = lax.broadcasted_iota(jnp.int32, (block, tokens), 1) <= (
        lax.broadcasted_iota(jnp.int32, (block, tokens), 0) % tokens
    )

    def query_rows(index):
        first = (part * blocks + index) * block_heads * HD
        columns = [
            pl.ds(pl.multiple_of(first + head * HD, HD), HD) for head in range(block_heads)
        ]
        return jnp.concatenate([q_ref[:, column] for column in columns], axis=0)

    def scores_of(query, group, start, is_span):
        made = lax.dot_general(
            query,
            keys[group, pl.ds(start, chunk), :],
            (((1,), (1,)), ((), ())),
            preferred_element_type=jnp.float32,
        )
        if start == 0 and is_span:
            own = jnp.where(causal, made[:, :tokens], MASKED)
            made = jnp.concatenate([own, made[:, tokens:]], axis=1)
        return made

    def give(index, result):
        kept = tokens // head_size
        for head in range(block_heads):
            column = pl.ds((index * block_heads + head) * HD, HD)
            one = result[head * tokens : (head + 1) * tokens]
            if head_size == 2:
                low, high = one[:kept], one[kept:]
                outs[0][:, column] = jnp.where(my_head == 0, low, high)
                outs[1][:, column] = jnp.where(my_head == 0, high, low)
            else:
                outs[0][:, column] = one[:kept]
                outs[1][:, column] = one[kept:]

    halves, layout = key_sets[-1]
    total_keys = key_count(halves)
    extras = [extra_columns(layout, half) for half in range(2)]
    longest = [None] * groups

    def begin(group):
        fill(group, halves, extras)
        if first_phase:
            key = keys[group, :total_keys, :HD].astype(jnp.float32)
            squares = jnp.sum(key * key, axis=1, keepdims=True)
            longest[group] = jnp.max(squares, axis=0, keepdims=True)

    def weigh(index):
        group = index // blocks_a_group
        query = query_rows(index)
        if first_phase:
            wide = query.astype(jnp.float32)
            bound = jnp.sqrt(jnp.sum(wide * wide, axis=1, keepdims=True) * longest[group])
            shift = jnp.ceil(bound * (1.0 / SHIFT_STEP)) * SHIFT_STEP
            extra = jnp.where(lane == 0, 1.0, jnp.where(lane == 1, -shift, 0.0))
            extra = extra.astype(jnp.bfloat16)
            state_extra[pl.ds(index * block, block), :] = extra
        else:
            extra = state_extra[pl.ds((part * blocks + index) * block, block), :]
        query = jnp.concatenate([query, extra], axis=1)
        for start in range(0, total_keys, chunk):
            made = scores_of(query, group, start, first_phase)
            weights[index % 2][:, pl.ds(start, chunk)] = jnp.exp2(made * EXP2_SCALE).astype(
                jnp.bfloat16
            )

    def finish(index, extremes):
        group = index // blocks_a_group
        summed = jnp.dot(
            weights[index % 2][:, :total_keys],
            values[group, :total_keys, :],
            preferred_element_type=jnp.float32,
        )
        rows = pl.ds(index * block, block)
        if first_phase:
            state_sum[rows, :] = summed
            return extremes
        old = pl.ds((part * blocks + index) * block, block)
        summed = summed + state_sum[old, :]
        total = summed[:, HD:]
        give(index, (summed[:, :HD] / total).astype(jnp.bfloat16))
        return jnp.minimum(extremes[0], total), jnp.maximum(extremes[1], total)

    begin(0)
    extremes = (jnp.ones((block, HD), jnp.float32),) * 2
    for index in range(blocks + 1):
        if index >= 1:
            extremes = finish(index - 1, extremes)
        if index < blocks:
            weigh(index)
            if (index + 1) % blocks_a_group == 0 and index + 1 < blocks:
                begin((index + 1) // blocks_a_group)
    if first_phase:
        return

    @pl.when((jnp.min(extremes[0]) < LOWEST_TOTAL) | (jnp.max(extremes[1]) > HIGHEST_TOTAL))
    def exact():
        for number, (halves, layout) in enumerate(key_sets):
            extras = [extra_columns(layout, half) for half in range(2)]
            for group in range(groups):
                fill(group, halves, extras)

            def one_block(index, carry):
                group = index // blocks_a_group
                extra = (lane == 0).astype(jnp.float32).astype(jnp.bfloat16)
                query = jnp.concatenate([query_rows(index), extra], axis=1)
                rows = pl.ds(pl.multiple_of(index * block, block), block)
                if number == 0:
                    top = jnp.full((block, HD), MASKED, jnp.float32)
                    summed = jnp.zeros((block, 2 * HD), jnp.float32)
                else:
                    top = slow_top[rows, :]
                    summed = slow_sum[rows, :]
                best = top
                for start in range(0, key_count(halves), chunk):
                    made = scores_of(query, group, start, number == 0)
                    for at in range(0, chunk, HD):
                        best = jnp.maximum(best, made[:, at : at + HD])
                best = jnp.broadcast_to(jnp.max(best, axis=1, keepdims=True), (block, HD))
                fade = jnp.exp2((top - best) * EXP2_SCALE)
                summed = summed * jnp.concatenate([fade, fade], axis=1)
                for start in range(0, key_count(halves), chunk):
                    made = scores_of(query, group, start, number == 0)
                    parts = [
                        jnp.exp2((made[:, at : at + HD] - best) * EXP2_SCALE)
                        for at in range(0, chunk, HD)
                    ]
                    summed = summed + jnp.dot(
                        jnp.concatenate(parts, axis=1).astype(jnp.bfloat16),
                        values[group, pl.ds(start, chunk), :],
                        preferred_element_type=jnp.float32,
                    )
                slow_top[rows, :] = best
                slow_sum[rows, :] = summed
                return carry

            lax.fori_loop(0, blocks, one_block, 0)
        for index in range(blocks):
            rows = pl.ds(index * block, block)
            give(index, (slow_sum[rows, :HD] / slow_sum[rows, HD:]).astype(jnp.bfloat16))


def attend(limits, owners, queries, part, parts, key_sets, spec, state):
    tokens, _, _, head_size = spec[:4]
    total_keys = 2 * max(sum(piece.shape[0] for piece in mine) for mine, _, _ in key_sets)
    columns = queries.shape[1] // parts
    groups = columns // (PER_GROUP * HD)
    block_heads = 4
    block = block_heads * tokens
    rows = PER_GROUP * groups * tokens
    pieces = [piece for mine, theirs, _ in key_sets for piece in mine + theirs]
    layouts = tuple(
        (tuple(layout), (len(mine), len(theirs))) for mine, theirs, layout in key_sets
    )
    operands = queries.size * 2 + sum(piece.size for piece in pieces) * 2 + rows * HD * 12
    scratch = groups * total_keys * HD * 8 + block * total_keys * 4 + rows * HD * 12
    whole = pl.BlockSpec(memory_space=pltpu.VMEM)
    scalars = pl.BlockSpec(memory_space=pltpu.SMEM)
    kept = tokens // head_size
    scratch_shapes = [
        pltpu.SMEM((owners.shape[1],), jnp.int32),
        pltpu.VMEM((groups, total_keys, 2 * HD), jnp.bfloat16),
        pltpu.VMEM((groups, total_keys, 2 * HD), jnp.bfloat16),
    ] + [pltpu.VMEM((block, total_keys), jnp.bfloat16)] * 2
    if state is None:
        state = ()
        out_shape = [
            jax.ShapeDtypeStruct((rows, 2 * HD), jnp.float32),
            jax.ShapeDtypeStruct((rows, HD), jnp.bfloat16),
        ]
    else:
        out_shape = [
            jax.ShapeDtypeStruct((kept, columns), jnp.bfloat16),
            jax.ShapeDtypeStruct((tokens - kept, columns), jnp.bfloat16),
        ]
        scratch_shapes += [
            pltpu.VMEM((rows, 2 * HD), jnp.float32),
            pltpu.VMEM((rows, HD), jnp.float32),
        ]
    return pl.pallas_call(
        functools.partial(attend_kernel, spec, layouts, part, block_heads, groups),
        out_shape=out_shape,
        in_specs=[scalars] * 2 + [whole] * (1 + len(pieces) + len(state)),
        out_specs=[whole] * 2,
        scratch_shapes=scratch_shapes,
        compiler_params=pltpu.CompilerParams(vmem_limit_bytes=operands + scratch + (6 << 20)),
        cost_estimate=pl.CostEstimate(
            flops=8 * tokens * columns * total_keys,
            bytes_accessed=4 * tokens * columns + 2 * total_keys * columns // PER_GROUP,
            transcendentals=0,
        ),
    )(limits, owners, queries, *pieces, *state)


def pick_kernel(group_size, cache_ref, other_ref, own_ref):
    request = lax.axis_index("seq") // group_size
    other_ref[...] = cache_ref[1 - request]
    own_ref[...] = cache_ref[request]


def pick(cache, group_size):
    whole = pl.BlockSpec(memory_space=pltpu.VMEM)
    return pl.pallas_call(
        functools.partial(pick_kernel, group_size),
        out_shape=[jax.ShapeDtypeStruct(cache.shape[1:], cache.dtype)] * 2,
        in_specs=[whole],
        out_specs=[whole] * 2,
        compiler_params=pltpu.CompilerParams(vmem_limit_bytes=8 << 20),
    )(cache)


def hold_kernel(from_ref, to_ref):
    to_ref[...] = from_ref[...]


def hold(value):
    whole = pl.BlockSpec(memory_space=pltpu.VMEM)
    return pl.pallas_call(
        hold_kernel,
        out_shape=jax.ShapeDtypeStruct(value.shape, value.dtype),
        in_specs=[whole],
        out_specs=whole,
        compiler_params=pltpu.CompilerParams(vmem_limit_bytes=8 << 20),
    )(value)


def join_kernel(spots, count, *refs):
    parts, (out_ref, done) = refs[len(refs) - 2 - count : -2], refs[-2:]
    side = out_ref.shape[1] // 2
    my_head = lax.axis_index("head")
    copies = []
    for at, (ref, (received, start)) in enumerate(zip(parts, spots)):
        owner = 1 - my_head if received else my_head
        first = pl.multiple_of(owner * side + start, HD)
        copies.append(
            pltpu.make_async_copy(ref, out_ref.at[:, pl.ds(first, ref.shape[1])], done.at[at])
        )
    for copy in copies:
        copy.start()
    for copy in copies:
        copy.wait()


def join(pieces, spots, columns, partial):
    earlier = [] if partial is None else [partial]
    return pl.pallas_call(
        functools.partial(join_kernel, spots, len(pieces)),
        out_shape=jax.ShapeDtypeStruct((pieces[0].shape[0], columns), pieces[0].dtype),
        in_specs=[pl.BlockSpec(memory_space=pl.ANY)] * len(earlier)
        + [pl.BlockSpec(memory_space=pltpu.VMEM)] * len(pieces),
        out_specs=pl.BlockSpec(memory_space=pl.ANY),
        scratch_shapes=[pltpu.SemaphoreType.DMA((len(pieces),))],
        input_output_aliases={0: 0} if earlier else {},
        compiler_params=pltpu.CompilerParams(vmem_limit_bytes=8 << 20),
    )(*earlier, *pieces)


def put_together(kept, received):
    columns = kept[0].shape[1]
    pieces = kept + received
    spots = [(at >= len(kept), at % len(kept) * columns) for at in range(len(pieces))]
    out = join(pieces[:-1], spots[:-1], columns * len(pieces), None)
    return join(pieces[-1:], spots[-1:], columns * len(pieces), out)


def body(span_query, span_kv, prefix_cache, prefix_len, block_owner):
    seq_size = lax.axis_size("seq")
    head_size = lax.axis_size("head")
    group_size = seq_size // REQS
    tokens = span_kv.shape[0]
    page = prefix_cache.shape[1]
    groups = span_kv.shape[1] // (2 * HD)
    parts = 2 if groups % 2 == 0 else 1
    bits = [1 << at for at in range(1, group_size.bit_length() - 1)]
    orders = (bits, bits[::-1])

    stages = len(bits)

    def send(rows, stage):
        return hop(rows, tuple(order[stage] for order in orders))

    def swap_cores(pieces):
        return hop(pieces[0] if len(pieces) == 1 else jnp.concatenate(pieces, axis=0), (1, 1))

    def whole_layout(layout):
        for stage in range(stages):
            layout = layout + shifted(layout, 1 << stage)
        return layout

    span_layout = whole_layout([(0, SPAN_ROWS, tokens)])
    page_layout = whole_layout([(0, OWN_PAGE, page), (0, CROSSED_PAGE, page)])
    near_count = (1 << (stages - 1)) + 1
    near_layout, far_layout = span_layout[:near_count], span_layout[near_count:] + page_layout

    columns = span_kv.shape[1] // parts
    cuts = [slice(part * columns, (part + 1) * columns) for part in range(parts)]

    other_page, own_page = pick(prefix_cache, group_size)
    crossed = [hop(other_page[:, cut], (group_size, group_size)) for cut in cuts]

    span_early = send(span_kv, stages - 1)
    span_forward = send(span_kv, 0)
    for stage in range(1, stages - 1):
        seen = jnp.concatenate([span_kv, span_forward], axis=0)
        span_forward = jnp.concatenate([span_forward, send(seen, stage)], axis=0)
    span_late = send(span_forward, stages - 1)
    span_own, crossed[0] = together(hold(span_kv), crossed[0])

    span_forward, span_early, *rest = together(span_forward, span_early, *crossed[1:])
    crossed = crossed[:1] + rest
    pages = [
        [jnp.concatenate([own_page[:, cut], one], axis=0)] for cut, one in zip(cuts, crossed)
    ]
    for mine in pages:
        mine.append(send(mine[0], 0))

    def held(part):
        for stage in range(1, stages - 1):
            pages[part].append(send(jnp.concatenate(pages[part], axis=0), stage))
        return jnp.concatenate(pages[part], axis=0)

    spec = (tokens, page, group_size, head_size, orders)
    common = (prefix_len, block_owner, span_query)
    full = [held(part) for part in range(parts)]
    near = [span_own, span_forward, span_early]
    near_swapped, *full = together(swap_cores(near), *full)
    near_set = (near, [near_swapped], near_layout)
    state = attend(*common, 0, 1, [near_set], spec, None)

    arrived = [send(rows, stages - 1) for rows in full]
    span_late, arrived[0], state = together(span_late, arrived[0], state)
    results = []
    for part in range(parts):
        if part:
            arrived[part], state = together(arrived[part], state)
        mine = [span_late[:, cuts[part]], full[part], arrived[part]]
        far_set = (mine, [swap_cores(mine)], far_layout)
        results.append(attend(*common, part, parts, [near_set, far_set], spec, state))
    if head_size != 2:
        rows = jnp.concatenate([jnp.concatenate(pair, axis=0) for pair in results], axis=1)
        return lax.all_to_all(rows, "head", split_axis=0, concat_axis=1, tiled=True)
    kept = [pair[0] for pair in results]
    received = [lax.ppermute(pair[1], "head", [(0, 1), (1, 0)]) for pair in results]
    return put_together(kept, received)


def solution(mesh):
    placed = (P("seq", "head"), P("seq", "head"), P("seq", None, "head"), P(), P())
    return jax.shard_map(
        body, mesh=mesh, in_specs=placed, out_specs=P(("seq", "head"), None), check_vma=False
    )
```

```python
import functools
import math

import jax
import jax.numpy as jnp
from jax import lax
from jax.experimental import pallas as pl
from jax.experimental.pallas import tpu as pltpu
from jax.sharding import PartitionSpec as P

QH = 64
KVH = 8
HD = 128
REQS = 2
PER_GROUP = QH // KVH
EXP2_SCALE = HD ** (-0.5) * math.log2(math.e)
MASKED = -1e30
KEY_CHUNK = 256
SHIFT_STEP = 32.0
LOWEST_TOTAL = 1e-20
HIGHEST_TOTAL = 1e30
SPAN_ROWS, OWN_PAGE, CROSSED_PAGE = range(3)


def hop(value, bit_of_core):
    count = lax.axis_size("seq")
    return lax.ppermute(
        value, "seq", [(source, source ^ bit_of_core[source % 2]) for source in range(count)]
    )


def together(*values):
    return lax.optimization_barrier(values)


def shifted(layout, slots):
    return [(slot + slots, kind, rows) for slot, kind, rows in layout]


def hypercube_order(bits):
    order = [0]
    for bit in bits:
        order = order + [offset ^ bit for offset in order]
    return order


def attend_kernel(spec, layouts, part, block_heads, groups, limit_ref, owner_ref, q_ref, *refs):
    tokens, page, group_size, head_size, orders = spec
    first_phase = len(layouts) == 1
    key_sets = []
    for layout, counts in layouts:
        halves = []
        for count in counts:
            halves.append(refs[:count])
            refs = refs[count:]
        key_sets.append((halves, layout))
    (state_sum, state_extra), refs = refs[:2], refs[2:]
    if first_phase:
        page_seen, keys, values = refs[:3]
        weights = refs[3:5]
    else:
        outs = refs[:2]
        page_seen, keys, values = refs[2:5]
        weights, slow_sum, slow_top = refs[5:7], refs[7], refs[8]
    chunk = KEY_CHUNK
    me = lax.axis_index("seq")
    my_head = lax.axis_index("head")
    request = me // group_size
    offsets = [hypercube_order(order) for order in orders]

    def note_page(index, carry):
        page_seen[owner_ref[request, index]] = jnp.clip(limit_ref[request] - index * page, 0, page)
        return carry

    if not first_phase:
        lax.fori_loop(0, owner_ref.shape[1], note_page, 0)

    def extra_columns(layout, half):
        holder = me ^ half
        pieces = []
        for slot, kind, rows in layout:
            source = holder ^ jnp.where(holder % 2 == 0, offsets[0][slot], offsets[1][slot])
            if kind == SPAN_ROWS:
                count = jnp.where(source <= me, tokens, 0)
            elif kind == OWN_PAGE:
                count = page_seen[source]
            else:
                count = page_seen[source ^ group_size]
            row = lax.broadcasted_iota(jnp.int32, (rows, HD), 0)
            column = lax.broadcasted_iota(jnp.int32, (rows, HD), 1)
            mask = jnp.where(row < count, jnp.float32(0.0), jnp.float32(MASKED))
            one = jnp.where(column == 1, jnp.float32(1.0), jnp.float32(0.0))
            pieces.append(jnp.where(column == 0, mask, one).astype(jnp.bfloat16))
        return pieces

    def key_count(halves):
        return sum(ref.shape[0] for half in halves for ref in half)

    def fill(group, halves, extras):
        total_keys = key_count(halves)
        half_keys = total_keys // 2
        for half in range(2):
            start = half * half_keys
            for piece in extras[half]:
                keys[group, pl.ds(start, piece.shape[0]), HD:] = piece
                start += piece.shape[0]
            start = half * half_keys
            for ref in halves[half]:
                column = (part * groups + group) * 2 * HD % ref.shape[1]
                at = pl.ds(start, ref.shape[0])
                keys[group, at, :HD] = ref[:, pl.ds(column, HD)]
                values[group, at, :HD] = ref[:, pl.ds(column + HD, HD)]
                start += ref.shape[0]
        values[group, :total_keys, HD:] = jnp.ones((total_keys, HD), jnp.bfloat16)

    block = block_heads * tokens
    blocks_a_group = PER_GROUP // block_heads
    blocks = groups * blocks_a_group
    lane = lax.broadcasted_iota(jnp.int32, (block, HD), 1)
    causal = lax.broadcasted_iota(jnp.int32, (block, tokens), 1) <= (
        lax.broadcasted_iota(jnp.int32, (block, tokens), 0) % tokens
    )

    def query_rows(index):
        first = (part * blocks + index) * block_heads * HD
        columns = [
            pl.ds(pl.multiple_of(first + head * HD, HD), HD) for head in range(block_heads)
        ]
        return jnp.concatenate([q_ref[:, column] for column in columns], axis=0)

    def scores_of(query, group, start, is_span):
        made = lax.dot_general(
            query,
            keys[group, pl.ds(start, chunk), :],
            (((1,), (1,)), ((), ())),
            preferred_element_type=jnp.float32,
        )
        if start == 0 and is_span:
            own = jnp.where(causal, made[:, :tokens], MASKED)
            made = jnp.concatenate([own, made[:, tokens:]], axis=1)
        return made

    def give(index, result):
        kept = tokens // head_size
        for head in range(block_heads):
            column = pl.ds((index * block_heads + head) * HD, HD)
            one = result[head * tokens : (head + 1) * tokens]
            if head_size == 2:
                low, high = one[:kept], one[kept:]
                outs[0][:, column] = jnp.where(my_head == 0, low, high)
                outs[1][:, column] = jnp.where(my_head == 0, high, low)
            else:
                outs[0][:, column] = one[:kept]
                outs[1][:, column] = one[kept:]

    halves, layout = key_sets[-1]
    total_keys = key_count(halves)
    extras = [extra_columns(layout, half) for half in range(2)]
    longest = [None] * groups

    def begin(group):
        fill(group, halves, extras)
        if first_phase:
            key = keys[group, :total_keys, :HD].astype(jnp.float32)
            squares = jnp.sum(key * key, axis=1, keepdims=True)
            longest[group] = jnp.max(squares, axis=0, keepdims=True)

    def weigh(index):
        group = index // blocks_a_group
        query = query_rows(index)
        if first_phase:
            wide = query.astype(jnp.float32)
            bound = jnp.sqrt(jnp.sum(wide * wide, axis=1, keepdims=True) * longest[group])
            shift = jnp.ceil(bound * (1.0 / SHIFT_STEP)) * SHIFT_STEP
            extra = jnp.where(lane == 0, 1.0, jnp.where(lane == 1, -shift, 0.0))
            extra = extra.astype(jnp.bfloat16)
            state_extra[pl.ds(index * block, block), :] = extra
        else:
            extra = state_extra[pl.ds((part * blocks + index) * block, block), :]
        query = jnp.concatenate([query, extra], axis=1)
        for start in range(0, total_keys, chunk):
            made = scores_of(query, group, start, first_phase)
            weights[index % 2][:, pl.ds(start, chunk)] = jnp.exp2(made * EXP2_SCALE).astype(
                jnp.bfloat16
            )
            yield

    def gather_values(index):
        group = index // blocks_a_group
        if first_phase:
            summed = None
        else:
            summed = state_sum[pl.ds((part * blocks + index) * block, block), :]
        for start in range(0, total_keys, chunk):
            at = pl.ds(start, chunk)
            more = jnp.dot(
                weights[index % 2][:, at], values[group, at, :], preferred_element_type=jnp.float32
            )
            summed = more if summed is None else summed + more
            yield
        if first_phase:
            state_sum[pl.ds(index * block, block), :] = summed
            return
        total = summed[:, HD:]
        give(index, (summed[:, :HD] / total).astype(jnp.bfloat16))
        extremes[0] = jnp.minimum(extremes[0], total)
        extremes[1] = jnp.maximum(extremes[1], total)

    begin(0)
    extremes = [jnp.ones((block, HD), jnp.float32)] * 2
    for index in range(blocks + 1):
        steps = []
        if index < blocks:
            steps.append(weigh(index))
        if index >= 1:
            steps.append(gather_values(index - 1))
        while steps:
            steps = [step for step in steps if next(step, steps) is not steps]
        if (index + 1) % blocks_a_group == 0 and index + 1 < blocks:
            begin((index + 1) // blocks_a_group)
    if first_phase:
        return

    @pl.when((jnp.min(extremes[0]) < LOWEST_TOTAL) | (jnp.max(extremes[1]) > HIGHEST_TOTAL))
    def exact():
        for number, (halves, layout) in enumerate(key_sets):
            extras = [extra_columns(layout, half) for half in range(2)]
            for group in range(groups):
                fill(group, halves, extras)

            def one_block(index, carry):
                group = index // blocks_a_group
                extra = (lane == 0).astype(jnp.float32).astype(jnp.bfloat16)
                query = jnp.concatenate([query_rows(index), extra], axis=1)
                rows = pl.ds(pl.multiple_of(index * block, block), block)
                if number == 0:
                    top = jnp.full((block, HD), MASKED, jnp.float32)
                    summed = jnp.zeros((block, 2 * HD), jnp.float32)
                else:
                    top = slow_top[rows, :]
                    summed = slow_sum[rows, :]
                best = top
                for start in range(0, key_count(halves), chunk):
                    made = scores_of(query, group, start, number == 0)
                    for at in range(0, chunk, HD):
                        best = jnp.maximum(best, made[:, at : at + HD])
                best = jnp.broadcast_to(jnp.max(best, axis=1, keepdims=True), (block, HD))
                fade = jnp.exp2((top - best) * EXP2_SCALE)
                summed = summed * jnp.concatenate([fade, fade], axis=1)
                for start in range(0, key_count(halves), chunk):
                    made = scores_of(query, group, start, number == 0)
                    parts = [
                        jnp.exp2((made[:, at : at + HD] - best) * EXP2_SCALE)
                        for at in range(0, chunk, HD)
                    ]
                    summed = summed + jnp.dot(
                        jnp.concatenate(parts, axis=1).astype(jnp.bfloat16),
                        values[group, pl.ds(start, chunk), :],
                        preferred_element_type=jnp.float32,
                    )
                slow_top[rows, :] = best
                slow_sum[rows, :] = summed
                return carry

            lax.fori_loop(0, blocks, one_block, 0)
        for index in range(blocks):
            rows = pl.ds(index * block, block)
            give(index, (slow_sum[rows, :HD] / slow_sum[rows, HD:]).astype(jnp.bfloat16))


def attend(limits, owners, queries, part, parts, key_sets, spec, state):
    tokens, _, _, head_size = spec[:4]
    total_keys = 2 * max(sum(piece.shape[0] for piece in mine) for mine, _, _ in key_sets)
    columns = queries.shape[1] // parts
    groups = columns // (PER_GROUP * HD)
    block_heads = 4
    block = block_heads * tokens
    rows = PER_GROUP * groups * tokens
    pieces = [piece for mine, theirs, _ in key_sets for piece in mine + theirs]
    layouts = tuple(
        (tuple(layout), (len(mine), len(theirs))) for mine, theirs, layout in key_sets
    )
    operands = queries.size * 2 + sum(piece.size for piece in pieces) * 2 + rows * HD * 12
    scratch = groups * total_keys * HD * 8 + block * total_keys * 4 + rows * HD * 12
    whole = pl.BlockSpec(memory_space=pltpu.VMEM)
    scalars = pl.BlockSpec(memory_space=pltpu.SMEM)
    kept = tokens // head_size
    scratch_shapes = [
        pltpu.SMEM((owners.shape[1],), jnp.int32),
        pltpu.VMEM((groups, total_keys, 2 * HD), jnp.bfloat16),
        pltpu.VMEM((groups, total_keys, 2 * HD), jnp.bfloat16),
    ] + [pltpu.VMEM((block, total_keys), jnp.bfloat16)] * 2
    if state is None:
        state = ()
        out_shape = [
            jax.ShapeDtypeStruct((rows, 2 * HD), jnp.float32),
            jax.ShapeDtypeStruct((rows, HD), jnp.bfloat16),
        ]
    else:
        out_shape = [
            jax.ShapeDtypeStruct((kept, columns), jnp.bfloat16),
            jax.ShapeDtypeStruct((tokens - kept, columns), jnp.bfloat16),
        ]
        scratch_shapes += [
            pltpu.VMEM((rows, 2 * HD), jnp.float32),
            pltpu.VMEM((rows, HD), jnp.float32),
        ]
    return pl.pallas_call(
        functools.partial(attend_kernel, spec, layouts, part, block_heads, groups),
        out_shape=out_shape,
        in_specs=[scalars] * 2 + [whole] * (1 + len(pieces) + len(state)),
        out_specs=[whole] * 2,
        scratch_shapes=scratch_shapes,
        compiler_params=pltpu.CompilerParams(vmem_limit_bytes=operands + scratch + block * total_keys * 4 + (6 << 20)),
        cost_estimate=pl.CostEstimate(
            flops=8 * tokens * columns * total_keys,
            bytes_accessed=4 * tokens * columns + 2 * total_keys * columns // PER_GROUP,
            transcendentals=0,
        ),
    )(limits, owners, queries, *pieces, *state)


def pick_kernel(group_size, cache_ref, other_ref, own_ref):
    request = lax.axis_index("seq") // group_size
    other_ref[...] = cache_ref[1 - request]
    own_ref[...] = cache_ref[request]


def pick(cache, group_size):
    whole = pl.BlockSpec(memory_space=pltpu.VMEM)
    return pl.pallas_call(
        functools.partial(pick_kernel, group_size),
        out_shape=[jax.ShapeDtypeStruct(cache.shape[1:], cache.dtype)] * 2,
        in_specs=[whole],
        out_specs=[whole] * 2,
        compiler_params=pltpu.CompilerParams(vmem_limit_bytes=8 << 20),
    )(cache)


def hold_kernel(from_ref, to_ref):
    to_ref[...] = from_ref[...]


def hold(value):
    whole = pl.BlockSpec(memory_space=pltpu.VMEM)
    return pl.pallas_call(
        hold_kernel,
        out_shape=jax.ShapeDtypeStruct(value.shape, value.dtype),
        in_specs=[whole],
        out_specs=whole,
        compiler_params=pltpu.CompilerParams(vmem_limit_bytes=8 << 20),
    )(value)


def join_kernel(spots, count, *refs):
    parts, (out_ref, done) = refs[len(refs) - 2 - count : -2], refs[-2:]
    side = out_ref.shape[1] // 2
    my_head = lax.axis_index("head")
    copies = []
    for at, (ref, (received, start)) in enumerate(zip(parts, spots)):
        owner = 1 - my_head if received else my_head
        first = pl.multiple_of(owner * side + start, HD)
        copies.append(
            pltpu.make_async_copy(ref, out_ref.at[:, pl.ds(first, ref.shape[1])], done.at[at])
        )
    for copy in copies:
        copy.start()
    for copy in copies:
        copy.wait()


def join(pieces, spots, columns, partial):
    earlier = [] if partial is None else [partial]
    return pl.pallas_call(
        functools.partial(join_kernel, spots, len(pieces)),
        out_shape=jax.ShapeDtypeStruct((pieces[0].shape[0], columns), pieces[0].dtype),
        in_specs=[pl.BlockSpec(memory_space=pl.ANY)] * len(earlier)
        + [pl.BlockSpec(memory_space=pltpu.VMEM)] * len(pieces),
        out_specs=pl.BlockSpec(memory_space=pl.ANY),
        scratch_shapes=[pltpu.SemaphoreType.DMA((len(pieces),))],
        input_output_aliases={0: 0} if earlier else {},
        compiler_params=pltpu.CompilerParams(vmem_limit_bytes=8 << 20),
    )(*earlier, *pieces)


def put_together(kept, received):
    columns = kept[0].shape[1]
    pieces = kept + received
    spots = [(at >= len(kept), at % len(kept) * columns) for at in range(len(pieces))]
    out = join(pieces[:-1], spots[:-1], columns * len(pieces), None)
    return join(pieces[-1:], spots[-1:], columns * len(pieces), out)


def body(span_query, span_kv, prefix_cache, prefix_len, block_owner):
    seq_size = lax.axis_size("seq")
    head_size = lax.axis_size("head")
    group_size = seq_size // REQS
    tokens = span_kv.shape[0]
    page = prefix_cache.shape[1]
    groups = span_kv.shape[1] // (2 * HD)
    parts = 2 if groups % 2 == 0 else 1
    bits = [1 << at for at in range(1, group_size.bit_length() - 1)]
    orders = (bits, bits[::-1])

    stages = len(bits)

    def send(rows, stage):
        return hop(rows, tuple(order[stage] for order in orders))

    def swap_cores(pieces):
        return hop(pieces[0] if len(pieces) == 1 else jnp.concatenate(pieces, axis=0), (1, 1))

    def whole_layout(layout):
        for stage in range(stages):
            layout = layout + shifted(layout, 1 << stage)
        return layout

    span_layout = whole_layout([(0, SPAN_ROWS, tokens)])
    page_layout = whole_layout([(0, OWN_PAGE, page), (0, CROSSED_PAGE, page)])
    near_count = (1 << (stages - 1)) + 1
    near_layout, far_layout = span_layout[:near_count], span_layout[near_count:] + page_layout

    columns = span_kv.shape[1] // parts
    cuts = [slice(part * columns, (part + 1) * columns) for part in range(parts)]

    other_page, own_page = pick(prefix_cache, group_size)
    crossed = [hop(other_page[:, cut], (group_size, group_size)) for cut in cuts]

    span_early = send(span_kv, stages - 1)
    span_forward = send(span_kv, 0)
    for stage in range(1, stages - 1):
        seen = jnp.concatenate([span_kv, span_forward], axis=0)
        span_forward = jnp.concatenate([span_forward, send(seen, stage)], axis=0)
    span_late = send(span_forward, stages - 1)
    span_own, crossed[0] = together(hold(span_kv), crossed[0])

    span_forward, span_early, *rest = together(span_forward, span_early, *crossed[1:])
    crossed = crossed[:1] + rest
    pages = [
        [jnp.concatenate([own_page[:, cut], one], axis=0)] for cut, one in zip(cuts, crossed)
    ]
    for mine in pages:
        mine.append(send(mine[0], 0))

    def held(part):
        for stage in range(1, stages - 1):
            pages[part].append(send(jnp.concatenate(pages[part], axis=0), stage))
        return jnp.concatenate(pages[part], axis=0)

    spec = (tokens, page, group_size, head_size, orders)
    common = (prefix_len, block_owner, span_query)
    full = [held(part) for part in range(parts)]
    near = [span_own, span_forward, span_early]
    near_swapped, span_late, *full = together(swap_cores(near), span_late, *full)
    near_set = (near, [near_swapped], near_layout)
    state = attend(*common, 0, 1, [near_set], spec, None)

    arrived = [send(rows, stages - 1) for rows in full]
    results = []
    for part in range(parts):
        arrived[part], state = together(arrived[part], state)
        mine = [span_late[:, cuts[part]], full[part], arrived[part]]
        far_set = (mine, [swap_cores(mine)], far_layout)
        results.append(attend(*common, part, parts, [near_set, far_set], spec, state))
    if head_size != 2:
        rows = jnp.concatenate([jnp.concatenate(pair, axis=0) for pair in results], axis=1)
        return lax.all_to_all(rows, "head", split_axis=0, concat_axis=1, tiled=True)
    kept = [pair[0] for pair in results]
    received = [lax.ppermute(pair[1], "head", [(0, 1), (1, 0)]) for pair in results]
    return put_together(kept, received)


def solution(mesh):
    placed = (P("seq", "head"), P("seq", "head"), P("seq", None, "head"), P(), P())
    return jax.shard_map(
        body, mesh=mesh, in_specs=placed, out_specs=P(("seq", "head"), None), check_vma=False
    )
```

```python
import functools
import math

import jax
import jax.numpy as jnp
from jax import lax
from jax.experimental import pallas as pl
from jax.experimental.pallas import tpu as pltpu
from jax.sharding import PartitionSpec as P

QH = 64
KVH = 8
HD = 128
REQS = 2
PER_GROUP = QH // KVH
EXP2_SCALE = HD ** (-0.5) * math.log2(math.e)
MASKED = -1e30
KEY_CHUNK = 256
SHIFT_STEP = 32.0
LOWEST_TOTAL = 1e-20
HIGHEST_TOTAL = 1e30
SPAN_ROWS, OWN_PAGE, CROSSED_PAGE = range(3)


def hop(value, bit_of_core):
    count = lax.axis_size("seq")
    return lax.ppermute(
        value, "seq", [(source, source ^ bit_of_core[source % 2]) for source in range(count)]
    )


def together(*values):
    return lax.optimization_barrier(values)


def shifted(layout, slots):
    return [(slot + slots, kind, rows) for slot, kind, rows in layout]


def hypercube_order(bits):
    order = [0]
    for bit in bits:
        order = order + [offset ^ bit for offset in order]
    return order


def attend_kernel(spec, layouts, part, block_heads, groups, limit_ref, owner_ref, q_ref, *refs):
    tokens, page, group_size, head_size, orders = spec
    first_phase = len(layouts) == 1
    key_sets = []
    for layout, counts in layouts:
        halves = []
        for count in counts:
            halves.append(refs[:count])
            refs = refs[count:]
        key_sets.append((halves, layout))
    (state_sum, state_extra), refs = refs[:2], refs[2:]
    if first_phase:
        page_seen, keys, values = refs[:3]
        weights = refs[3:5]
    else:
        outs = refs[:2]
        page_seen, keys, values = refs[2:5]
        weights, slow_sum, slow_top = refs[5:7], refs[7], refs[8]
    chunk = KEY_CHUNK
    me = lax.axis_index("seq")
    my_head = lax.axis_index("head")
    request = me // group_size
    offsets = [hypercube_order(order) for order in orders]

    def note_page(index, carry):
        page_seen[owner_ref[request, index]] = jnp.clip(limit_ref[request] - index * page, 0, page)
        return carry

    if not first_phase:
        lax.fori_loop(0, owner_ref.shape[1], note_page, 0)

    def extra_columns(layout, half):
        holder = me ^ half
        pieces = []
        for slot, kind, rows in layout:
            source = holder ^ jnp.where(holder % 2 == 0, offsets[0][slot], offsets[1][slot])
            if kind == SPAN_ROWS:
                count = jnp.where(source <= me, tokens, 0)
            elif kind == OWN_PAGE:
                count = page_seen[source]
            else:
                count = page_seen[source ^ group_size]
            row = lax.broadcasted_iota(jnp.int32, (rows, HD), 0)
            column = lax.broadcasted_iota(jnp.int32, (rows, HD), 1)
            mask = jnp.where(row < count, jnp.float32(0.0), jnp.float32(MASKED))
            one = jnp.where(column == 1, jnp.float32(1.0), jnp.float32(0.0))
            pieces.append(jnp.where(column == 0, mask, one).astype(jnp.bfloat16))
        return pieces

    def key_count(halves):
        return sum(ref.shape[0] for half in halves for ref in half)

    def fill(group, halves, extras):
        total_keys = key_count(halves)
        half_keys = total_keys // 2
        for half in range(2):
            start = half * half_keys
            for piece in extras[half]:
                keys[group, pl.ds(start, piece.shape[0]), HD:] = piece
                start += piece.shape[0]
            start = half * half_keys
            for ref in halves[half]:
                column = (part * groups + group) * 2 * HD % ref.shape[1]
                at = pl.ds(start, ref.shape[0])
                keys[group, at, :HD] = ref[:, pl.ds(column, HD)]
                values[group, at, :HD] = ref[:, pl.ds(column + HD, HD)]
                start += ref.shape[0]
        values[group, :total_keys, HD:] = jnp.ones((total_keys, HD), jnp.bfloat16)

    block = block_heads * tokens
    blocks_a_group = PER_GROUP // block_heads
    blocks = groups * blocks_a_group
    lane = lax.broadcasted_iota(jnp.int32, (block, HD), 1)
    causal = lax.broadcasted_iota(jnp.int32, (block, tokens), 1) <= (
        lax.broadcasted_iota(jnp.int32, (block, tokens), 0) % tokens
    )

    def query_rows(index):
        first = (part * blocks + index) * block_heads * HD
        columns = [
            pl.ds(pl.multiple_of(first + head * HD, HD), HD) for head in range(block_heads)
        ]
        return jnp.concatenate([q_ref[:, column] for column in columns], axis=0)

    def scores_of(query, group, start, is_span):
        made = lax.dot_general(
            query,
            keys[group, pl.ds(start, chunk), :],
            (((1,), (1,)), ((), ())),
            preferred_element_type=jnp.float32,
        )
        if start == 0 and is_span:
            own = jnp.where(causal, made[:, :tokens], MASKED)
            made = jnp.concatenate([own, made[:, tokens:]], axis=1)
        return made

    def give(index, result):
        kept = tokens // head_size
        for head in range(block_heads):
            column = pl.ds((index * block_heads + head) * HD, HD)
            one = result[head * tokens : (head + 1) * tokens]
            if head_size == 2:
                low, high = one[:kept], one[kept:]
                outs[0][:, column] = jnp.where(my_head == 0, low, high)
                outs[1][:, column] = jnp.where(my_head == 0, high, low)
            else:
                outs[0][:, column] = one[:kept]
                outs[1][:, column] = one[kept:]

    halves, layout = key_sets[-1]
    total_keys = key_count(halves)
    extras = [extra_columns(layout, half) for half in range(2)]
    longest = [None] * groups

    def begin(group):
        fill(group, halves, extras)
        if first_phase:
            key = keys[group, :total_keys, :HD].astype(jnp.float32)
            squares = jnp.sum(key * key, axis=1, keepdims=True)
            longest[group] = jnp.max(squares, axis=0, keepdims=True)

    def weigh(index):
        group = index // blocks_a_group
        query = query_rows(index)
        if first_phase:
            wide = query.astype(jnp.float32)
            bound = jnp.sqrt(jnp.sum(wide * wide, axis=1, keepdims=True) * longest[group])
            shift = jnp.ceil(bound * (1.0 / SHIFT_STEP)) * SHIFT_STEP
            extra = jnp.where(lane == 0, 1.0, jnp.where(lane == 1, -shift, 0.0))
            extra = extra.astype(jnp.bfloat16)
            state_extra[pl.ds(index * block, block), :] = extra
        else:
            extra = state_extra[pl.ds(index * block, block), :]
        query = jnp.concatenate([query, extra], axis=1)
        for start in range(0, total_keys, chunk):
            made = scores_of(query, group, start, first_phase)
            weights[index % 2][:, pl.ds(start, chunk)] = jnp.exp2(made * EXP2_SCALE).astype(
                jnp.bfloat16
            )

    def finish(index, extremes):
        group = index // blocks_a_group
        summed = jnp.dot(
            weights[index % 2][:, :total_keys],
            values[group, :total_keys, :],
            preferred_element_type=jnp.float32,
        )
        rows = pl.ds(index * block, block)
        if first_phase:
            state_sum[rows, :] = summed
            return extremes
        summed = summed + state_sum[rows, :]
        total = summed[:, HD:]
        give(index, (summed[:, :HD] / total).astype(jnp.bfloat16))
        return jnp.minimum(extremes[0], total), jnp.maximum(extremes[1], total)

    begin(0)
    extremes = (jnp.ones((block, HD), jnp.float32),) * 2
    for index in range(blocks + 1):
        if index >= 1:
            extremes = finish(index - 1, extremes)
        if index < blocks:
            weigh(index)
            if (index + 1) % blocks_a_group == 0 and index + 1 < blocks:
                begin((index + 1) // blocks_a_group)
    if first_phase:
        return

    @pl.when((jnp.min(extremes[0]) < LOWEST_TOTAL) | (jnp.max(extremes[1]) > HIGHEST_TOTAL))
    def exact():
        for number, (halves, layout) in enumerate(key_sets):
            extras = [extra_columns(layout, half) for half in range(2)]
            for group in range(groups):
                fill(group, halves, extras)

            def one_block(index, carry):
                group = index // blocks_a_group
                extra = (lane == 0).astype(jnp.float32).astype(jnp.bfloat16)
                query = jnp.concatenate([query_rows(index), extra], axis=1)
                rows = pl.ds(pl.multiple_of(index * block, block), block)
                if number == 0:
                    top = jnp.full((block, HD), MASKED, jnp.float32)
                    summed = jnp.zeros((block, 2 * HD), jnp.float32)
                else:
                    top = slow_top[rows, :]
                    summed = slow_sum[rows, :]
                best = top
                for start in range(0, key_count(halves), chunk):
                    made = scores_of(query, group, start, number == 0)
                    for at in range(0, chunk, HD):
                        best = jnp.maximum(best, made[:, at : at + HD])
                best = jnp.broadcast_to(jnp.max(best, axis=1, keepdims=True), (block, HD))
                fade = jnp.exp2((top - best) * EXP2_SCALE)
                summed = summed * jnp.concatenate([fade, fade], axis=1)
                for start in range(0, key_count(halves), chunk):
                    made = scores_of(query, group, start, number == 0)
                    parts = [
                        jnp.exp2((made[:, at : at + HD] - best) * EXP2_SCALE)
                        for at in range(0, chunk, HD)
                    ]
                    summed = summed + jnp.dot(
                        jnp.concatenate(parts, axis=1).astype(jnp.bfloat16),
                        values[group, pl.ds(start, chunk), :],
                        preferred_element_type=jnp.float32,
                    )
                slow_top[rows, :] = best
                slow_sum[rows, :] = summed
                return carry

            lax.fori_loop(0, blocks, one_block, 0)
        for index in range(blocks):
            rows = pl.ds(index * block, block)
            give(index, (slow_sum[rows, :HD] / slow_sum[rows, HD:]).astype(jnp.bfloat16))


def attend(limits, owners, queries, part, parts, key_sets, spec, state):
    tokens, _, _, head_size = spec[:4]
    total_keys = 2 * max(sum(piece.shape[0] for piece in mine) for mine, _, _ in key_sets)
    columns = queries.shape[1] // parts
    groups = columns // (PER_GROUP * HD)
    block_heads = 4
    block = block_heads * tokens
    rows = PER_GROUP * groups * tokens
    pieces = [piece for mine, theirs, _ in key_sets for piece in mine + theirs]
    layouts = tuple(
        (tuple(layout), (len(mine), len(theirs))) for mine, theirs, layout in key_sets
    )
    operands = queries.size * 2 + sum(piece.size for piece in pieces) * 2 + rows * HD * 12
    scratch = groups * total_keys * HD * 8 + block * total_keys * 4 + rows * HD * 12
    whole = pl.BlockSpec(memory_space=pltpu.VMEM)
    scalars = pl.BlockSpec(memory_space=pltpu.SMEM)
    kept = tokens // head_size
    scratch_shapes = [
        pltpu.SMEM((owners.shape[1],), jnp.int32),
        pltpu.VMEM((groups, total_keys, 2 * HD), jnp.bfloat16),
        pltpu.VMEM((groups, total_keys, 2 * HD), jnp.bfloat16),
    ] + [pltpu.VMEM((block, total_keys), jnp.bfloat16)] * 2
    if state is None:
        state = ()
        out_shape = [
            jax.ShapeDtypeStruct((rows, 2 * HD), jnp.float32),
            jax.ShapeDtypeStruct((rows, HD), jnp.bfloat16),
        ]
    else:
        out_shape = [
            jax.ShapeDtypeStruct((kept, columns), jnp.bfloat16),
            jax.ShapeDtypeStruct((tokens - kept, columns), jnp.bfloat16),
        ]
        scratch_shapes += [
            pltpu.VMEM((rows, 2 * HD), jnp.float32),
            pltpu.VMEM((rows, HD), jnp.float32),
        ]
    return pl.pallas_call(
        functools.partial(attend_kernel, spec, layouts, part, block_heads, groups),
        out_shape=out_shape,
        in_specs=[scalars] * 2 + [whole] * (1 + len(pieces) + len(state)),
        out_specs=[whole] * 2,
        scratch_shapes=scratch_shapes,
        compiler_params=pltpu.CompilerParams(vmem_limit_bytes=operands + scratch + (6 << 20)),
        cost_estimate=pl.CostEstimate(
            flops=8 * tokens * columns * total_keys,
            bytes_accessed=4 * tokens * columns + 2 * total_keys * columns // PER_GROUP,
            transcendentals=0,
        ),
    )(limits, owners, queries, *pieces, *state)


def pick_kernel(group_size, parts, cache_ref, *refs):
    request = lax.axis_index("seq") // group_size
    columns = cache_ref.shape[2] // parts
    for part in range(parts):
        at = pl.ds(part * columns, columns)
        refs[part][...] = cache_ref[1 - request, :, at]
        refs[parts + part][...] = cache_ref[request, :, at]


def pick(cache, group_size, parts):
    whole = pl.BlockSpec(memory_space=pltpu.VMEM)
    one = jax.ShapeDtypeStruct((cache.shape[1], cache.shape[2] // parts), cache.dtype)
    picked = pl.pallas_call(
        functools.partial(pick_kernel, group_size, parts),
        out_shape=[one] * (2 * parts),
        in_specs=[whole],
        out_specs=[whole] * (2 * parts),
        compiler_params=pltpu.CompilerParams(vmem_limit_bytes=8 << 20),
    )(cache)
    return list(picked[:parts]), list(picked[parts:])


def split_kernel(from_ref, *to_refs):
    columns = to_refs[0].shape[1]
    for part, ref in enumerate(to_refs):
        ref[...] = from_ref[:, pl.ds(part * columns, columns)]


def split(value, parts):
    whole = pl.BlockSpec(memory_space=pltpu.VMEM)
    one = jax.ShapeDtypeStruct((value.shape[0], value.shape[1] // parts), value.dtype)
    return list(
        pl.pallas_call(
            split_kernel,
            out_shape=[one] * parts,
            in_specs=[whole],
            out_specs=[whole] * parts,
            compiler_params=pltpu.CompilerParams(vmem_limit_bytes=8 << 20),
        )(value)
    )


def join_kernel(spots, count, *refs):
    parts, (out_ref, done) = refs[len(refs) - 2 - count : -2], refs[-2:]
    side = out_ref.shape[1] // 2
    my_head = lax.axis_index("head")
    copies = []
    for at, (ref, (received, start)) in enumerate(zip(parts, spots)):
        owner = 1 - my_head if received else my_head
        first = pl.multiple_of(owner * side + start, HD)
        copies.append(
            pltpu.make_async_copy(ref, out_ref.at[:, pl.ds(first, ref.shape[1])], done.at[at])
        )
    for copy in copies:
        copy.start()
    for copy in copies:
        copy.wait()


def join(pieces, spots, columns, partial):
    earlier = [] if partial is None else [partial]
    return pl.pallas_call(
        functools.partial(join_kernel, spots, len(pieces)),
        out_shape=jax.ShapeDtypeStruct((pieces[0].shape[0], columns), pieces[0].dtype),
        in_specs=[pl.BlockSpec(memory_space=pl.ANY)] * len(earlier)
        + [pl.BlockSpec(memory_space=pltpu.VMEM)] * len(pieces),
        out_specs=pl.BlockSpec(memory_space=pl.ANY),
        scratch_shapes=[pltpu.SemaphoreType.DMA((len(pieces),))],
        input_output_aliases={0: 0} if earlier else {},
        compiler_params=pltpu.CompilerParams(vmem_limit_bytes=8 << 20),
    )(*earlier, *pieces)


def put_together(kept, received):
    columns = kept[0].shape[1]
    pieces = kept + received
    spots = [(at >= len(kept), at % len(kept) * columns) for at in range(len(pieces))]
    out = join(pieces[:-1], spots[:-1], columns * len(pieces), None)
    return join(pieces[-1:], spots[-1:], columns * len(pieces), out)


def body(span_query, span_kv, prefix_cache, prefix_len, block_owner):
    seq_size = lax.axis_size("seq")
    head_size = lax.axis_size("head")
    group_size = seq_size // REQS
    tokens = span_kv.shape[0]
    page = prefix_cache.shape[1]
    groups = span_kv.shape[1] // (2 * HD)
    parts = 2 if groups % 2 == 0 else 1
    bits = [1 << at for at in range(1, group_size.bit_length() - 1)]
    orders = (bits, bits[::-1])

    stages = len(bits)

    def send(rows, stage):
        return hop(rows, tuple(order[stage] for order in orders))

    def swap_cores(pieces):
        return hop(pieces[0] if len(pieces) == 1 else jnp.concatenate(pieces, axis=0), (1, 1))

    def whole_layout(layout):
        for stage in range(stages):
            layout = layout + shifted(layout, 1 << stage)
        return layout

    span_layout = whole_layout([(0, SPAN_ROWS, tokens)])
    page_layout = whole_layout([(0, OWN_PAGE, page), (0, CROSSED_PAGE, page)])
    near_count = (1 << (stages - 1)) + 1
    near_layout, far_layout = span_layout[:near_count], span_layout[near_count:] + page_layout

    spec = (tokens, page, group_size, head_size, orders)
    common = (prefix_len, block_owner, span_query)

    def exchange(rows):
        early = send(rows, stages - 1)
        forward = send(rows, 0)
        for stage in range(1, stages - 1):
            seen = jnp.concatenate([rows, forward], axis=0)
            forward = jnp.concatenate([forward, send(seen, stage)], axis=0)
        return early, forward

    def round_pages(rows, first):
        pieces = [rows, first]
        for stage in range(1, stages - 1):
            pieces.append(send(jnp.concatenate(pieces, axis=0), stage))
        return jnp.concatenate(pieces, axis=0)

    span = split(span_kv, parts)
    other_pages, own_pages = pick(prefix_cache, group_size, parts)
    crossed, early, forward = [], [], []
    for part in range(parts):
        if part:
            forward[-1], span[part] = together(forward[-1], span[part])
            crossed[-1], other_pages[part] = together(crossed[-1], other_pages[part])
        crossed.append(hop(other_pages[part], (group_size, group_size)))
        one_early, one_forward = exchange(span[part])
        early.append(one_early)
        forward.append(one_forward)
    near = [list(pieces) for pieces in zip(span, forward, early)]
    late = [send(rows, stages - 1) for rows in forward]
    pages = [jnp.concatenate(pair, axis=0) for pair in zip(own_pages, crossed)]
    full = [round_pages(pages[0], send(pages[0], 0))] + [None] * (parts - 1)
    near_swapped = [swap_cores(near[0])]
    near_swapped[0], full[0], *tied = together(
        near_swapped[0], full[0], *pages[1:], *forward[1:], *early[1:]
    )
    for part in range(1, parts):
        pages[part], forward[part], early[part] = tied[part - 1 :: parts - 1]
        late[part] = send(forward[part], stages - 1)
        near[part] = [span[part], forward[part], early[part]]
        near_swapped.append(swap_cores(near[part]))

    results = []
    for part in range(parts):
        near_set = (near[part], [near_swapped[part]], near_layout)
        state = attend(*common, part, parts, [near_set], spec, None)
        arrived, state = together(send(full[part], stages - 1), state)
        if part + 1 < parts:
            first, state = together(send(pages[part + 1], 0), state)
            full[part + 1] = round_pages(pages[part + 1], first)
        mine = [late[part], full[part], arrived]
        swapped = swap_cores(mine)
        far_set = (mine, [swapped], far_layout)
        results.append(attend(*common, part, parts, [near_set, far_set], spec, state))
    if head_size != 2:
        rows = jnp.concatenate([jnp.concatenate(pair, axis=0) for pair in results], axis=1)
        return lax.all_to_all(rows, "head", split_axis=0, concat_axis=1, tiled=True)
    kept = [pair[0] for pair in results]
    received = [lax.ppermute(pair[1], "head", [(0, 1), (1, 0)]) for pair in results]
    return put_together(kept, received)


def solution(mesh):
    placed = (P("seq", "head"), P("seq", "head"), P("seq", None, "head"), P(), P())
    return jax.shard_map(
        body, mesh=mesh, in_specs=placed, out_specs=P(("seq", "head"), None), check_vma=False
    )
```

```python
import functools
import math

import jax
import jax.numpy as jnp
from jax import lax
from jax.experimental import pallas as pl
from jax.experimental.pallas import tpu as pltpu
from jax.sharding import PartitionSpec as P

QH = 64
KVH = 8
HD = 128
REQS = 2
PER_GROUP = QH // KVH
EXP2_SCALE = HD ** (-0.5) * math.log2(math.e)
MASKED = -1e30
KEY_CHUNK = 256
HEADS_A_BLOCK = (2, 4, 2)
SHIFT_STEP = 32.0
LOWEST_TOTAL = 1e-20
HIGHEST_TOTAL = 1e30
SPAN_ROWS, OWN_PAGE, CROSSED_PAGE = range(3)


def hop(value, bit_of_core):
    count = lax.axis_size("seq")
    return lax.ppermute(
        value, "seq", [(source, source ^ bit_of_core[source % 2]) for source in range(count)]
    )


def together(*values):
    return lax.optimization_barrier(values)


def shifted(layout, slots):
    return [(slot + slots, kind, rows) for slot, kind, rows in layout]


def hypercube_order(bits):
    order = [0]
    for bit in bits:
        order = order + [offset ^ bit for offset in order]
    return order


def mask_kernel(spec, layouts, limit_ref, owner_ref, *refs):
    tokens, page, group_size, _, orders = spec
    outs, page_seen = refs[:-1], refs[-1]
    me = lax.axis_index("seq")
    request = me // group_size
    offsets = [hypercube_order(order) for order in orders]

    def note_page(index, carry):
        page_seen[owner_ref[request, index]] = jnp.clip(limit_ref[request] - index * page, 0, page)
        return carry

    lax.fori_loop(0, owner_ref.shape[1], note_page, 0)
    for out, layout in zip(outs, layouts):
        start = 0
        for half in range(2):
            holder = me ^ half
            for slot, kind, rows in layout:
                source = holder ^ jnp.where(holder % 2 == 0, offsets[0][slot], offsets[1][slot])
                if kind == SPAN_ROWS:
                    count = jnp.where(source <= me, tokens, 0)
                elif kind == OWN_PAGE:
                    count = page_seen[source]
                else:
                    count = page_seen[source ^ group_size]
                row = lax.broadcasted_iota(jnp.int32, (rows, HD), 0)
                column = lax.broadcasted_iota(jnp.int32, (rows, HD), 1)
                mask = jnp.where(row < count, jnp.float32(0.0), jnp.float32(MASKED))
                one = jnp.where(column == 1, jnp.float32(1.0), jnp.float32(0.0))
                out[pl.ds(start, rows), :] = jnp.where(column == 0, mask, one).astype(jnp.bfloat16)
                start += rows


def masks(limits, owners, layouts, spec):
    scalars = pl.BlockSpec(memory_space=pltpu.SMEM)
    counts = [2 * sum(rows for _, _, rows in layout) for layout in layouts]
    return list(
        pl.pallas_call(
            functools.partial(mask_kernel, spec, layouts),
            out_shape=[jax.ShapeDtypeStruct((count, HD), jnp.bfloat16) for count in counts],
            in_specs=[scalars] * 2,
            out_specs=[pl.BlockSpec(memory_space=pltpu.VMEM)] * len(counts),
            scratch_shapes=[pltpu.SMEM((owners.shape[1],), jnp.int32)],
            compiler_params=pltpu.CompilerParams(vmem_limit_bytes=16 << 20),
        )(limits, owners)
    )


def attend_kernel(spec, sizes, part, groups, q_ref, *refs):
    tokens, _, _, head_size, _ = spec
    first_phase = len(sizes) == 1
    key_sets = []
    for counts in sizes:
        extra, refs = refs[0], refs[1:]
        halves = []
        for count in counts:
            halves.append(refs[:count])
            refs = refs[count:]
        key_sets.append((halves, extra))
    (state_sum, state_extra), refs = refs[:2], refs[2:]
    if first_phase:
        keys, values, weights = refs[0], refs[1], refs[2:4]
    else:
        outs, keys, values, weights = refs[:2], refs[2], refs[3], refs[4:6]
        slow_sum, slow_top = refs[6], refs[7]
    chunk = KEY_CHUNK
    my_head = lax.axis_index("head")

    def key_count(halves):
        return sum(ref.shape[0] for half in halves for ref in half)

    def fill(group, halves, extra):
        total_keys = key_count(halves)
        column = (part * groups + group) * 2 * HD
        start = 0
        for ref in [ref for half in halves for ref in half]:
            at = pl.ds(start, ref.shape[0])
            first = column % ref.shape[1]
            keys[group, at, :HD] = ref[:, pl.ds(first, HD)]
            values[group, at, :HD] = ref[:, pl.ds(first + HD, HD)]
            start += ref.shape[0]
        keys[group, :total_keys, HD:] = extra[...]
        values[group, :total_keys, HD:] = jnp.ones((total_keys, HD), jnp.bfloat16)

    def lane_of(heads):
        return lax.broadcasted_iota(jnp.int32, (heads * tokens, HD), 1)

    def query_rows(first, heads):
        at = part * groups * PER_GROUP + first
        columns = [pl.ds(pl.multiple_of((at + head) * HD, HD), HD) for head in range(heads)]
        return jnp.concatenate([q_ref[:, column] for column in columns], axis=0)

    def scores_of(query, group, start, is_span):
        made = lax.dot_general(
            query,
            keys[group, pl.ds(start, chunk), :],
            (((1,), (1,)), ((), ())),
            preferred_element_type=jnp.float32,
        )
        if start == 0 and is_span:
            rows = query.shape[0]
            causal = lax.broadcasted_iota(jnp.int32, (rows, tokens), 1) <= (
                lax.broadcasted_iota(jnp.int32, (rows, tokens), 0) % tokens
            )
            own = jnp.where(causal, made[:, :tokens], MASKED)
            made = jnp.concatenate([own, made[:, tokens:]], axis=1)
        return made

    def give(first, heads, result):
        kept = tokens // head_size
        for head in range(heads):
            column = pl.ds((first + head) * HD, HD)
            one = result[head * tokens : (head + 1) * tokens]
            if head_size == 2:
                low, high = one[:kept], one[kept:]
                outs[0][:, column] = jnp.where(my_head == 0, low, high)
                outs[1][:, column] = jnp.where(my_head == 0, high, low)
            else:
                outs[0][:, column] = one[:kept]
                outs[1][:, column] = one[kept:]

    halves, extra_ref = key_sets[-1]
    total_keys = key_count(halves)
    longest = [None] * groups

    def begin(group):
        fill(group, halves, extra_ref)
        if first_phase:
            key = keys[group, :total_keys, :HD].astype(jnp.float32)
            squares = jnp.sum(key * key, axis=1, keepdims=True)
            longest[group] = jnp.max(squares, axis=0, keepdims=True)

    def weigh(index):
        group, first, heads = blocks[index]
        rows = pl.ds(first * tokens, heads * tokens)
        query = query_rows(first, heads)
        if first_phase:
            wide = query.astype(jnp.float32)
            bound = jnp.sqrt(jnp.sum(wide * wide, axis=1, keepdims=True) * longest[group])
            shift = jnp.ceil(bound * (1.0 / SHIFT_STEP)) * SHIFT_STEP
            lane = lane_of(heads)
            extra = jnp.where(lane == 0, 1.0, jnp.where(lane == 1, -shift, 0.0))
            extra = extra.astype(jnp.bfloat16)
            state_extra[rows, :] = extra
        else:
            extra = state_extra[pl.ds((part * groups * PER_GROUP + first) * tokens, heads * tokens), :]
        query = jnp.concatenate([query, extra], axis=1)
        for start in range(0, total_keys, chunk):
            made = scores_of(query, group, start, first_phase)
            weights[index % 2][: heads * tokens, pl.ds(start, chunk)] = jnp.exp2(
                made * EXP2_SCALE
            ).astype(jnp.bfloat16)

    def finish(index, extremes):
        group, first, heads = blocks[index]
        summed = jnp.dot(
            weights[index % 2][: heads * tokens, :total_keys],
            values[group, :total_keys, :],
            preferred_element_type=jnp.float32,
        )
        if first_phase:
            state_sum[pl.ds(first * tokens, heads * tokens), :] = summed
            return extremes
        old = pl.ds((part * groups * PER_GROUP + first) * tokens, heads * tokens)
        summed = summed + state_sum[old, :]
        total = summed[:, HD:]
        give(first, heads, (summed[:, :HD] / total).astype(jnp.bfloat16))
        lowest, highest = extremes
        for head in range(heads):
            one = total[head * tokens : (head + 1) * tokens]
            lowest, highest = jnp.minimum(lowest, one), jnp.maximum(highest, one)
        return lowest, highest

    blocks = []
    for group in range(groups):
        at = group * PER_GROUP
        for heads in HEADS_A_BLOCK:
            blocks.append((group, at, heads))
            at += heads
    begin(0)
    extremes = (jnp.ones((tokens, HD), jnp.float32),) * 2
    for index in range(len(blocks) + 1):
        if index >= 1:
            extremes = finish(index - 1, extremes)
        if index < len(blocks):
            weigh(index)
            if index + 1 < len(blocks) and blocks[index + 1][0] != blocks[index][0]:
                begin(blocks[index + 1][0])
    if first_phase:
        return

    @pl.when((jnp.min(extremes[0]) < LOWEST_TOTAL) | (jnp.max(extremes[1]) > HIGHEST_TOTAL))
    def exact():
        heads = 4
        block = heads * tokens
        count = groups * PER_GROUP // heads
        for number, (halves, extra_ref) in enumerate(key_sets):
            for group in range(groups):
                fill(group, halves, extra_ref)

            def one_block(index, carry):
                group = index * heads // PER_GROUP
                extra = (lane_of(heads) == 0).astype(jnp.float32).astype(jnp.bfloat16)
                query = jnp.concatenate([query_rows(index * heads, heads), extra], axis=1)
                rows = pl.ds(pl.multiple_of(index * block, block), block)
                if number == 0:
                    top = jnp.full((block, HD), MASKED, jnp.float32)
                    summed = jnp.zeros((block, 2 * HD), jnp.float32)
                else:
                    top = slow_top[rows, :]
                    summed = slow_sum[rows, :]
                best = top
                for start in range(0, key_count(halves), chunk):
                    made = scores_of(query, group, start, number == 0)
                    for at in range(0, chunk, HD):
                        best = jnp.maximum(best, made[:, at : at + HD])
                best = jnp.broadcast_to(jnp.max(best, axis=1, keepdims=True), (block, HD))
                fade = jnp.exp2((top - best) * EXP2_SCALE)
                summed = summed * jnp.concatenate([fade, fade], axis=1)
                for start in range(0, key_count(halves), chunk):
                    made = scores_of(query, group, start, number == 0)
                    parts = [
                        jnp.exp2((made[:, at : at + HD] - best) * EXP2_SCALE)
                        for at in range(0, chunk, HD)
                    ]
                    summed = summed + jnp.dot(
                        jnp.concatenate(parts, axis=1).astype(jnp.bfloat16),
                        values[group, pl.ds(start, chunk), :],
                        preferred_element_type=jnp.float32,
                    )
                slow_top[rows, :] = best
                slow_sum[rows, :] = summed
                return carry

            lax.fori_loop(0, count, one_block, 0)
        for index in range(count):
            rows = pl.ds(index * block, block)
            result = (slow_sum[rows, :HD] / slow_sum[rows, HD:]).astype(jnp.bfloat16)
            give(index * heads, heads, result)


def attend(queries, part, parts, key_sets, spec, state):
    tokens, _, _, head_size = spec[:4]
    total_keys = max(extra.shape[0] for _, _, extra in key_sets)
    columns = queries.shape[1] // parts
    groups = columns // (PER_GROUP * HD)
    block = max(HEADS_A_BLOCK) * tokens
    rows = PER_GROUP * groups * tokens
    pieces = [piece for mine, theirs, extra in key_sets for piece in [extra] + mine + theirs]
    sizes = tuple((len(mine), len(theirs)) for mine, theirs, _ in key_sets)
    operands = queries.size * 2 + sum(piece.size for piece in pieces) * 2 + rows * HD * 12
    scratch = groups * total_keys * HD * 8 + block * total_keys * 4 + rows * HD * 12
    whole = pl.BlockSpec(memory_space=pltpu.VMEM)
    kept = tokens // head_size
    scratch_shapes = [pltpu.VMEM((groups, total_keys, 2 * HD), jnp.bfloat16)] * 2
    scratch_shapes += [pltpu.VMEM((block, total_keys), jnp.bfloat16)] * 2
    if state is None:
        state = ()
        out_shape = [
            jax.ShapeDtypeStruct((rows, 2 * HD), jnp.float32),
            jax.ShapeDtypeStruct((rows, HD), jnp.bfloat16),
        ]
    else:
        out_shape = [
            jax.ShapeDtypeStruct((kept, columns), jnp.bfloat16),
            jax.ShapeDtypeStruct((tokens - kept, columns), jnp.bfloat16),
        ]
        scratch_shapes += [
            pltpu.VMEM((rows, 2 * HD), jnp.float32),
            pltpu.VMEM((rows, HD), jnp.float32),
        ]
    return pl.pallas_call(
        functools.partial(attend_kernel, spec, sizes, part, groups),
        out_shape=out_shape,
        in_specs=[whole] * (1 + len(pieces) + len(state)),
        out_specs=[whole] * 2,
        scratch_shapes=scratch_shapes,
        compiler_params=pltpu.CompilerParams(vmem_limit_bytes=operands + scratch + (8 << 20)),
        cost_estimate=pl.CostEstimate(
            flops=8 * tokens * columns * total_keys,
            bytes_accessed=4 * tokens * columns + 2 * total_keys * columns // PER_GROUP,
            transcendentals=0,
        ),
    )(queries, *pieces, *state)


def pick_kernel(group_size, cache_ref, other_ref, own_ref):
    request = lax.axis_index("seq") // group_size
    other_ref[...] = cache_ref[1 - request]
    own_ref[...] = cache_ref[request]


def pick(cache, group_size):
    whole = pl.BlockSpec(memory_space=pltpu.VMEM)
    return pl.pallas_call(
        functools.partial(pick_kernel, group_size),
        out_shape=[jax.ShapeDtypeStruct(cache.shape[1:], cache.dtype)] * 2,
        in_specs=[whole],
        out_specs=[whole] * 2,
        compiler_params=pltpu.CompilerParams(vmem_limit_bytes=8 << 20),
    )(cache)


def join_kernel(spots, count, *refs):
    parts, (out_ref, done) = refs[len(refs) - 2 - count : -2], refs[-2:]
    side = out_ref.shape[1] // 2
    my_head = lax.axis_index("head")
    copies = []
    for at, (ref, (received, start)) in enumerate(zip(parts, spots)):
        owner = 1 - my_head if received else my_head
        first = pl.multiple_of(owner * side + start, HD)
        copies.append(
            pltpu.make_async_copy(ref, out_ref.at[:, pl.ds(first, ref.shape[1])], done.at[at])
        )
    for copy in copies:
        copy.start()
    for copy in copies:
        copy.wait()


def join(pieces, spots, columns, partial):
    earlier = [] if partial is None else [partial]
    return pl.pallas_call(
        functools.partial(join_kernel, spots, len(pieces)),
        out_shape=jax.ShapeDtypeStruct((pieces[0].shape[0], columns), pieces[0].dtype),
        in_specs=[pl.BlockSpec(memory_space=pl.ANY)] * len(earlier)
        + [pl.BlockSpec(memory_space=pltpu.VMEM)] * len(pieces),
        out_specs=pl.BlockSpec(memory_space=pl.ANY),
        scratch_shapes=[pltpu.SemaphoreType.DMA((len(pieces),))],
        input_output_aliases={0: 0} if earlier else {},
        compiler_params=pltpu.CompilerParams(vmem_limit_bytes=8 << 20),
    )(*earlier, *pieces)


def put_together(kept, received):
    columns = kept[0].shape[1]
    pieces = kept + received
    spots = [(at >= len(kept), at % len(kept) * columns) for at in range(len(pieces))]
    out = join(pieces[:-1], spots[:-1], columns * len(pieces), None)
    return join(pieces[-1:], spots[-1:], columns * len(pieces), out)


def body(span_query, span_kv, prefix_cache, prefix_len, block_owner):
    seq_size = lax.axis_size("seq")
    head_size = lax.axis_size("head")
    group_size = seq_size // REQS
    tokens = span_kv.shape[0]
    page = prefix_cache.shape[1]
    groups = span_kv.shape[1] // (2 * HD)
    parts = 2 if groups % 2 == 0 else 1
    bits = [1 << at for at in range(1, group_size.bit_length() - 1)]
    orders = (bits, bits[::-1])

    stages = len(bits)

    def send(rows, stage):
        return hop(rows, tuple(order[stage] for order in orders))

    def swap_cores(pieces):
        return hop(pieces[0] if len(pieces) == 1 else jnp.concatenate(pieces, axis=0), (1, 1))

    def whole_layout(layout):
        for stage in range(stages):
            layout = layout + shifted(layout, 1 << stage)
        return layout

    span_layout = whole_layout([(0, SPAN_ROWS, tokens)])
    page_layout = whole_layout([(0, OWN_PAGE, page), (0, CROSSED_PAGE, page)])

    other_page, own_page = pick(prefix_cache, group_size)
    crossed = hop(other_page, (group_size, group_size))

    span_early = send(span_kv, stages - 1)
    span_forward = send(span_kv, 0)
    for stage in range(1, stages - 1):
        seen = jnp.concatenate([span_kv, span_forward], axis=0)
        span_forward = jnp.concatenate([span_forward, send(seen, stage)], axis=0)
    span_late = send(span_forward, stages - 1)
    spec = (tokens, page, group_size, head_size, orders)
    span_masks, page_masks = masks(prefix_len, block_owner, (span_layout, page_layout), spec)
    span_forward, span_masks, crossed = together(span_forward, span_masks, crossed)
    pages = [jnp.concatenate([own_page, crossed], axis=0)]
    pages.append(send(pages[0], 0))
    span_early, span_late = together(span_early, span_late)
    pages[1], span_late = together(pages[1], span_late)
    span = [jnp.concatenate([span_kv, span_forward, span_early, span_late], axis=0)]
    span_swapped = [swap_cores(span)]

    span_set = (span, span_swapped, span_masks)
    state = attend(span_query, 0, 1, [span_set], spec, None)

    for stage in range(1, stages - 1):
        pages.append(send(jnp.concatenate(pages, axis=0), stage))
    columns = span_kv.shape[1] // parts
    cuts = [slice(part * columns, (part + 1) * columns) for part in range(parts)]
    held = [jnp.concatenate([piece[:, cut] for piece in pages], axis=0) for cut in cuts]
    arrived = [send(rows, stages - 1) for rows in held]
    results = []
    for part in range(parts):
        arrived[part], state = together(arrived[part], state)
        mine = [held[part], arrived[part]]
        page_set = (mine, [swap_cores(mine)], page_masks)
        results.append(attend(span_query, part, parts, [span_set, page_set], spec, state))
    if head_size != 2:
        rows = jnp.concatenate([jnp.concatenate(pair, axis=0) for pair in results], axis=1)
        return lax.all_to_all(rows, "head", split_axis=0, concat_axis=1, tiled=True)
    kept = [pair[0] for pair in results]
    received = [lax.ppermute(pair[1], "head", [(0, 1), (1, 0)]) for pair in results]
    return put_together(kept, received)


def solution(mesh):
    placed = (P("seq", "head"), P("seq", "head"), P("seq", None, "head"), P(), P())
    return jax.shard_map(
        body, mesh=mesh, in_specs=placed, out_specs=P(("seq", "head"), None), check_vma=False
    )
```

```python
import functools
import math

import jax
import jax.numpy as jnp
from jax import lax
from jax.experimental import pallas as pl
from jax.experimental.pallas import tpu as pltpu
from jax.sharding import PartitionSpec as P

QH = 64
KVH = 8
HD = 128
REQS = 2
PER_GROUP = QH // KVH
EXP2_SCALE = HD ** (-0.5) * math.log2(math.e)
MASKED = -1e30
KEY_CHUNK = 256
MOST_HEADS = 4
SHIFT_STEP = 32.0
LOWEST_TOTAL = 1e-20
HIGHEST_TOTAL = 1e30
SPAN_ROWS, OWN_PAGE, CROSSED_PAGE = range(3)


def hop(value, bit_of_core):
    count = lax.axis_size("seq")
    return lax.ppermute(
        value, "seq", [(source, source ^ bit_of_core[source % 2]) for source in range(count)]
    )


def together(*values):
    return lax.optimization_barrier(values)


def shifted(layout, slots):
    return [(slot + slots, kind, rows) for slot, kind, rows in layout]


def hypercube_order(bits):
    order = [0]
    for bit in bits:
        order = order + [offset ^ bit for offset in order]
    return order


def mask_kernel(spec, layouts, limit_ref, owner_ref, *refs):
    tokens, page, group_size, _, orders = spec
    outs, page_seen = refs[:-1], refs[-1]
    me = lax.axis_index("seq")
    request = me // group_size
    offsets = [hypercube_order(order) for order in orders]

    def note_page(index, carry):
        page_seen[owner_ref[request, index]] = jnp.clip(limit_ref[request] - index * page, 0, page)
        return carry

    lax.fori_loop(0, owner_ref.shape[1], note_page, 0)
    for out, layout in zip(outs, layouts):
        start = 0
        for half in range(2):
            holder = me ^ half
            for slot, kind, rows in layout:
                source = holder ^ jnp.where(holder % 2 == 0, offsets[0][slot], offsets[1][slot])
                if kind == SPAN_ROWS:
                    count = jnp.where(source <= me, tokens, 0)
                elif kind == OWN_PAGE:
                    count = page_seen[source]
                else:
                    count = page_seen[source ^ group_size]
                row = lax.broadcasted_iota(jnp.int32, (rows, HD), 0)
                column = lax.broadcasted_iota(jnp.int32, (rows, HD), 1)
                mask = jnp.where(row < count, jnp.float32(0.0), jnp.float32(MASKED))
                one = jnp.where(column == 1, jnp.float32(1.0), jnp.float32(0.0))
                out[pl.ds(start, rows), :] = jnp.where(column == 0, mask, one).astype(jnp.bfloat16)
                start += rows


def masks(limits, owners, layouts, spec):
    scalars = pl.BlockSpec(memory_space=pltpu.SMEM)
    counts = [2 * sum(rows for _, _, rows in layout) for layout in layouts]
    return list(
        pl.pallas_call(
            functools.partial(mask_kernel, spec, layouts),
            out_shape=[jax.ShapeDtypeStruct((count, HD), jnp.bfloat16) for count in counts],
            in_specs=[scalars] * 2,
            out_specs=[pl.BlockSpec(memory_space=pltpu.VMEM)] * len(counts),
            scratch_shapes=[pltpu.SMEM((owners.shape[1],), jnp.int32)],
            compiler_params=pltpu.CompilerParams(vmem_limit_bytes=16 << 20),
        )(limits, owners)
    )


def attend_kernel(spec, sizes, part, groups, q_ref, *refs):
    tokens, _, _, head_size, _ = spec
    first_phase = len(sizes) == 1
    key_sets = []
    for counts in sizes:
        extra, refs = refs[0], refs[1:]
        halves = []
        for count in counts:
            halves.append(refs[:count])
            refs = refs[count:]
        key_sets.append((halves, extra))
    (state_sum, state_extra), refs = refs[:2], refs[2:]
    if first_phase:
        keys, values, weights = refs[0], refs[1], refs[2:4]
    else:
        outs, keys, values, weights = refs[:2], refs[2], refs[3], refs[4:6]
        slow_sum, slow_top = refs[6], refs[7]
    chunk = KEY_CHUNK
    my_head = lax.axis_index("head")

    def key_count(halves):
        return sum(ref.shape[0] for half in halves for ref in half)

    def fill(group, halves, extra):
        total_keys = key_count(halves)
        column = (part * groups + group) * 2 * HD
        start = 0
        for ref in [ref for half in halves for ref in half]:
            at = pl.ds(start, ref.shape[0])
            first = column % ref.shape[1]
            keys[group, at, :HD] = ref[:, pl.ds(first, HD)]
            values[group, at, :HD] = ref[:, pl.ds(first + HD, HD)]
            start += ref.shape[0]
        keys[group, :total_keys, HD:] = extra[...]
        values[group, :total_keys, HD:] = jnp.ones((total_keys, HD), jnp.bfloat16)

    def lane_of(heads):
        return lax.broadcasted_iota(jnp.int32, (heads * tokens, HD), 1)

    def query_rows(first, heads):
        at = part * groups * PER_GROUP + first
        columns = [pl.ds(pl.multiple_of((at + head) * HD, HD), HD) for head in range(heads)]
        return jnp.concatenate([q_ref[:, column] for column in columns], axis=0)

    def scores_of(query, group, start, is_span):
        made = lax.dot_general(
            query,
            keys[group, pl.ds(start, chunk), :],
            (((1,), (1,)), ((), ())),
            preferred_element_type=jnp.float32,
        )
        if start == 0 and is_span:
            rows = query.shape[0]
            causal = lax.broadcasted_iota(jnp.int32, (rows, tokens), 1) <= (
                lax.broadcasted_iota(jnp.int32, (rows, tokens), 0) % tokens
            )
            own = jnp.where(causal, made[:, :tokens], MASKED)
            made = jnp.concatenate([own, made[:, tokens:]], axis=1)
        return made

    def give(first, heads, result):
        kept = tokens // head_size
        for head in range(heads):
            column = pl.ds((first + head) * HD, HD)
            one = result[head * tokens : (head + 1) * tokens]
            if head_size == 2:
                low, high = one[:kept], one[kept:]
                outs[0][:, column] = jnp.where(my_head == 0, low, high)
                outs[1][:, column] = jnp.where(my_head == 0, high, low)
            else:
                outs[0][:, column] = one[:kept]
                outs[1][:, column] = one[kept:]

    halves, extra_ref = key_sets[-1]
    total_keys = key_count(halves)
    longest = [None] * groups

    def begin(group):
        fill(group, halves, extra_ref)
        if first_phase:
            key = keys[group, :total_keys, :HD].astype(jnp.float32)
            squares = jnp.sum(key * key, axis=1, keepdims=True)
            longest[group] = jnp.max(squares, axis=0, keepdims=True)

    def weigh(index):
        group, first, heads = blocks[index]
        rows = pl.ds(first * tokens, heads * tokens)
        query = query_rows(first, heads)
        if first_phase:
            wide = query.astype(jnp.float32)
            bound = jnp.sqrt(jnp.sum(wide * wide, axis=1, keepdims=True) * longest[group])
            shift = jnp.ceil(bound * (1.0 / SHIFT_STEP)) * SHIFT_STEP
            lane = lane_of(heads)
            extra = jnp.where(lane == 0, 1.0, jnp.where(lane == 1, -shift, 0.0))
            extra = extra.astype(jnp.bfloat16)
            state_extra[rows, :] = extra
        else:
            extra = state_extra[pl.ds((part * groups * PER_GROUP + first) * tokens, heads * tokens), :]
        query = jnp.concatenate([query, extra], axis=1)
        for start in range(0, total_keys, chunk):
            made = scores_of(query, group, start, first_phase)
            weights[index % 2][: heads * tokens, pl.ds(start, chunk)] = jnp.exp2(
                made * EXP2_SCALE
            ).astype(jnp.bfloat16)

    def finish(index, extremes):
        group, first, heads = blocks[index]
        summed = jnp.dot(
            weights[index % 2][: heads * tokens, :total_keys],
            values[group, :total_keys, :],
            preferred_element_type=jnp.float32,
        )
        if first_phase:
            state_sum[pl.ds(first * tokens, heads * tokens), :] = summed
            return extremes
        old = pl.ds((part * groups * PER_GROUP + first) * tokens, heads * tokens)
        summed = summed + state_sum[old, :]
        total = summed[:, HD:]
        give(first, heads, (summed[:, :HD] / total).astype(jnp.bfloat16))
        lowest, highest = extremes
        for head in range(heads):
            one = total[head * tokens : (head + 1) * tokens]
            lowest, highest = jnp.minimum(lowest, one), jnp.maximum(highest, one)
        return lowest, highest

    blocks = []
    for group in range(groups):
        at = group * PER_GROUP
        counts = [4, 4]
        if group == 0:
            counts = [1, 3] + counts[1:]
        if group == groups - 1:
            counts = counts[:-1] + [3, 1]
        for heads in counts:
            blocks.append((group, at, heads))
            at += heads
    begin(0)
    extremes = (jnp.ones((tokens, HD), jnp.float32),) * 2
    for index in range(len(blocks) + 1):
        if index >= 1:
            extremes = finish(index - 1, extremes)
        if index < len(blocks):
            weigh(index)
            if index + 1 < len(blocks) and blocks[index + 1][0] != blocks[index][0]:
                begin(blocks[index + 1][0])
    if first_phase:
        return

    @pl.when((jnp.min(extremes[0]) < LOWEST_TOTAL) | (jnp.max(extremes[1]) > HIGHEST_TOTAL))
    def exact():
        heads = 4
        block = heads * tokens
        count = groups * PER_GROUP // heads
        for number, (halves, extra_ref) in enumerate(key_sets):
            for group in range(groups):
                fill(group, halves, extra_ref)

            def one_block(index, carry):
                group = index * heads // PER_GROUP
                extra = (lane_of(heads) == 0).astype(jnp.float32).astype(jnp.bfloat16)
                query = jnp.concatenate([query_rows(index * heads, heads), extra], axis=1)
                rows = pl.ds(pl.multiple_of(index * block, block), block)
                if number == 0:
                    top = jnp.full((block, HD), MASKED, jnp.float32)
                    summed = jnp.zeros((block, 2 * HD), jnp.float32)
                else:
                    top = slow_top[rows, :]
                    summed = slow_sum[rows, :]
                best = top
                for start in range(0, key_count(halves), chunk):
                    made = scores_of(query, group, start, number == 0)
                    for at in range(0, chunk, HD):
                        best = jnp.maximum(best, made[:, at : at + HD])
                best = jnp.broadcast_to(jnp.max(best, axis=1, keepdims=True), (block, HD))
                fade = jnp.exp2((top - best) * EXP2_SCALE)
                summed = summed * jnp.concatenate([fade, fade], axis=1)
                for start in range(0, key_count(halves), chunk):
                    made = scores_of(query, group, start, number == 0)
                    parts = [
                        jnp.exp2((made[:, at : at + HD] - best) * EXP2_SCALE)
                        for at in range(0, chunk, HD)
                    ]
                    summed = summed + jnp.dot(
                        jnp.concatenate(parts, axis=1).astype(jnp.bfloat16),
                        values[group, pl.ds(start, chunk), :],
                        preferred_element_type=jnp.float32,
                    )
                slow_top[rows, :] = best
                slow_sum[rows, :] = summed
                return carry

            lax.fori_loop(0, count, one_block, 0)
        for index in range(count):
            rows = pl.ds(index * block, block)
            result = (slow_sum[rows, :HD] / slow_sum[rows, HD:]).astype(jnp.bfloat16)
            give(index * heads, heads, result)


def attend(queries, part, parts, key_sets, spec, state):
    tokens, _, _, head_size = spec[:4]
    total_keys = max(extra.shape[0] for _, _, extra in key_sets)
    columns = queries.shape[1] // parts
    groups = columns // (PER_GROUP * HD)
    block = MOST_HEADS * tokens
    rows = PER_GROUP * groups * tokens
    pieces = [piece for mine, theirs, extra in key_sets for piece in [extra] + mine + theirs]
    sizes = tuple((len(mine), len(theirs)) for mine, theirs, _ in key_sets)
    operands = queries.size * 2 + sum(piece.size for piece in pieces) * 2 + rows * HD * 12
    scratch = groups * total_keys * HD * 8 + block * total_keys * 4 + rows * HD * 12
    whole = pl.BlockSpec(memory_space=pltpu.VMEM)
    kept = tokens // head_size
    scratch_shapes = [pltpu.VMEM((groups, total_keys, 2 * HD), jnp.bfloat16)] * 2
    scratch_shapes += [pltpu.VMEM((block, total_keys), jnp.bfloat16)] * 2
    if state is None:
        state = ()
        out_shape = [
            jax.ShapeDtypeStruct((rows, 2 * HD), jnp.float32),
            jax.ShapeDtypeStruct((rows, HD), jnp.bfloat16),
        ]
    else:
        out_shape = [
            jax.ShapeDtypeStruct((kept, columns), jnp.bfloat16),
            jax.ShapeDtypeStruct((tokens - kept, columns), jnp.bfloat16),
        ]
        scratch_shapes += [
            pltpu.VMEM((rows, 2 * HD), jnp.float32),
            pltpu.VMEM((rows, HD), jnp.float32),
        ]
    return pl.pallas_call(
        functools.partial(attend_kernel, spec, sizes, part, groups),
        out_shape=out_shape,
        in_specs=[whole] * (1 + len(pieces) + len(state)),
        out_specs=[whole] * 2,
        scratch_shapes=scratch_shapes,
        compiler_params=pltpu.CompilerParams(vmem_limit_bytes=operands + scratch + (8 << 20)),
        cost_estimate=pl.CostEstimate(
            flops=8 * tokens * columns * total_keys,
            bytes_accessed=4 * tokens * columns + 2 * total_keys * columns // PER_GROUP,
            transcendentals=0,
        ),
    )(queries, *pieces, *state)


def pick_kernel(group_size, cache_ref, other_ref, own_ref):
    request = lax.axis_index("seq") // group_size
    other_ref[...] = cache_ref[1 - request]
    own_ref[...] = cache_ref[request]


def pick(cache, group_size):
    whole = pl.BlockSpec(memory_space=pltpu.VMEM)
    return pl.pallas_call(
        functools.partial(pick_kernel, group_size),
        out_shape=[jax.ShapeDtypeStruct(cache.shape[1:], cache.dtype)] * 2,
        in_specs=[whole],
        out_specs=[whole] * 2,
        compiler_params=pltpu.CompilerParams(vmem_limit_bytes=8 << 20),
    )(cache)


def join_kernel(spots, count, *refs):
    parts, (out_ref, done) = refs[len(refs) - 2 - count : -2], refs[-2:]
    side = out_ref.shape[1] // 2
    my_head = lax.axis_index("head")
    copies = []
    for at, (ref, (received, start)) in enumerate(zip(parts, spots)):
        owner = 1 - my_head if received else my_head
        first = pl.multiple_of(owner * side + start, HD)
        copies.append(
            pltpu.make_async_copy(ref, out_ref.at[:, pl.ds(first, ref.shape[1])], done.at[at])
        )
    for copy in copies:
        copy.start()
    for copy in copies:
        copy.wait()


def join(pieces, spots, columns, partial):
    earlier = [] if partial is None else [partial]
    return pl.pallas_call(
        functools.partial(join_kernel, spots, len(pieces)),
        out_shape=jax.ShapeDtypeStruct((pieces[0].shape[0], columns), pieces[0].dtype),
        in_specs=[pl.BlockSpec(memory_space=pl.ANY)] * len(earlier)
        + [pl.BlockSpec(memory_space=pltpu.VMEM)] * len(pieces),
        out_specs=pl.BlockSpec(memory_space=pl.ANY),
        scratch_shapes=[pltpu.SemaphoreType.DMA((len(pieces),))],
        input_output_aliases={0: 0} if earlier else {},
        compiler_params=pltpu.CompilerParams(vmem_limit_bytes=8 << 20),
    )(*earlier, *pieces)


def put_together(kept, received):
    columns = kept[0].shape[1]
    pieces = kept + received
    spots = [(at >= len(kept), at % len(kept) * columns) for at in range(len(pieces))]
    out = join(pieces[:-1], spots[:-1], columns * len(pieces), None)
    return join(pieces[-1:], spots[-1:], columns * len(pieces), out)


def body(span_query, span_kv, prefix_cache, prefix_len, block_owner):
    seq_size = lax.axis_size("seq")
    head_size = lax.axis_size("head")
    group_size = seq_size // REQS
    tokens = span_kv.shape[0]
    page = prefix_cache.shape[1]
    groups = span_kv.shape[1] // (2 * HD)
    parts = 2 if groups % 2 == 0 else 1
    bits = [1 << at for at in range(1, group_size.bit_length() - 1)]
    orders = (bits, bits[::-1])

    stages = len(bits)

    def send(rows, stage):
        return hop(rows, tuple(order[stage] for order in orders))

    def swap_cores(pieces):
        return hop(pieces[0] if len(pieces) == 1 else jnp.concatenate(pieces, axis=0), (1, 1))

    def whole_layout(layout):
        for stage in range(stages):
            layout = layout + shifted(layout, 1 << stage)
        return layout

    span_layout = whole_layout([(0, SPAN_ROWS, tokens)])
    page_layout = whole_layout([(0, OWN_PAGE, page), (0, CROSSED_PAGE, page)])

    other_page, own_page = pick(prefix_cache, group_size)
    crossed = hop(other_page, (group_size, group_size))

    span_early = send(span_kv, stages - 1)
    span_forward = send(span_kv, 0)
    for stage in range(1, stages - 1):
        seen = jnp.concatenate([span_kv, span_forward], axis=0)
        span_forward = jnp.concatenate([span_forward, send(seen, stage)], axis=0)
    span_late = send(span_forward, stages - 1)
    spec = (tokens, page, group_size, head_size, orders)
    span_masks, page_masks = masks(prefix_len, block_owner, (span_layout, page_layout), spec)
    span_forward, span_masks, crossed = together(span_forward, span_masks, crossed)
    pages = [jnp.concatenate([own_page, crossed], axis=0)]
    pages.append(send(pages[0], 0))
    span_early, span_late = together(span_early, span_late)
    pages[1], span_late = together(pages[1], span_late)
    span = [jnp.concatenate([span_kv, span_forward, span_early, span_late], axis=0)]
    span_swapped = [swap_cores(span)]

    span_set = (span, span_swapped, span_masks)
    state = attend(span_query, 0, 1, [span_set], spec, None)

    for stage in range(1, stages):
        pages.append(send(jnp.concatenate(pages, axis=0), stage))
    pages[-1], state = together(pages[-1], state)
    columns = span_kv.shape[1] // parts
    results = []
    for part in range(parts):
        cut = slice(part * columns, (part + 1) * columns)
        theirs = swap_cores([piece[:, cut] for piece in pages])
        page_set = (pages, [theirs], page_masks)
        results.append(attend(span_query, part, parts, [span_set, page_set], spec, state))
    if head_size != 2:
        rows = jnp.concatenate([jnp.concatenate(pair, axis=0) for pair in results], axis=1)
        return lax.all_to_all(rows, "head", split_axis=0, concat_axis=1, tiled=True)
    kept = [pair[0] for pair in results]
    received = [lax.ppermute(pair[1], "head", [(0, 1), (1, 0)]) for pair in results]
    return put_together(kept, received)


def solution(mesh):
    placed = (P("seq", "head"), P("seq", "head"), P("seq", None, "head"), P(), P())
    return jax.shard_map(
        body, mesh=mesh, in_specs=placed, out_specs=P(("seq", "head"), None), check_vma=False
    )
```

```python
import functools
import math

import jax
import jax.numpy as jnp
from jax import lax
from jax.experimental import pallas as pl
from jax.experimental.pallas import tpu as pltpu
from jax.sharding import PartitionSpec as P

QH = 64
KVH = 8
HD = 128
REQS = 2
PER_GROUP = QH // KVH
EXP2_SCALE = HD ** (-0.5) * math.log2(math.e)
MASKED = -1e30
KEY_CHUNK = 256
HEADS_A_BLOCK = (2, 2, 2, 2)
SHIFT_STEP = 32.0
LOWEST_TOTAL = 1e-20
HIGHEST_TOTAL = 1e30
SPAN_ROWS, OWN_PAGE, CROSSED_PAGE = range(3)


def hop(value, bit_of_core):
    count = lax.axis_size("seq")
    return lax.ppermute(
        value, "seq", [(source, source ^ bit_of_core[source % 2]) for source in range(count)]
    )


def together(*values):
    return lax.optimization_barrier(values)


def shifted(layout, slots):
    return [(slot + slots, kind, rows) for slot, kind, rows in layout]


def hypercube_order(bits):
    order = [0]
    for bit in bits:
        order = order + [offset ^ bit for offset in order]
    return order


def mask_kernel(spec, layouts, limit_ref, owner_ref, *refs):
    tokens, page, group_size, _, orders = spec
    outs, page_seen = refs[:-1], refs[-1]
    me = lax.axis_index("seq")
    request = me // group_size
    offsets = [hypercube_order(order) for order in orders]

    def note_page(index, carry):
        page_seen[owner_ref[request, index]] = jnp.clip(limit_ref[request] - index * page, 0, page)
        return carry

    lax.fori_loop(0, owner_ref.shape[1], note_page, 0)
    for out, layout in zip(outs, layouts):
        start = 0
        for half in range(2):
            holder = me ^ half
            for slot, kind, rows in layout:
                source = holder ^ jnp.where(holder % 2 == 0, offsets[0][slot], offsets[1][slot])
                if kind == SPAN_ROWS:
                    count = jnp.where(source <= me, tokens, 0)
                elif kind == OWN_PAGE:
                    count = page_seen[source]
                else:
                    count = page_seen[source ^ group_size]
                row = lax.broadcasted_iota(jnp.int32, (rows, HD), 0)
                column = lax.broadcasted_iota(jnp.int32, (rows, HD), 1)
                mask = jnp.where(row < count, jnp.float32(0.0), jnp.float32(MASKED))
                one = jnp.where(column == 1, jnp.float32(1.0), jnp.float32(0.0))
                out[pl.ds(start, rows), :] = jnp.where(column == 0, mask, one).astype(jnp.bfloat16)
                start += rows


def masks(limits, owners, layouts, spec):
    scalars = pl.BlockSpec(memory_space=pltpu.SMEM)
    counts = [2 * sum(rows for _, _, rows in layout) for layout in layouts]
    return list(
        pl.pallas_call(
            functools.partial(mask_kernel, spec, layouts),
            out_shape=[jax.ShapeDtypeStruct((count, HD), jnp.bfloat16) for count in counts],
            in_specs=[scalars] * 2,
            out_specs=[pl.BlockSpec(memory_space=pltpu.VMEM)] * len(counts),
            scratch_shapes=[pltpu.SMEM((owners.shape[1],), jnp.int32)],
            compiler_params=pltpu.CompilerParams(vmem_limit_bytes=16 << 20),
        )(limits, owners)
    )


def attend_kernel(spec, sizes, part, groups, q_ref, *refs):
    tokens, _, _, head_size, _ = spec
    first_phase = len(sizes) == 1
    key_sets = []
    for counts in sizes:
        extra, refs = refs[0], refs[1:]
        halves = []
        for count in counts:
            halves.append(refs[:count])
            refs = refs[count:]
        key_sets.append((halves, extra))
    (state_sum, state_extra), refs = refs[:2], refs[2:]
    if first_phase:
        keys, values, weights = refs[0], refs[1], refs[2:4]
    else:
        outs, keys, values, weights = refs[:2], refs[2], refs[3], refs[4:6]
        slow_sum, slow_top = refs[6], refs[7]
    chunk = KEY_CHUNK
    my_head = lax.axis_index("head")

    def key_count(halves):
        return sum(ref.shape[0] for half in halves for ref in half)

    def fill(group, halves, extra):
        total_keys = key_count(halves)
        column = (part * groups + group) * 2 * HD
        start = 0
        for ref in [ref for half in halves for ref in half]:
            at = pl.ds(start, ref.shape[0])
            first = column % ref.shape[1]
            keys[group, at, :HD] = ref[:, pl.ds(first, HD)]
            values[group, at, :HD] = ref[:, pl.ds(first + HD, HD)]
            start += ref.shape[0]
        keys[group, :total_keys, HD:] = extra[...]
        values[group, :total_keys, HD:] = jnp.ones((total_keys, HD), jnp.bfloat16)

    def lane_of(heads):
        return lax.broadcasted_iota(jnp.int32, (heads * tokens, HD), 1)

    def query_rows(first, heads):
        at = part * groups * PER_GROUP + first
        columns = [pl.ds(pl.multiple_of((at + head) * HD, HD), HD) for head in range(heads)]
        return jnp.concatenate([q_ref[:, column] for column in columns], axis=0)

    def scores_of(query, group, start, is_span):
        made = lax.dot_general(
            query,
            keys[group, pl.ds(start, chunk), :],
            (((1,), (1,)), ((), ())),
            preferred_element_type=jnp.float32,
        )
        if start == 0 and is_span:
            rows = query.shape[0]
            causal = lax.broadcasted_iota(jnp.int32, (rows, tokens), 1) <= (
                lax.broadcasted_iota(jnp.int32, (rows, tokens), 0) % tokens
            )
            own = jnp.where(causal, made[:, :tokens], MASKED)
            made = jnp.concatenate([own, made[:, tokens:]], axis=1)
        return made

    def give(first, heads, result):
        kept = tokens // head_size
        for head in range(heads):
            column = pl.ds((first + head) * HD, HD)
            one = result[head * tokens : (head + 1) * tokens]
            if head_size == 2:
                low, high = one[:kept], one[kept:]
                outs[0][:, column] = jnp.where(my_head == 0, low, high)
                outs[1][:, column] = jnp.where(my_head == 0, high, low)
            else:
                outs[0][:, column] = one[:kept]
                outs[1][:, column] = one[kept:]

    halves, extra_ref = key_sets[-1]
    total_keys = key_count(halves)
    longest = [None] * groups

    def begin(group):
        fill(group, halves, extra_ref)
        if first_phase:
            key = keys[group, :total_keys, :HD].astype(jnp.float32)
            squares = jnp.sum(key * key, axis=1, keepdims=True)
            longest[group] = jnp.max(squares, axis=0, keepdims=True)

    def weigh(index):
        group, first, heads = blocks[index]
        rows = pl.ds(first * tokens, heads * tokens)
        query = query_rows(first, heads)
        if first_phase:
            wide = query.astype(jnp.float32)
            bound = jnp.sqrt(jnp.sum(wide * wide, axis=1, keepdims=True) * longest[group])
            shift = jnp.ceil(bound * (1.0 / SHIFT_STEP)) * SHIFT_STEP
            lane = lane_of(heads)
            extra = jnp.where(lane == 0, 1.0, jnp.where(lane == 1, -shift, 0.0))
            extra = extra.astype(jnp.bfloat16)
            state_extra[rows, :] = extra
        else:
            extra = state_extra[pl.ds((part * groups * PER_GROUP + first) * tokens, heads * tokens), :]
        query = jnp.concatenate([query, extra], axis=1)
        for start in range(0, total_keys, chunk):
            made = scores_of(query, group, start, first_phase)
            weights[index % 2][: heads * tokens, pl.ds(start, chunk)] = jnp.exp2(
                made * EXP2_SCALE
            ).astype(jnp.bfloat16)

    def finish(index, extremes):
        group, first, heads = blocks[index]
        summed = jnp.dot(
            weights[index % 2][: heads * tokens, :total_keys],
            values[group, :total_keys, :],
            preferred_element_type=jnp.float32,
        )
        if first_phase:
            state_sum[pl.ds(first * tokens, heads * tokens), :] = summed
            return extremes
        old = pl.ds((part * groups * PER_GROUP + first) * tokens, heads * tokens)
        summed = summed + state_sum[old, :]
        total = summed[:, HD:]
        give(first, heads, (summed[:, :HD] / total).astype(jnp.bfloat16))
        lowest, highest = extremes
        for head in range(heads):
            one = total[head * tokens : (head + 1) * tokens]
            lowest, highest = jnp.minimum(lowest, one), jnp.maximum(highest, one)
        return lowest, highest

    blocks = []
    for group in range(groups):
        at = group * PER_GROUP
        for heads in HEADS_A_BLOCK:
            blocks.append((group, at, heads))
            at += heads
    begin(0)
    extremes = (jnp.ones((tokens, HD), jnp.float32),) * 2
    for index in range(len(blocks) + 1):
        if index >= 1:
            extremes = finish(index - 1, extremes)
        if index < len(blocks):
            weigh(index)
            if index + 1 < len(blocks) and blocks[index + 1][0] != blocks[index][0]:
                begin(blocks[index + 1][0])
    if first_phase:
        return

    @pl.when((jnp.min(extremes[0]) < LOWEST_TOTAL) | (jnp.max(extremes[1]) > HIGHEST_TOTAL))
    def exact():
        heads = 4
        block = heads * tokens
        count = groups * PER_GROUP // heads
        for number, (halves, extra_ref) in enumerate(key_sets):
            for group in range(groups):
                fill(group, halves, extra_ref)

            def one_block(index, carry):
                group = index * heads // PER_GROUP
                extra = (lane_of(heads) == 0).astype(jnp.float32).astype(jnp.bfloat16)
                query = jnp.concatenate([query_rows(index * heads, heads), extra], axis=1)
                rows = pl.ds(pl.multiple_of(index * block, block), block)
                if number == 0:
                    top = jnp.full((block, HD), MASKED, jnp.float32)
                    summed = jnp.zeros((block, 2 * HD), jnp.float32)
                else:
                    top = slow_top[rows, :]
                    summed = slow_sum[rows, :]
                best = top
                for start in range(0, key_count(halves), chunk):
                    made = scores_of(query, group, start, number == 0)
                    for at in range(0, chunk, HD):
                        best = jnp.maximum(best, made[:, at : at + HD])
                best = jnp.broadcast_to(jnp.max(best, axis=1, keepdims=True), (block, HD))
                fade = jnp.exp2((top - best) * EXP2_SCALE)
                summed = summed * jnp.concatenate([fade, fade], axis=1)
                for start in range(0, key_count(halves), chunk):
                    made = scores_of(query, group, start, number == 0)
                    parts = [
                        jnp.exp2((made[:, at : at + HD] - best) * EXP2_SCALE)
                        for at in range(0, chunk, HD)
                    ]
                    summed = summed + jnp.dot(
                        jnp.concatenate(parts, axis=1).astype(jnp.bfloat16),
                        values[group, pl.ds(start, chunk), :],
                        preferred_element_type=jnp.float32,
                    )
                slow_top[rows, :] = best
                slow_sum[rows, :] = summed
                return carry

            lax.fori_loop(0, count, one_block, 0)
        for index in range(count):
            rows = pl.ds(index * block, block)
            result = (slow_sum[rows, :HD] / slow_sum[rows, HD:]).astype(jnp.bfloat16)
            give(index * heads, heads, result)


def attend(queries, part, parts, key_sets, spec, state):
    tokens, _, _, head_size = spec[:4]
    total_keys = max(extra.shape[0] for _, _, extra in key_sets)
    columns = queries.shape[1] // parts
    groups = columns // (PER_GROUP * HD)
    block = max(HEADS_A_BLOCK) * tokens
    rows = PER_GROUP * groups * tokens
    pieces = [piece for mine, theirs, extra in key_sets for piece in [extra] + mine + theirs]
    sizes = tuple((len(mine), len(theirs)) for mine, theirs, _ in key_sets)
    operands = queries.size * 2 + sum(piece.size for piece in pieces) * 2 + rows * HD * 12
    scratch = groups * total_keys * HD * 8 + block * total_keys * 4 + rows * HD * 12
    whole = pl.BlockSpec(memory_space=pltpu.VMEM)
    kept = tokens // head_size
    scratch_shapes = [pltpu.VMEM((groups, total_keys, 2 * HD), jnp.bfloat16)] * 2
    scratch_shapes += [pltpu.VMEM((block, total_keys), jnp.bfloat16)] * 2
    if state is None:
        state = ()
        out_shape = [
            jax.ShapeDtypeStruct((rows, 2 * HD), jnp.float32),
            jax.ShapeDtypeStruct((rows, HD), jnp.bfloat16),
        ]
    else:
        out_shape = [
            jax.ShapeDtypeStruct((kept, columns), jnp.bfloat16),
            jax.ShapeDtypeStruct((tokens - kept, columns), jnp.bfloat16),
        ]
        scratch_shapes += [
            pltpu.VMEM((rows, 2 * HD), jnp.float32),
            pltpu.VMEM((rows, HD), jnp.float32),
        ]
    return pl.pallas_call(
        functools.partial(attend_kernel, spec, sizes, part, groups),
        out_shape=out_shape,
        in_specs=[whole] * (1 + len(pieces) + len(state)),
        out_specs=[whole] * 2,
        scratch_shapes=scratch_shapes,
        compiler_params=pltpu.CompilerParams(vmem_limit_bytes=operands + scratch + (8 << 20)),
        cost_estimate=pl.CostEstimate(
            flops=8 * tokens * columns * total_keys,
            bytes_accessed=4 * tokens * columns + 2 * total_keys * columns // PER_GROUP,
            transcendentals=0,
        ),
    )(queries, *pieces, *state)


def pick_kernel(group_size, cache_ref, other_ref, own_ref):
    request = lax.axis_index("seq") // group_size
    other_ref[...] = cache_ref[1 - request]
    own_ref[...] = cache_ref[request]


def pick(cache, group_size):
    whole = pl.BlockSpec(memory_space=pltpu.VMEM)
    return pl.pallas_call(
        functools.partial(pick_kernel, group_size),
        out_shape=[jax.ShapeDtypeStruct(cache.shape[1:], cache.dtype)] * 2,
        in_specs=[whole],
        out_specs=[whole] * 2,
        compiler_params=pltpu.CompilerParams(vmem_limit_bytes=8 << 20),
    )(cache)


def join_kernel(spots, count, *refs):
    parts, (out_ref, done) = refs[len(refs) - 2 - count : -2], refs[-2:]
    side = out_ref.shape[1] // 2
    my_head = lax.axis_index("head")
    copies = []
    for at, (ref, (received, start)) in enumerate(zip(parts, spots)):
        owner = 1 - my_head if received else my_head
        first = pl.multiple_of(owner * side + start, HD)
        copies.append(
            pltpu.make_async_copy(ref, out_ref.at[:, pl.ds(first, ref.shape[1])], done.at[at])
        )
    for copy in copies:
        copy.start()
    for copy in copies:
        copy.wait()


def join(pieces, spots, columns, partial):
    earlier = [] if partial is None else [partial]
    return pl.pallas_call(
        functools.partial(join_kernel, spots, len(pieces)),
        out_shape=jax.ShapeDtypeStruct((pieces[0].shape[0], columns), pieces[0].dtype),
        in_specs=[pl.BlockSpec(memory_space=pl.ANY)] * len(earlier)
        + [pl.BlockSpec(memory_space=pltpu.VMEM)] * len(pieces),
        out_specs=pl.BlockSpec(memory_space=pl.ANY),
        scratch_shapes=[pltpu.SemaphoreType.DMA((len(pieces),))],
        input_output_aliases={0: 0} if earlier else {},
        compiler_params=pltpu.CompilerParams(vmem_limit_bytes=8 << 20),
    )(*earlier, *pieces)


def put_together(kept, received):
    columns = kept[0].shape[1]
    pieces = kept + received
    spots = [(at >= len(kept), at % len(kept) * columns) for at in range(len(pieces))]
    out = join(pieces[:-1], spots[:-1], columns * len(pieces), None)
    return join(pieces[-1:], spots[-1:], columns * len(pieces), out)


def body(span_query, span_kv, prefix_cache, prefix_len, block_owner):
    seq_size = lax.axis_size("seq")
    head_size = lax.axis_size("head")
    group_size = seq_size // REQS
    tokens = span_kv.shape[0]
    page = prefix_cache.shape[1]
    groups = span_kv.shape[1] // (2 * HD)
    parts = 2 if groups % 2 == 0 else 1
    bits = [1 << at for at in range(1, group_size.bit_length() - 1)]
    orders = (bits, bits[::-1])

    stages = len(bits)

    def send(rows, stage):
        return hop(rows, tuple(order[stage] for order in orders))

    def swap_cores(pieces):
        return hop(pieces[0] if len(pieces) == 1 else jnp.concatenate(pieces, axis=0), (1, 1))

    def whole_layout(layout):
        for stage in range(stages):
            layout = layout + shifted(layout, 1 << stage)
        return layout

    span_layout = whole_layout([(0, SPAN_ROWS, tokens)])
    page_layout = whole_layout([(0, OWN_PAGE, page), (0, CROSSED_PAGE, page)])

    other_page, own_page = pick(prefix_cache, group_size)
    crossed = hop(other_page, (group_size, group_size))

    span_early = send(span_kv, stages - 1)
    span_forward = send(span_kv, 0)
    for stage in range(1, stages - 1):
        seen = jnp.concatenate([span_kv, span_forward], axis=0)
        span_forward = jnp.concatenate([span_forward, send(seen, stage)], axis=0)
    span_late = send(span_forward, stages - 1)
    spec = (tokens, page, group_size, head_size, orders)
    span_masks, page_masks = masks(prefix_len, block_owner, (span_layout, page_layout), spec)
    span_forward, span_masks, crossed = together(span_forward, span_masks, crossed)
    pages = [jnp.concatenate([own_page, crossed], axis=0)]
    pages.append(send(pages[0], 0))
    span_early, span_late = together(span_early, span_late)
    pages[1], span_late = together(pages[1], span_late)
    span = [jnp.concatenate([span_kv, span_forward, span_early, span_late], axis=0)]
    span_swapped = [swap_cores(span)]

    span_set = (span, span_swapped, span_masks)
    state = attend(span_query, 0, 1, [span_set], spec, None)

    for stage in range(1, stages - 1):
        pages.append(send(jnp.concatenate(pages, axis=0), stage))
    columns = span_kv.shape[1] // parts
    cuts = [slice(part * columns, (part + 1) * columns) for part in range(parts)]
    held = [jnp.concatenate([piece[:, cut] for piece in pages], axis=0) for cut in cuts]
    arrived = [send(rows, stages - 1) for rows in held]
    results = []
    for part in range(parts):
        arrived[part], state = together(arrived[part], state)
        mine = [held[part], arrived[part]]
        page_set = (mine, [swap_cores(mine)], page_masks)
        results.append(attend(span_query, part, parts, [span_set, page_set], spec, state))
    if head_size != 2:
        rows = jnp.concatenate([jnp.concatenate(pair, axis=0) for pair in results], axis=1)
        return lax.all_to_all(rows, "head", split_axis=0, concat_axis=1, tiled=True)
    kept = [pair[0] for pair in results]
    received = [lax.ppermute(pair[1], "head", [(0, 1), (1, 0)]) for pair in results]
    return put_together(kept, received)


def solution(mesh):
    placed = (P("seq", "head"), P("seq", "head"), P("seq", None, "head"), P(), P())
    return jax.shard_map(
        body, mesh=mesh, in_specs=placed, out_specs=P(("seq", "head"), None), check_vma=False
    )
```

```python
import functools
import math

import jax
import jax.numpy as jnp
from jax import lax
from jax.experimental import pallas as pl
from jax.experimental.pallas import tpu as pltpu
from jax.sharding import PartitionSpec as P

QH = 64
KVH = 8
HD = 128
REQS = 2
PER_GROUP = QH // KVH
EXP2_SCALE = HD ** (-0.5) * math.log2(math.e)
MASKED = -1e30
KEY_CHUNK = 256
HEADS_A_BLOCK = (2, 2, 2, 2)
SHIFT_STEP = 32.0
LOWEST_TOTAL = 1e-20
HIGHEST_TOTAL = 1e30
SPAN_ROWS, OWN_PAGE, CROSSED_PAGE = range(3)


def hop(value, bit_of_core):
    count = lax.axis_size("seq")
    return lax.ppermute(
        value, "seq", [(source, source ^ bit_of_core[source % 2]) for source in range(count)]
    )


def together(*values):
    return lax.optimization_barrier(values)


def shifted(layout, slots):
    return [(slot + slots, kind, rows) for slot, kind, rows in layout]


def hypercube_order(bits):
    order = [0]
    for bit in bits:
        order = order + [offset ^ bit for offset in order]
    return order


def mask_kernel(spec, layouts, limit_ref, owner_ref, *refs):
    tokens, page, group_size, _, orders = spec
    outs, page_seen = refs[:-1], refs[-1]
    me = lax.axis_index("seq")
    request = me // group_size
    offsets = [hypercube_order(order) for order in orders]

    def note_page(index, carry):
        page_seen[owner_ref[request, index]] = jnp.clip(limit_ref[request] - index * page, 0, page)
        return carry

    lax.fori_loop(0, owner_ref.shape[1], note_page, 0)
    for out, layout in zip(outs, layouts):
        start = 0
        for half in range(2):
            holder = me ^ half
            for slot, kind, rows in layout:
                source = holder ^ jnp.where(holder % 2 == 0, offsets[0][slot], offsets[1][slot])
                if kind == SPAN_ROWS:
                    count = jnp.where(source <= me, tokens, 0)
                elif kind == OWN_PAGE:
                    count = page_seen[source]
                else:
                    count = page_seen[source ^ group_size]
                row = lax.broadcasted_iota(jnp.int32, (rows, HD), 0)
                column = lax.broadcasted_iota(jnp.int32, (rows, HD), 1)
                mask = jnp.where(row < count, jnp.float32(0.0), jnp.float32(MASKED))
                one = jnp.where(column == 1, jnp.float32(1.0), jnp.float32(0.0))
                out[pl.ds(start, rows), :] = jnp.where(column == 0, mask, one).astype(jnp.bfloat16)
                start += rows


def masks(limits, owners, layouts, spec):
    scalars = pl.BlockSpec(memory_space=pltpu.SMEM)
    counts = [2 * sum(rows for _, _, rows in layout) for layout in layouts]
    return list(
        pl.pallas_call(
            functools.partial(mask_kernel, spec, layouts),
            out_shape=[jax.ShapeDtypeStruct((count, HD), jnp.bfloat16) for count in counts],
            in_specs=[scalars] * 2,
            out_specs=[pl.BlockSpec(memory_space=pltpu.VMEM)] * len(counts),
            scratch_shapes=[pltpu.SMEM((owners.shape[1],), jnp.int32)],
            compiler_params=pltpu.CompilerParams(vmem_limit_bytes=16 << 20),
        )(limits, owners)
    )


def attend_kernel(spec, sizes, part, groups, q_ref, *refs):
    tokens, _, _, head_size, _ = spec
    first_phase = len(sizes) == 1
    key_sets = []
    for counts in sizes:
        extra, refs = refs[0], refs[1:]
        halves = []
        for count in counts:
            halves.append(refs[:count])
            refs = refs[count:]
        key_sets.append((halves, extra))
    (state_sum, state_extra), refs = refs[:2], refs[2:]
    if first_phase:
        keys, values, weights = refs[0], refs[1], refs[2:4]
    else:
        outs, keys, values, weights = refs[:2], refs[2], refs[3], refs[4:6]
        slow_sum, slow_top = refs[6], refs[7]
    chunk = KEY_CHUNK
    my_head = lax.axis_index("head")

    def key_count(halves):
        return sum(ref.shape[0] for half in halves for ref in half)

    def fill(group, halves, extra):
        total_keys = key_count(halves)
        column = (part * groups + group) * 2 * HD
        start = 0
        for ref in [ref for half in halves for ref in half]:
            at = pl.ds(start, ref.shape[0])
            first = column % ref.shape[1]
            keys[group, at, :HD] = ref[:, pl.ds(first, HD)]
            values[group, at, :HD] = ref[:, pl.ds(first + HD, HD)]
            start += ref.shape[0]
        keys[group, :total_keys, HD:] = extra[...]
        values[group, :total_keys, HD:] = jnp.ones((total_keys, HD), jnp.bfloat16)

    def lane_of(heads):
        return lax.broadcasted_iota(jnp.int32, (heads * tokens, HD), 1)

    def query_rows(first, heads):
        at = part * groups * PER_GROUP + first
        columns = [pl.ds(pl.multiple_of((at + head) * HD, HD), HD) for head in range(heads)]
        return jnp.concatenate([q_ref[:, column] for column in columns], axis=0)

    def scores_of(query, group, start, is_span):
        made = lax.dot_general(
            query,
            keys[group, pl.ds(start, chunk), :],
            (((1,), (1,)), ((), ())),
            preferred_element_type=jnp.float32,
        )
        if start == 0 and is_span:
            rows = query.shape[0]
            causal = lax.broadcasted_iota(jnp.int32, (rows, tokens), 1) <= (
                lax.broadcasted_iota(jnp.int32, (rows, tokens), 0) % tokens
            )
            own = jnp.where(causal, made[:, :tokens], MASKED)
            made = jnp.concatenate([own, made[:, tokens:]], axis=1)
        return made

    def give(first, heads, result):
        kept = tokens // head_size
        for head in range(heads):
            column = pl.ds((first + head) * HD, HD)
            one = result[head * tokens : (head + 1) * tokens]
            if head_size == 2:
                low, high = one[:kept], one[kept:]
                outs[0][:, column] = jnp.where(my_head == 0, low, high)
                outs[1][:, column] = jnp.where(my_head == 0, high, low)
            else:
                outs[0][:, column] = one[:kept]
                outs[1][:, column] = one[kept:]

    halves, extra_ref = key_sets[-1]
    total_keys = key_count(halves)
    longest = [None] * groups

    def begin(group):
        fill(group, halves, extra_ref)
        if first_phase:
            key = keys[group, :total_keys, :HD].astype(jnp.float32)
            squares = jnp.sum(key * key, axis=1, keepdims=True)
            longest[group] = jnp.max(squares, axis=0, keepdims=True)

    def weigh(index):
        group, first, heads = blocks[index]
        rows = pl.ds(first * tokens, heads * tokens)
        query = query_rows(first, heads)
        if first_phase:
            wide = query.astype(jnp.float32)
            bound = jnp.sqrt(jnp.sum(wide * wide, axis=1, keepdims=True) * longest[group])
            shift = jnp.ceil(bound * (1.0 / SHIFT_STEP)) * SHIFT_STEP
            lane = lane_of(heads)
            extra = jnp.where(lane == 0, 1.0, jnp.where(lane == 1, -shift, 0.0))
            extra = extra.astype(jnp.bfloat16)
            state_extra[rows, :] = extra
        else:
            extra = state_extra[rows, :]
        query = jnp.concatenate([query, extra], axis=1)
        for start in range(0, total_keys, chunk):
            made = scores_of(query, group, start, first_phase)
            weights[index % 2][: heads * tokens, pl.ds(start, chunk)] = jnp.exp2(
                made * EXP2_SCALE
            ).astype(jnp.bfloat16)

    def finish(index, extremes):
        group, first, heads = blocks[index]
        summed = jnp.dot(
            weights[index % 2][: heads * tokens, :total_keys],
            values[group, :total_keys, :],
            preferred_element_type=jnp.float32,
        )
        if first_phase:
            state_sum[pl.ds(first * tokens, heads * tokens), :] = summed
            return extremes
        old = pl.ds(first * tokens, heads * tokens)
        summed = summed + state_sum[old, :]
        total = summed[:, HD:]
        give(first, heads, (summed[:, :HD] / total).astype(jnp.bfloat16))
        lowest, highest = extremes
        for head in range(heads):
            one = total[head * tokens : (head + 1) * tokens]
            lowest, highest = jnp.minimum(lowest, one), jnp.maximum(highest, one)
        return lowest, highest

    blocks = []
    for group in range(groups):
        at = group * PER_GROUP
        for heads in HEADS_A_BLOCK:
            blocks.append((group, at, heads))
            at += heads
    begin(0)
    extremes = (jnp.ones((tokens, HD), jnp.float32),) * 2
    for index in range(len(blocks) + 1):
        if index >= 1:
            extremes = finish(index - 1, extremes)
        if index < len(blocks):
            weigh(index)
            if index + 1 < len(blocks) and blocks[index + 1][0] != blocks[index][0]:
                begin(blocks[index + 1][0])
    if first_phase:
        return

    @pl.when((jnp.min(extremes[0]) < LOWEST_TOTAL) | (jnp.max(extremes[1]) > HIGHEST_TOTAL))
    def exact():
        heads = 4
        block = heads * tokens
        count = groups * PER_GROUP // heads
        for number, (halves, extra_ref) in enumerate(key_sets):
            for group in range(groups):
                fill(group, halves, extra_ref)

            def one_block(index, carry):
                group = index * heads // PER_GROUP
                extra = (lane_of(heads) == 0).astype(jnp.float32).astype(jnp.bfloat16)
                query = jnp.concatenate([query_rows(index * heads, heads), extra], axis=1)
                rows = pl.ds(pl.multiple_of(index * block, block), block)
                if number == 0:
                    top = jnp.full((block, HD), MASKED, jnp.float32)
                    summed = jnp.zeros((block, 2 * HD), jnp.float32)
                else:
                    top = slow_top[rows, :]
                    summed = slow_sum[rows, :]
                best = top
                for start in range(0, key_count(halves), chunk):
                    made = scores_of(query, group, start, number == 0)
                    for at in range(0, chunk, HD):
                        best = jnp.maximum(best, made[:, at : at + HD])
                best = jnp.broadcast_to(jnp.max(best, axis=1, keepdims=True), (block, HD))
                fade = jnp.exp2((top - best) * EXP2_SCALE)
                summed = summed * jnp.concatenate([fade, fade], axis=1)
                for start in range(0, key_count(halves), chunk):
                    made = scores_of(query, group, start, number == 0)
                    parts = [
                        jnp.exp2((made[:, at : at + HD] - best) * EXP2_SCALE)
                        for at in range(0, chunk, HD)
                    ]
                    summed = summed + jnp.dot(
                        jnp.concatenate(parts, axis=1).astype(jnp.bfloat16),
                        values[group, pl.ds(start, chunk), :],
                        preferred_element_type=jnp.float32,
                    )
                slow_top[rows, :] = best
                slow_sum[rows, :] = summed
                return carry

            lax.fori_loop(0, count, one_block, 0)
        for index in range(count):
            rows = pl.ds(index * block, block)
            result = (slow_sum[rows, :HD] / slow_sum[rows, HD:]).astype(jnp.bfloat16)
            give(index * heads, heads, result)


def attend(queries, part, parts, key_sets, spec, state):
    tokens, _, _, head_size = spec[:4]
    total_keys = max(extra.shape[0] for _, _, extra in key_sets)
    columns = queries.shape[1] // parts
    groups = columns // (PER_GROUP * HD)
    block = max(HEADS_A_BLOCK) * tokens
    rows = PER_GROUP * groups * tokens
    pieces = [piece for mine, theirs, extra in key_sets for piece in [extra] + mine + theirs]
    sizes = tuple((len(mine), len(theirs)) for mine, theirs, _ in key_sets)
    operands = queries.size * 2 + sum(piece.size for piece in pieces) * 2 + rows * HD * 12
    scratch = groups * total_keys * HD * 8 + block * total_keys * 4 + rows * HD * 12
    whole = pl.BlockSpec(memory_space=pltpu.VMEM)
    kept = tokens // head_size
    scratch_shapes = [pltpu.VMEM((groups, total_keys, 2 * HD), jnp.bfloat16)] * 2
    scratch_shapes += [pltpu.VMEM((block, total_keys), jnp.bfloat16)] * 2
    if state is None:
        state = ()
        out_shape = [
            jax.ShapeDtypeStruct((rows, 2 * HD), jnp.float32),
            jax.ShapeDtypeStruct((rows, HD), jnp.bfloat16),
        ]
    else:
        out_shape = [
            jax.ShapeDtypeStruct((kept, columns), jnp.bfloat16),
            jax.ShapeDtypeStruct((tokens - kept, columns), jnp.bfloat16),
        ]
        scratch_shapes += [
            pltpu.VMEM((rows, 2 * HD), jnp.float32),
            pltpu.VMEM((rows, HD), jnp.float32),
        ]
    return pl.pallas_call(
        functools.partial(attend_kernel, spec, sizes, part, groups),
        out_shape=out_shape,
        in_specs=[whole] * (1 + len(pieces) + len(state)),
        out_specs=[whole] * 2,
        scratch_shapes=scratch_shapes,
        compiler_params=pltpu.CompilerParams(vmem_limit_bytes=operands + scratch + (8 << 20)),
        cost_estimate=pl.CostEstimate(
            flops=8 * tokens * columns * total_keys,
            bytes_accessed=4 * tokens * columns + 2 * total_keys * columns // PER_GROUP,
            transcendentals=0,
        ),
    )(queries, *pieces, *state)


def pick_kernel(group_size, cache_ref, other_ref, own_ref):
    request = lax.axis_index("seq") // group_size
    other_ref[...] = cache_ref[1 - request]
    own_ref[...] = cache_ref[request]


def pick(cache, group_size):
    whole = pl.BlockSpec(memory_space=pltpu.VMEM)
    return pl.pallas_call(
        functools.partial(pick_kernel, group_size),
        out_shape=[jax.ShapeDtypeStruct(cache.shape[1:], cache.dtype)] * 2,
        in_specs=[whole],
        out_specs=[whole] * 2,
        compiler_params=pltpu.CompilerParams(vmem_limit_bytes=8 << 20),
    )(cache)


def join_kernel(spots, count, *refs):
    parts, (out_ref, done) = refs[len(refs) - 2 - count : -2], refs[-2:]
    side = out_ref.shape[1] // 2
    my_head = lax.axis_index("head")
    copies = []
    for at, (ref, (received, start)) in enumerate(zip(parts, spots)):
        owner = 1 - my_head if received else my_head
        first = pl.multiple_of(owner * side + start, HD)
        copies.append(
            pltpu.make_async_copy(ref, out_ref.at[:, pl.ds(first, ref.shape[1])], done.at[at])
        )
    for copy in copies:
        copy.start()
    for copy in copies:
        copy.wait()


def join(pieces, spots, columns, partial):
    earlier = [] if partial is None else [partial]
    return pl.pallas_call(
        functools.partial(join_kernel, spots, len(pieces)),
        out_shape=jax.ShapeDtypeStruct((pieces[0].shape[0], columns), pieces[0].dtype),
        in_specs=[pl.BlockSpec(memory_space=pl.ANY)] * len(earlier)
        + [pl.BlockSpec(memory_space=pltpu.VMEM)] * len(pieces),
        out_specs=pl.BlockSpec(memory_space=pl.ANY),
        scratch_shapes=[pltpu.SemaphoreType.DMA((len(pieces),))],
        input_output_aliases={0: 0} if earlier else {},
        compiler_params=pltpu.CompilerParams(vmem_limit_bytes=8 << 20),
    )(*earlier, *pieces)


def put_together(kept, received):
    columns = kept[0].shape[1]
    pieces = kept + received
    spots = [(at >= len(kept), at % len(kept) * columns) for at in range(len(pieces))]
    out = join(pieces[:-1], spots[:-1], columns * len(pieces), None)
    return join(pieces[-1:], spots[-1:], columns * len(pieces), out)


def body(span_query, span_kv, prefix_cache, prefix_len, block_owner):
    seq_size = lax.axis_size("seq")
    head_size = lax.axis_size("head")
    group_size = seq_size // REQS
    tokens = span_kv.shape[0]
    page = prefix_cache.shape[1]
    groups = span_kv.shape[1] // (2 * HD)
    parts = 2 if groups % 2 == 0 else 1
    bits = [1 << at for at in range(1, group_size.bit_length() - 1)]
    orders = (bits, bits[::-1])

    stages = len(bits)

    def send(rows, stage):
        return hop(rows, tuple(order[stage] for order in orders))

    def swap_cores(pieces):
        return hop(pieces[0] if len(pieces) == 1 else jnp.concatenate(pieces, axis=0), (1, 1))

    def whole_layout(layout):
        for stage in range(stages):
            layout = layout + shifted(layout, 1 << stage)
        return layout

    span_layout = whole_layout([(0, SPAN_ROWS, tokens)])
    page_layout = whole_layout([(0, OWN_PAGE, page), (0, CROSSED_PAGE, page)])

    other_page, own_page = pick(prefix_cache, group_size)
    crossed = hop(other_page, (group_size, group_size))

    span_early = send(span_kv, stages - 1)
    span_forward = send(span_kv, 0)
    for stage in range(1, stages - 1):
        seen = jnp.concatenate([span_kv, span_forward], axis=0)
        span_forward = jnp.concatenate([span_forward, send(seen, stage)], axis=0)
    span_late = send(span_forward, stages - 1)
    spec = (tokens, page, group_size, head_size, orders)
    span_masks, page_masks = masks(prefix_len, block_owner, (span_layout, page_layout), spec)
    span_forward, span_masks, crossed = together(span_forward, span_masks, crossed)
    pages = [jnp.concatenate([own_page, crossed], axis=0)]
    pages.append(send(pages[0], 0))
    span_early, span_late = together(span_early, span_late)
    pages[1], span_late = together(pages[1], span_late)
    span = [jnp.concatenate([span_kv, span_forward, span_early, span_late], axis=0)]
    span_swapped = [swap_cores(span)]

    span_set = (span, span_swapped, span_masks)
    states = [attend(span_query, part, parts, [span_set], spec, None) for part in range(parts)]

    for stage in range(1, stages - 1):
        pages.append(send(jnp.concatenate(pages, axis=0), stage))
    columns = span_kv.shape[1] // parts
    cuts = [slice(part * columns, (part + 1) * columns) for part in range(parts)]
    held = [jnp.concatenate([piece[:, cut] for piece in pages], axis=0) for cut in cuts]
    arrived = [send(rows, stages - 1) for rows in held]
    results = []
    for part in range(parts):
        arrived[part], state = together(arrived[part], states[part])
        mine = [held[part], arrived[part]]
        page_set = (mine, [swap_cores(mine)], page_masks)
        results.append(attend(span_query, part, parts, [span_set, page_set], spec, state))
    if head_size != 2:
        rows = jnp.concatenate([jnp.concatenate(pair, axis=0) for pair in results], axis=1)
        return lax.all_to_all(rows, "head", split_axis=0, concat_axis=1, tiled=True)
    kept = [pair[0] for pair in results]
    received = [lax.ppermute(pair[1], "head", [(0, 1), (1, 0)]) for pair in results]
    return put_together(kept, received)


def solution(mesh):
    placed = (P("seq", "head"), P("seq", "head"), P("seq", None, "head"), P(), P())
    return jax.shard_map(
        body, mesh=mesh, in_specs=placed, out_specs=P(("seq", "head"), None), check_vma=False
    )
```

```python
import functools
import math

import jax
import jax.numpy as jnp
from jax import lax
from jax.experimental import pallas as pl
from jax.experimental.pallas import tpu as pltpu
from jax.sharding import PartitionSpec as P

QH = 64
KVH = 8
HD = 128
REQS = 2
PER_GROUP = QH // KVH
EXP2_SCALE = HD ** (-0.5) * math.log2(math.e)
MASKED = -1e30
KEY_CHUNK = 512
HEADS_A_BLOCK = (2, 2, 2, 2)
SHIFT_STEP = 32.0
LOWEST_TOTAL = 1e-20
HIGHEST_TOTAL = 1e30
SPAN_ROWS, OWN_PAGE, CROSSED_PAGE = range(3)


def hop(value, bit_of_core):
    count = lax.axis_size("seq")
    return lax.ppermute(
        value, "seq", [(source, source ^ bit_of_core[source % 2]) for source in range(count)]
    )


def together(*values):
    return lax.optimization_barrier(values)


def shifted(layout, slots):
    return [(slot + slots, kind, rows) for slot, kind, rows in layout]


def hypercube_order(bits):
    order = [0]
    for bit in bits:
        order = order + [offset ^ bit for offset in order]
    return order


def mask_kernel(spec, layouts, limit_ref, owner_ref, *refs):
    tokens, page, group_size, _, orders = spec
    outs, page_seen = refs[:-1], refs[-1]
    me = lax.axis_index("seq")
    request = me // group_size
    offsets = [hypercube_order(order) for order in orders]

    def note_page(index, carry):
        page_seen[owner_ref[request, index]] = jnp.clip(limit_ref[request] - index * page, 0, page)
        return carry

    lax.fori_loop(0, owner_ref.shape[1], note_page, 0)
    for out, layout in zip(outs, layouts):
        start = 0
        for half in range(2):
            holder = me ^ half
            for slot, kind, rows in layout:
                source = holder ^ jnp.where(holder % 2 == 0, offsets[0][slot], offsets[1][slot])
                if kind == SPAN_ROWS:
                    count = jnp.where(source <= me, tokens, 0)
                elif kind == OWN_PAGE:
                    count = page_seen[source]
                else:
                    count = page_seen[source ^ group_size]
                row = lax.broadcasted_iota(jnp.int32, (rows, HD), 0)
                column = lax.broadcasted_iota(jnp.int32, (rows, HD), 1)
                mask = jnp.where(row < count, jnp.float32(0.0), jnp.float32(MASKED))
                one = jnp.where(column == 1, jnp.float32(1.0), jnp.float32(0.0))
                out[pl.ds(start, rows), :] = jnp.where(column == 0, mask, one).astype(jnp.bfloat16)
                start += rows


def masks(limits, owners, layouts, spec):
    scalars = pl.BlockSpec(memory_space=pltpu.SMEM)
    counts = [2 * sum(rows for _, _, rows in layout) for layout in layouts]
    return list(
        pl.pallas_call(
            functools.partial(mask_kernel, spec, layouts),
            out_shape=[jax.ShapeDtypeStruct((count, HD), jnp.bfloat16) for count in counts],
            in_specs=[scalars] * 2,
            out_specs=[pl.BlockSpec(memory_space=pltpu.VMEM)] * len(counts),
            scratch_shapes=[pltpu.SMEM((owners.shape[1],), jnp.int32)],
            compiler_params=pltpu.CompilerParams(vmem_limit_bytes=16 << 20),
        )(limits, owners)
    )


def attend_kernel(spec, sizes, part, groups, q_ref, *refs):
    tokens, _, _, head_size, _ = spec
    first_phase = len(sizes) == 1
    key_sets = []
    for counts in sizes:
        extra, refs = refs[0], refs[1:]
        halves = []
        for count in counts:
            halves.append(refs[:count])
            refs = refs[count:]
        key_sets.append((halves, extra))
    (state_sum, state_extra), refs = refs[:2], refs[2:]
    if first_phase:
        keys, values, weights = refs[0], refs[1], refs[2:4]
    else:
        outs, keys, values, weights = refs[:2], refs[2], refs[3], refs[4:6]
        slow_sum, slow_top = refs[6], refs[7]
    chunk = KEY_CHUNK
    my_head = lax.axis_index("head")

    def key_count(halves):
        return sum(ref.shape[0] for half in halves for ref in half)

    def fill(group, halves, extra):
        total_keys = key_count(halves)
        column = (part * groups + group) * 2 * HD
        start = 0
        for ref in [ref for half in halves for ref in half]:
            at = pl.ds(start, ref.shape[0])
            first = column % ref.shape[1]
            keys[group, at, :HD] = ref[:, pl.ds(first, HD)]
            values[group, at, :HD] = ref[:, pl.ds(first + HD, HD)]
            start += ref.shape[0]
        keys[group, :total_keys, HD:] = extra[...]
        values[group, :total_keys, HD:] = jnp.ones((total_keys, HD), jnp.bfloat16)

    def lane_of(heads):
        return lax.broadcasted_iota(jnp.int32, (heads * tokens, HD), 1)

    def query_rows(first, heads):
        at = part * groups * PER_GROUP + first
        columns = [pl.ds(pl.multiple_of((at + head) * HD, HD), HD) for head in range(heads)]
        return jnp.concatenate([q_ref[:, column] for column in columns], axis=0)

    def scores_of(query, group, start, is_span):
        made = lax.dot_general(
            query,
            keys[group, pl.ds(start, chunk), :],
            (((1,), (1,)), ((), ())),
            preferred_element_type=jnp.float32,
        )
        if start == 0 and is_span:
            rows = query.shape[0]
            causal = lax.broadcasted_iota(jnp.int32, (rows, tokens), 1) <= (
                lax.broadcasted_iota(jnp.int32, (rows, tokens), 0) % tokens
            )
            own = jnp.where(causal, made[:, :tokens], MASKED)
            made = jnp.concatenate([own, made[:, tokens:]], axis=1)
        return made

    def give(first, heads, result):
        kept = tokens // head_size
        for head in range(heads):
            column = pl.ds((first + head) * HD, HD)
            one = result[head * tokens : (head + 1) * tokens]
            if head_size == 2:
                low, high = one[:kept], one[kept:]
                outs[0][:, column] = jnp.where(my_head == 0, low, high)
                outs[1][:, column] = jnp.where(my_head == 0, high, low)
            else:
                outs[0][:, column] = one[:kept]
                outs[1][:, column] = one[kept:]

    halves, extra_ref = key_sets[-1]
    total_keys = key_count(halves)
    longest = [None] * groups

    def begin(group):
        fill(group, halves, extra_ref)
        if first_phase:
            key = keys[group, :total_keys, :HD].astype(jnp.float32)
            squares = jnp.sum(key * key, axis=1, keepdims=True)
            longest[group] = jnp.max(squares, axis=0, keepdims=True)

    def weigh(index):
        group, first, heads = blocks[index]
        rows = pl.ds(first * tokens, heads * tokens)
        query = query_rows(first, heads)
        if first_phase:
            wide = query.astype(jnp.float32)
            bound = jnp.sqrt(jnp.sum(wide * wide, axis=1, keepdims=True) * longest[group])
            shift = jnp.ceil(bound * (1.0 / SHIFT_STEP)) * SHIFT_STEP
            lane = lane_of(heads)
            extra = jnp.where(lane == 0, 1.0, jnp.where(lane == 1, -shift, 0.0))
            extra = extra.astype(jnp.bfloat16)
            state_extra[rows, :] = extra
        else:
            extra = state_extra[pl.ds((part * groups * PER_GROUP + first) * tokens, heads * tokens), :]
        query = jnp.concatenate([query, extra], axis=1)
        for start in range(0, total_keys, chunk):
            made = scores_of(query, group, start, first_phase)
            weights[index % 2][: heads * tokens, pl.ds(start, chunk)] = jnp.exp2(
                made * EXP2_SCALE
            ).astype(jnp.bfloat16)

    def finish(index, extremes):
        group, first, heads = blocks[index]
        summed = jnp.dot(
            weights[index % 2][: heads * tokens, :total_keys],
            values[group, :total_keys, :],
            preferred_element_type=jnp.float32,
        )
        if first_phase:
            state_sum[pl.ds(first * tokens, heads * tokens), :] = summed
            return extremes
        old = pl.ds((part * groups * PER_GROUP + first) * tokens, heads * tokens)
        summed = summed + state_sum[old, :]
        total = summed[:, HD:]
        give(first, heads, (summed[:, :HD] / total).astype(jnp.bfloat16))
        lowest, highest = extremes
        for head in range(heads):
            one = total[head * tokens : (head + 1) * tokens]
            lowest, highest = jnp.minimum(lowest, one), jnp.maximum(highest, one)
        return lowest, highest

    blocks = []
    for group in range(groups):
        at = group * PER_GROUP
        for heads in HEADS_A_BLOCK:
            blocks.append((group, at, heads))
            at += heads
    begin(0)
    extremes = (jnp.ones((tokens, HD), jnp.float32),) * 2
    for index in range(len(blocks) + 1):
        if index >= 1:
            extremes = finish(index - 1, extremes)
        if index < len(blocks):
            weigh(index)
            if index + 1 < len(blocks) and blocks[index + 1][0] != blocks[index][0]:
                begin(blocks[index + 1][0])
    if first_phase:
        return

    @pl.when((jnp.min(extremes[0]) < LOWEST_TOTAL) | (jnp.max(extremes[1]) > HIGHEST_TOTAL))
    def exact():
        heads = 4
        block = heads * tokens
        count = groups * PER_GROUP // heads
        for number, (halves, extra_ref) in enumerate(key_sets):
            for group in range(groups):
                fill(group, halves, extra_ref)

            def one_block(index, carry):
                group = index * heads // PER_GROUP
                extra = (lane_of(heads) == 0).astype(jnp.float32).astype(jnp.bfloat16)
                query = jnp.concatenate([query_rows(index * heads, heads), extra], axis=1)
                rows = pl.ds(pl.multiple_of(index * block, block), block)
                if number == 0:
                    top = jnp.full((block, HD), MASKED, jnp.float32)
                    summed = jnp.zeros((block, 2 * HD), jnp.float32)
                else:
                    top = slow_top[rows, :]
                    summed = slow_sum[rows, :]
                best = top
                for start in range(0, key_count(halves), chunk):
                    made = scores_of(query, group, start, number == 0)
                    for at in range(0, chunk, HD):
                        best = jnp.maximum(best, made[:, at : at + HD])
                best = jnp.broadcast_to(jnp.max(best, axis=1, keepdims=True), (block, HD))
                fade = jnp.exp2((top - best) * EXP2_SCALE)
                summed = summed * jnp.concatenate([fade, fade], axis=1)
                for start in range(0, key_count(halves), chunk):
                    made = scores_of(query, group, start, number == 0)
                    parts = [
                        jnp.exp2((made[:, at : at + HD] - best) * EXP2_SCALE)
                        for at in range(0, chunk, HD)
                    ]
                    summed = summed + jnp.dot(
                        jnp.concatenate(parts, axis=1).astype(jnp.bfloat16),
                        values[group, pl.ds(start, chunk), :],
                        preferred_element_type=jnp.float32,
                    )
                slow_top[rows, :] = best
                slow_sum[rows, :] = summed
                return carry

            lax.fori_loop(0, count, one_block, 0)
        for index in range(count):
            rows = pl.ds(index * block, block)
            result = (slow_sum[rows, :HD] / slow_sum[rows, HD:]).astype(jnp.bfloat16)
            give(index * heads, heads, result)


def attend(queries, part, parts, key_sets, spec, state):
    tokens, _, _, head_size = spec[:4]
    total_keys = max(extra.shape[0] for _, _, extra in key_sets)
    columns = queries.shape[1] // parts
    groups = columns // (PER_GROUP * HD)
    block = max(HEADS_A_BLOCK) * tokens
    rows = PER_GROUP * groups * tokens
    pieces = [piece for mine, theirs, extra in key_sets for piece in [extra] + mine + theirs]
    sizes = tuple((len(mine), len(theirs)) for mine, theirs, _ in key_sets)
    operands = queries.size * 2 + sum(piece.size for piece in pieces) * 2 + rows * HD * 12
    scratch = groups * total_keys * HD * 8 + block * total_keys * 4 + rows * HD * 12
    whole = pl.BlockSpec(memory_space=pltpu.VMEM)
    kept = tokens // head_size
    scratch_shapes = [pltpu.VMEM((groups, total_keys, 2 * HD), jnp.bfloat16)] * 2
    scratch_shapes += [pltpu.VMEM((block, total_keys), jnp.bfloat16)] * 2
    if state is None:
        state = ()
        out_shape = [
            jax.ShapeDtypeStruct((rows, 2 * HD), jnp.float32),
            jax.ShapeDtypeStruct((rows, HD), jnp.bfloat16),
        ]
    else:
        out_shape = [
            jax.ShapeDtypeStruct((kept, columns), jnp.bfloat16),
            jax.ShapeDtypeStruct((tokens - kept, columns), jnp.bfloat16),
        ]
        scratch_shapes += [
            pltpu.VMEM((rows, 2 * HD), jnp.float32),
            pltpu.VMEM((rows, HD), jnp.float32),
        ]
    return pl.pallas_call(
        functools.partial(attend_kernel, spec, sizes, part, groups),
        out_shape=out_shape,
        in_specs=[whole] * (1 + len(pieces) + len(state)),
        out_specs=[whole] * 2,
        scratch_shapes=scratch_shapes,
        compiler_params=pltpu.CompilerParams(vmem_limit_bytes=operands + scratch + (8 << 20)),
        cost_estimate=pl.CostEstimate(
            flops=8 * tokens * columns * total_keys,
            bytes_accessed=4 * tokens * columns + 2 * total_keys * columns // PER_GROUP,
            transcendentals=0,
        ),
    )(queries, *pieces, *state)


def pick_kernel(group_size, cache_ref, other_ref, own_ref):
    request = lax.axis_index("seq") // group_size
    other_ref[...] = cache_ref[1 - request]
    own_ref[...] = cache_ref[request]


def pick(cache, group_size):
    whole = pl.BlockSpec(memory_space=pltpu.VMEM)
    return pl.pallas_call(
        functools.partial(pick_kernel, group_size),
        out_shape=[jax.ShapeDtypeStruct(cache.shape[1:], cache.dtype)] * 2,
        in_specs=[whole],
        out_specs=[whole] * 2,
        compiler_params=pltpu.CompilerParams(vmem_limit_bytes=8 << 20),
    )(cache)


def join_kernel(spots, count, *refs):
    parts, (out_ref, done) = refs[len(refs) - 2 - count : -2], refs[-2:]
    side = out_ref.shape[1] // 2
    my_head = lax.axis_index("head")
    copies = []
    for at, (ref, (received, start)) in enumerate(zip(parts, spots)):
        owner = 1 - my_head if received else my_head
        first = pl.multiple_of(owner * side + start, HD)
        copies.append(
            pltpu.make_async_copy(ref, out_ref.at[:, pl.ds(first, ref.shape[1])], done.at[at])
        )
    for copy in copies:
        copy.start()
    for copy in copies:
        copy.wait()


def join(pieces, spots, columns, partial):
    earlier = [] if partial is None else [partial]
    return pl.pallas_call(
        functools.partial(join_kernel, spots, len(pieces)),
        out_shape=jax.ShapeDtypeStruct((pieces[0].shape[0], columns), pieces[0].dtype),
        in_specs=[pl.BlockSpec(memory_space=pl.ANY)] * len(earlier)
        + [pl.BlockSpec(memory_space=pltpu.VMEM)] * len(pieces),
        out_specs=pl.BlockSpec(memory_space=pl.ANY),
        scratch_shapes=[pltpu.SemaphoreType.DMA((len(pieces),))],
        input_output_aliases={0: 0} if earlier else {},
        compiler_params=pltpu.CompilerParams(vmem_limit_bytes=8 << 20),
    )(*earlier, *pieces)


def put_together(kept, received):
    columns = kept[0].shape[1]
    pieces = kept + received
    spots = [(at >= len(kept), at % len(kept) * columns) for at in range(len(pieces))]
    out = join(pieces[:-1], spots[:-1], columns * len(pieces), None)
    return join(pieces[-1:], spots[-1:], columns * len(pieces), out)


def body(span_query, span_kv, prefix_cache, prefix_len, block_owner):
    seq_size = lax.axis_size("seq")
    head_size = lax.axis_size("head")
    group_size = seq_size // REQS
    tokens = span_kv.shape[0]
    page = prefix_cache.shape[1]
    groups = span_kv.shape[1] // (2 * HD)
    parts = 2 if groups % 2 == 0 else 1
    bits = [1 << at for at in range(1, group_size.bit_length() - 1)]
    orders = (bits, bits[::-1])

    stages = len(bits)

    def send(rows, stage):
        return hop(rows, tuple(order[stage] for order in orders))

    def swap_cores(pieces):
        return hop(pieces[0] if len(pieces) == 1 else jnp.concatenate(pieces, axis=0), (1, 1))

    def whole_layout(layout):
        for stage in range(stages):
            layout = layout + shifted(layout, 1 << stage)
        return layout

    span_layout = whole_layout([(0, SPAN_ROWS, tokens)])
    page_layout = whole_layout([(0, OWN_PAGE, page), (0, CROSSED_PAGE, page)])

    other_page, own_page = pick(prefix_cache, group_size)
    crossed = hop(other_page, (group_size, group_size))

    span_early = send(span_kv, stages - 1)
    span_forward = send(span_kv, 0)
    for stage in range(1, stages - 1):
        seen = jnp.concatenate([span_kv, span_forward], axis=0)
        span_forward = jnp.concatenate([span_forward, send(seen, stage)], axis=0)
    span_late = send(span_forward, stages - 1)
    spec = (tokens, page, group_size, head_size, orders)
    span_masks, page_masks = masks(prefix_len, block_owner, (span_layout, page_layout), spec)
    span_forward, span_masks, crossed = together(span_forward, span_masks, crossed)
    pages = [jnp.concatenate([own_page, crossed], axis=0)]
    pages.append(send(pages[0], 0))
    span_early, span_late = together(span_early, span_late)
    pages[1], span_late = together(pages[1], span_late)
    span = [jnp.concatenate([span_kv, span_forward, span_early, span_late], axis=0)]
    span_swapped = [swap_cores(span)]

    span_set = (span, span_swapped, span_masks)
    state = attend(span_query, 0, 1, [span_set], spec, None)

    for stage in range(1, stages - 1):
        pages.append(send(jnp.concatenate(pages, axis=0), stage))
    columns = span_kv.shape[1] // parts
    cuts = [slice(part * columns, (part + 1) * columns) for part in range(parts)]
    held = [jnp.concatenate([piece[:, cut] for piece in pages], axis=0) for cut in cuts]
    arrived = [send(rows, stages - 1) for rows in held]
    results = []
    for part in range(parts):
        arrived[part], state = together(arrived[part], state)
        mine = [held[part], arrived[part]]
        page_set = (mine, [swap_cores(mine)], page_masks)
        results.append(attend(span_query, part, parts, [span_set, page_set], spec, state))
    if head_size != 2:
        rows = jnp.concatenate([jnp.concatenate(pair, axis=0) for pair in results], axis=1)
        return lax.all_to_all(rows, "head", split_axis=0, concat_axis=1, tiled=True)
    kept = [pair[0] for pair in results]
    received = [lax.ppermute(pair[1], "head", [(0, 1), (1, 0)]) for pair in results]
    return put_together(kept, received)


def solution(mesh):
    placed = (P("seq", "head"), P("seq", "head"), P("seq", None, "head"), P(), P())
    return jax.shard_map(
        body, mesh=mesh, in_specs=placed, out_specs=P(("seq", "head"), None), check_vma=False
    )
```

```python
import functools
import math

import jax
import jax.numpy as jnp
from jax import lax
from jax.experimental import pallas as pl
from jax.experimental.pallas import tpu as pltpu
from jax.sharding import PartitionSpec as P

QH = 64
KVH = 8
HD = 128
REQS = 2
PER_GROUP = QH // KVH
EXP2_SCALE = HD ** (-0.5) * math.log2(math.e)
MASKED = -1e30
KEY_CHUNK = 512
HEADS_A_BLOCK = (2, 2, 2, 2)
SHIFT_STEP = 32.0
LOWEST_TOTAL = 1e-20
HIGHEST_TOTAL = 1e30
SPAN_ROWS, OWN_PAGE, CROSSED_PAGE = range(3)


def hop(value, bit_of_core):
    count = lax.axis_size("seq")
    return lax.ppermute(
        value, "seq", [(source, source ^ bit_of_core[source % 2]) for source in range(count)]
    )


def together(*values):
    return lax.optimization_barrier(values)


def shifted(layout, slots):
    return [(slot + slots, kind, rows) for slot, kind, rows in layout]


def hypercube_order(bits):
    order = [0]
    for bit in bits:
        order = order + [offset ^ bit for offset in order]
    return order


def mask_kernel(spec, layouts, limit_ref, owner_ref, *refs):
    tokens, page, group_size, _, orders = spec
    outs, page_seen = refs[:-1], refs[-1]
    me = lax.axis_index("seq")
    request = me // group_size
    offsets = [hypercube_order(order) for order in orders]

    def note_page(index, carry):
        page_seen[owner_ref[request, index]] = jnp.clip(limit_ref[request] - index * page, 0, page)
        return carry

    lax.fori_loop(0, owner_ref.shape[1], note_page, 0)
    for out, layout in zip(outs, layouts):
        start = 0
        for half in range(2):
            holder = me ^ half
            for slot, kind, rows in layout:
                source = holder ^ jnp.where(holder % 2 == 0, offsets[0][slot], offsets[1][slot])
                if kind == SPAN_ROWS:
                    count = jnp.where(source <= me, tokens, 0)
                elif kind == OWN_PAGE:
                    count = page_seen[source]
                else:
                    count = page_seen[source ^ group_size]
                row = lax.broadcasted_iota(jnp.int32, (rows, HD), 0)
                column = lax.broadcasted_iota(jnp.int32, (rows, HD), 1)
                mask = jnp.where(row < count, jnp.float32(0.0), jnp.float32(MASKED))
                one = jnp.where(column == 1, jnp.float32(1.0), jnp.float32(0.0))
                out[pl.ds(start, rows), :] = jnp.where(column == 0, mask, one).astype(jnp.bfloat16)
                start += rows


def masks(limits, owners, layouts, spec):
    scalars = pl.BlockSpec(memory_space=pltpu.SMEM)
    counts = [2 * sum(rows for _, _, rows in layout) for layout in layouts]
    return list(
        pl.pallas_call(
            functools.partial(mask_kernel, spec, layouts),
            out_shape=[jax.ShapeDtypeStruct((count, HD), jnp.bfloat16) for count in counts],
            in_specs=[scalars] * 2,
            out_specs=[pl.BlockSpec(memory_space=pltpu.VMEM)] * len(counts),
            scratch_shapes=[pltpu.SMEM((owners.shape[1],), jnp.int32)],
            compiler_params=pltpu.CompilerParams(vmem_limit_bytes=16 << 20),
        )(limits, owners)
    )


def attend_kernel(spec, sizes, part, groups, q_ref, *refs):
    tokens, _, _, head_size, _ = spec
    first_phase = len(sizes) == 1
    key_sets = []
    for counts in sizes:
        extra, refs = refs[0], refs[1:]
        halves = []
        for count in counts:
            halves.append(refs[:count])
            refs = refs[count:]
        key_sets.append((halves, extra))
    (state_sum, state_extra), refs = refs[:2], refs[2:]
    if first_phase:
        keys, values, weights = refs[0], refs[1], refs[2:4]
    else:
        outs, keys, values, weights = refs[:2], refs[2], refs[3], refs[4:6]
        slow_sum, slow_top = refs[6], refs[7]
    chunk = KEY_CHUNK
    my_head = lax.axis_index("head")

    def key_count(halves):
        return sum(ref.shape[0] for half in halves for ref in half)

    def fill(group, halves, extra):
        total_keys = key_count(halves)
        column = (part * groups + group) * 2 * HD
        start = 0
        for ref in [ref for half in halves for ref in half]:
            at = pl.ds(start, ref.shape[0])
            first = column % ref.shape[1]
            keys[group, at, :HD] = ref[:, pl.ds(first, HD)]
            values[group, at, :HD] = ref[:, pl.ds(first + HD, HD)]
            start += ref.shape[0]
        keys[group, :total_keys, HD:] = extra[...]
        values[group, :total_keys, HD:] = jnp.ones((total_keys, HD), jnp.bfloat16)

    def lane_of(heads):
        return lax.broadcasted_iota(jnp.int32, (heads * tokens, HD), 1)

    def query_rows(first, heads):
        at = part * groups * PER_GROUP + first
        columns = [pl.ds(pl.multiple_of((at + head) * HD, HD), HD) for head in range(heads)]
        return jnp.concatenate([q_ref[:, column] for column in columns], axis=0)

    def scores_of(query, group, start, is_span):
        made = lax.dot_general(
            query,
            keys[group, pl.ds(start, chunk), :],
            (((1,), (1,)), ((), ())),
            preferred_element_type=jnp.float32,
        )
        if start == 0 and is_span:
            rows = query.shape[0]
            causal = lax.broadcasted_iota(jnp.int32, (rows, tokens), 1) <= (
                lax.broadcasted_iota(jnp.int32, (rows, tokens), 0) % tokens
            )
            own = jnp.where(causal, made[:, :tokens], MASKED)
            made = jnp.concatenate([own, made[:, tokens:]], axis=1)
        return made

    def give(first, heads, result):
        kept = tokens // head_size
        for head in range(heads):
            column = pl.ds((first + head) * HD, HD)
            one = result[head * tokens : (head + 1) * tokens]
            if head_size == 2:
                low, high = one[:kept], one[kept:]
                outs[0][:, column] = jnp.where(my_head == 0, low, high)
                outs[1][:, column] = jnp.where(my_head == 0, high, low)
            else:
                outs[0][:, column] = one[:kept]
                outs[1][:, column] = one[kept:]

    halves, extra_ref = key_sets[-1]
    total_keys = key_count(halves)
    longest = [None] * groups

    def begin(group):
        fill(group, halves, extra_ref)
        if first_phase:
            key = keys[group, :total_keys, :HD].astype(jnp.float32)
            squares = jnp.sum(key * key, axis=1, keepdims=True)
            longest[group] = jnp.max(squares, axis=0, keepdims=True)

    def weigh(index):
        group, first, heads = blocks[index]
        rows = pl.ds(first * tokens, heads * tokens)
        query = query_rows(first, heads)
        if first_phase:
            wide = query.astype(jnp.float32)
            bound = jnp.sqrt(jnp.sum(wide * wide, axis=1, keepdims=True) * longest[group])
            shift = jnp.ceil(bound * (1.0 / SHIFT_STEP)) * SHIFT_STEP
            lane = lane_of(heads)
            extra = jnp.where(lane == 0, 1.0, jnp.where(lane == 1, -shift, 0.0))
            extra = extra.astype(jnp.bfloat16)
            state_extra[rows, :] = extra
        else:
            extra = state_extra[pl.ds((part * groups * PER_GROUP + first) * tokens, heads * tokens), :]
        query = jnp.concatenate([query, extra], axis=1)
        for start in range(0, total_keys, chunk):
            made = scores_of(query, group, start, first_phase)
            weights[index % 2][: heads * tokens, pl.ds(start, chunk)] = jnp.exp2(
                made * EXP2_SCALE
            ).astype(jnp.bfloat16)

    def finish(index, extremes):
        group, first, heads = blocks[index]
        summed = jnp.dot(
            weights[index % 2][: heads * tokens, :total_keys],
            values[group, :total_keys, :],
            preferred_element_type=jnp.float32,
        )
        if first_phase:
            state_sum[pl.ds(first * tokens, heads * tokens), :] = summed
            return extremes
        old = pl.ds((part * groups * PER_GROUP + first) * tokens, heads * tokens)
        summed = summed + state_sum[old, :]
        total = summed[:, HD:]
        give(first, heads, (summed[:, :HD] / total).astype(jnp.bfloat16))
        lowest, highest = extremes
        for head in range(heads):
            one = total[head * tokens : (head + 1) * tokens]
            lowest, highest = jnp.minimum(lowest, one), jnp.maximum(highest, one)
        return lowest, highest

    blocks = []
    for group in range(groups):
        at = group * PER_GROUP
        for heads in HEADS_A_BLOCK:
            blocks.append((group, at, heads))
            at += heads
    begin(0)
    extremes = (jnp.ones((tokens, HD), jnp.float32),) * 2
    for index in range(len(blocks) + 1):
        if index >= 1:
            extremes = finish(index - 1, extremes)
        if index < len(blocks):
            weigh(index)
            if index + 1 < len(blocks) and blocks[index + 1][0] != blocks[index][0]:
                begin(blocks[index + 1][0])
    if first_phase:
        return

    @pl.when((jnp.min(extremes[0]) < LOWEST_TOTAL) | (jnp.max(extremes[1]) > HIGHEST_TOTAL))
    def exact():
        heads = 4
        block = heads * tokens
        count = groups * PER_GROUP // heads
        for number, (halves, extra_ref) in enumerate(key_sets):
            for group in range(groups):
                fill(group, halves, extra_ref)

            def one_block(index, carry):
                group = index * heads // PER_GROUP
                extra = (lane_of(heads) == 0).astype(jnp.float32).astype(jnp.bfloat16)
                query = jnp.concatenate([query_rows(index * heads, heads), extra], axis=1)
                rows = pl.ds(pl.multiple_of(index * block, block), block)
                if number == 0:
                    top = jnp.full((block, HD), MASKED, jnp.float32)
                    summed = jnp.zeros((block, 2 * HD), jnp.float32)
                else:
                    top = slow_top[rows, :]
                    summed = slow_sum[rows, :]
                best = top
                for start in range(0, key_count(halves), chunk):
                    made = scores_of(query, group, start, number == 0)
                    for at in range(0, chunk, HD):
                        best = jnp.maximum(best, made[:, at : at + HD])
                best = jnp.broadcast_to(jnp.max(best, axis=1, keepdims=True), (block, HD))
                fade = jnp.exp2((top - best) * EXP2_SCALE)
                summed = summed * jnp.concatenate([fade, fade], axis=1)
                for start in range(0, key_count(halves), chunk):
                    made = scores_of(query, group, start, number == 0)
                    parts = [
                        jnp.exp2((made[:, at : at + HD] - best) * EXP2_SCALE)
                        for at in range(0, chunk, HD)
                    ]
                    summed = summed + jnp.dot(
                        jnp.concatenate(parts, axis=1).astype(jnp.bfloat16),
                        values[group, pl.ds(start, chunk), :],
                        preferred_element_type=jnp.float32,
                    )
                slow_top[rows, :] = best
                slow_sum[rows, :] = summed
                return carry

            lax.fori_loop(0, count, one_block, 0)
        for index in range(count):
            rows = pl.ds(index * block, block)
            result = (slow_sum[rows, :HD] / slow_sum[rows, HD:]).astype(jnp.bfloat16)
            give(index * heads, heads, result)


def attend(queries, part, parts, key_sets, spec, state):
    tokens, _, _, head_size = spec[:4]
    total_keys = max(extra.shape[0] for _, _, extra in key_sets)
    columns = queries.shape[1] // parts
    groups = columns // (PER_GROUP * HD)
    block = max(HEADS_A_BLOCK) * tokens
    rows = PER_GROUP * groups * tokens
    pieces = [piece for mine, theirs, extra in key_sets for piece in [extra] + mine + theirs]
    sizes = tuple((len(mine), len(theirs)) for mine, theirs, _ in key_sets)
    operands = queries.size * 2 + sum(piece.size for piece in pieces) * 2 + rows * HD * 12
    scratch = groups * total_keys * HD * 8 + block * total_keys * 4 + rows * HD * 12
    whole = pl.BlockSpec(memory_space=pltpu.VMEM)
    kept = tokens // head_size
    scratch_shapes = [pltpu.VMEM((groups, total_keys, 2 * HD), jnp.bfloat16)] * 2
    scratch_shapes += [pltpu.VMEM((block, total_keys), jnp.bfloat16)] * 2
    if state is None:
        state = ()
        out_shape = [
            jax.ShapeDtypeStruct((rows, 2 * HD), jnp.float32),
            jax.ShapeDtypeStruct((rows, HD), jnp.bfloat16),
        ]
    else:
        out_shape = [
            jax.ShapeDtypeStruct((kept, columns), jnp.bfloat16),
            jax.ShapeDtypeStruct((tokens - kept, columns), jnp.bfloat16),
        ]
        scratch_shapes += [
            pltpu.VMEM((rows, 2 * HD), jnp.float32),
            pltpu.VMEM((rows, HD), jnp.float32),
        ]
    return pl.pallas_call(
        functools.partial(attend_kernel, spec, sizes, part, groups),
        out_shape=out_shape,
        in_specs=[whole] * (1 + len(pieces) + len(state)),
        out_specs=[whole] * 2,
        scratch_shapes=scratch_shapes,
        compiler_params=pltpu.CompilerParams(vmem_limit_bytes=operands + scratch + (8 << 20)),
        cost_estimate=pl.CostEstimate(
            flops=8 * tokens * columns * total_keys,
            bytes_accessed=4 * tokens * columns + 2 * total_keys * columns // PER_GROUP,
            transcendentals=0,
        ),
    )(queries, *pieces, *state)


def pick_kernel(group_size, cache_ref, other_ref, own_ref):
    request = lax.axis_index("seq") // group_size
    other_ref[...] = cache_ref[1 - request]
    own_ref[...] = cache_ref[request]


def pick(cache, group_size):
    whole = pl.BlockSpec(memory_space=pltpu.VMEM)
    return pl.pallas_call(
        functools.partial(pick_kernel, group_size),
        out_shape=[jax.ShapeDtypeStruct(cache.shape[1:], cache.dtype)] * 2,
        in_specs=[whole],
        out_specs=[whole] * 2,
        compiler_params=pltpu.CompilerParams(vmem_limit_bytes=8 << 20),
    )(cache)


def join_kernel(spots, count, *refs):
    parts, (out_ref, done) = refs[len(refs) - 2 - count : -2], refs[-2:]
    side = out_ref.shape[1] // 2
    my_head = lax.axis_index("head")
    copies = []
    for at, (ref, (received, start)) in enumerate(zip(parts, spots)):
        owner = 1 - my_head if received else my_head
        first = pl.multiple_of(owner * side + start, HD)
        copies.append(
            pltpu.make_async_copy(ref, out_ref.at[:, pl.ds(first, ref.shape[1])], done.at[at])
        )
    for copy in copies:
        copy.start()
    for copy in copies:
        copy.wait()


def join(pieces, spots, columns, partial):
    earlier = [] if partial is None else [partial]
    return pl.pallas_call(
        functools.partial(join_kernel, spots, len(pieces)),
        out_shape=jax.ShapeDtypeStruct((pieces[0].shape[0], columns), pieces[0].dtype),
        in_specs=[pl.BlockSpec(memory_space=pl.ANY)] * len(earlier)
        + [pl.BlockSpec(memory_space=pltpu.VMEM)] * len(pieces),
        out_specs=pl.BlockSpec(memory_space=pl.ANY),
        scratch_shapes=[pltpu.SemaphoreType.DMA((len(pieces),))],
        input_output_aliases={0: 0} if earlier else {},
        compiler_params=pltpu.CompilerParams(vmem_limit_bytes=8 << 20),
    )(*earlier, *pieces)


def put_together(kept, received):
    columns = kept[0].shape[1]
    pieces = kept + received
    spots = [(at >= len(kept), at % len(kept) * columns) for at in range(len(pieces))]
    out = join(pieces[:-1], spots[:-1], columns * len(pieces), None)
    return join(pieces[-1:], spots[-1:], columns * len(pieces), out)


def body(span_query, span_kv, prefix_cache, prefix_len, block_owner):
    seq_size = lax.axis_size("seq")
    head_size = lax.axis_size("head")
    group_size = seq_size // REQS
    tokens = span_kv.shape[0]
    page = prefix_cache.shape[1]
    groups = span_kv.shape[1] // (2 * HD)
    parts = 2 if groups % 2 == 0 else 1
    bits = [1 << at for at in range(1, group_size.bit_length() - 1)]
    orders = (bits, bits[::-1])

    stages = len(bits)

    def send(rows, stage):
        return hop(rows, tuple(order[stage] for order in orders))

    def swap_cores(pieces):
        return hop(pieces[0] if len(pieces) == 1 else jnp.concatenate(pieces, axis=0), (1, 1))

    def whole_layout(layout):
        for stage in range(stages):
            layout = layout + shifted(layout, 1 << stage)
        return layout

    span_layout = whole_layout([(0, SPAN_ROWS, tokens)])
    page_layout = whole_layout([(0, OWN_PAGE, page), (0, CROSSED_PAGE, page)])

    other_page, own_page = pick(prefix_cache, group_size)
    crossed = hop(other_page, (group_size, group_size))

    span_early = send(span_kv, stages - 1)
    span_forward = send(span_kv, 0)
    for stage in range(1, stages - 1):
        seen = jnp.concatenate([span_kv, span_forward], axis=0)
        span_forward = jnp.concatenate([span_forward, send(seen, stage)], axis=0)
    span_late = send(span_forward, stages - 1)
    spec = (tokens, page, group_size, head_size, orders)
    span_masks, page_masks = masks(prefix_len, block_owner, (span_layout, page_layout), spec)
    span_forward, span_masks, crossed = together(span_forward, span_masks, crossed)
    pages = [jnp.concatenate([own_page, crossed], axis=0)]
    pages.append(send(pages[0], 0))
    near = jnp.concatenate([span_kv, span_forward, span_early], axis=0)
    pages[1], span_late = together(pages[1], span_late)
    span = [near, span_late]
    span_swapped = [swap_cores(span[:1]), swap_cores(span[1:])]

    span_set = (span, span_swapped, span_masks)
    state = attend(span_query, 0, 1, [span_set], spec, None)

    for stage in range(1, stages - 1):
        pages.append(send(jnp.concatenate(pages, axis=0), stage))
    columns = span_kv.shape[1] // parts
    cuts = [slice(part * columns, (part + 1) * columns) for part in range(parts)]
    held = [jnp.concatenate([piece[:, cut] for piece in pages], axis=0) for cut in cuts]
    arrived = [send(rows, stages - 1) for rows in held]
    results = []
    for part in range(parts):
        arrived[part], state = together(arrived[part], state)
        mine = [held[part], arrived[part]]
        page_set = (mine, [swap_cores(mine)], page_masks)
        results.append(attend(span_query, part, parts, [span_set, page_set], spec, state))
    if head_size != 2:
        rows = jnp.concatenate([jnp.concatenate(pair, axis=0) for pair in results], axis=1)
        return lax.all_to_all(rows, "head", split_axis=0, concat_axis=1, tiled=True)
    kept = [pair[0] for pair in results]
    received = [lax.ppermute(pair[1], "head", [(0, 1), (1, 0)]) for pair in results]
    return put_together(kept, received)


def solution(mesh):
    placed = (P("seq", "head"), P("seq", "head"), P("seq", None, "head"), P(), P())
    return jax.shard_map(
        body, mesh=mesh, in_specs=placed, out_specs=P(("seq", "head"), None), check_vma=False
    )
```

```python
import functools
import math

import jax
import jax.numpy as jnp
from jax import lax
from jax.experimental import pallas as pl
from jax.experimental.pallas import tpu as pltpu
from jax.sharding import PartitionSpec as P

QH = 64
KVH = 8
HD = 128
REQS = 2
PER_GROUP = QH // KVH
EXP2_SCALE = HD ** (-0.5) * math.log2(math.e)
MASKED = -1e30
KEY_CHUNK = 512
HEADS_A_BLOCK = (2, 2, 2, 2)
SHIFT_STEP = 32.0
LOWEST_TOTAL = 1e-20
HIGHEST_TOTAL = 1e30
SPAN_ROWS, OWN_PAGE, CROSSED_PAGE = range(3)


def hop(value, bit_of_core):
    count = lax.axis_size("seq")
    return lax.ppermute(
        value, "seq", [(source, source ^ bit_of_core[source % 2]) for source in range(count)]
    )


def together(*values):
    return lax.optimization_barrier(values)


def shifted(layout, slots):
    return [(slot + slots, kind, rows) for slot, kind, rows in layout]


def hypercube_order(bits):
    order = [0]
    for bit in bits:
        order = order + [offset ^ bit for offset in order]
    return order


def mask_kernel(spec, layouts, limit_ref, owner_ref, *refs):
    tokens, page, group_size, _, orders = spec
    outs, page_seen = refs[:-1], refs[-1]
    me = lax.axis_index("seq")
    request = me // group_size
    offsets = [hypercube_order(order) for order in orders]

    def note_page(index, carry):
        page_seen[owner_ref[request, index]] = jnp.clip(limit_ref[request] - index * page, 0, page)
        return carry

    lax.fori_loop(0, owner_ref.shape[1], note_page, 0)
    for out, layout in zip(outs, layouts):
        start = 0
        for half in range(2):
            holder = me ^ half
            for slot, kind, rows in layout:
                source = holder ^ jnp.where(holder % 2 == 0, offsets[0][slot], offsets[1][slot])
                if kind == SPAN_ROWS:
                    count = jnp.where(source <= me, tokens, 0)
                elif kind == OWN_PAGE:
                    count = page_seen[source]
                else:
                    count = page_seen[source ^ group_size]
                row = lax.broadcasted_iota(jnp.int32, (rows, HD), 0)
                column = lax.broadcasted_iota(jnp.int32, (rows, HD), 1)
                mask = jnp.where(row < count, jnp.float32(0.0), jnp.float32(MASKED))
                one = jnp.where(column == 1, jnp.float32(1.0), jnp.float32(0.0))
                out[pl.ds(start, rows), :] = jnp.where(column == 0, mask, one).astype(jnp.bfloat16)
                start += rows


def masks(limits, owners, layouts, spec):
    scalars = pl.BlockSpec(memory_space=pltpu.SMEM)
    counts = [2 * sum(rows for _, _, rows in layout) for layout in layouts]
    return list(
        pl.pallas_call(
            functools.partial(mask_kernel, spec, layouts),
            out_shape=[jax.ShapeDtypeStruct((count, HD), jnp.bfloat16) for count in counts],
            in_specs=[scalars] * 2,
            out_specs=[pl.BlockSpec(memory_space=pltpu.VMEM)] * len(counts),
            scratch_shapes=[pltpu.SMEM((owners.shape[1],), jnp.int32)],
            compiler_params=pltpu.CompilerParams(vmem_limit_bytes=16 << 20),
        )(limits, owners)
    )


def attend_kernel(spec, sizes, part, groups, q_ref, *refs):
    tokens, _, _, head_size, _ = spec
    first_phase = len(sizes) == 1
    key_sets = []
    for counts in sizes:
        extra, refs = refs[0], refs[1:]
        halves = []
        for count in counts:
            halves.append(refs[:count])
            refs = refs[count:]
        key_sets.append((halves, extra))
    (state_sum, state_extra), refs = refs[:2], refs[2:]
    if first_phase:
        keys, values, weights = refs[0], refs[1], refs[2:4]
    else:
        outs, keys, values, weights = refs[:2], refs[2], refs[3], refs[4:6]
        slow_sum, slow_top = refs[6], refs[7]
    chunk = KEY_CHUNK
    my_head = lax.axis_index("head")

    def key_count(halves):
        return sum(ref.shape[0] for half in halves for ref in half)

    def fill(group, halves, extra):
        total_keys = key_count(halves)
        column = (part * groups + group) * 2 * HD
        start = 0
        for ref in [ref for half in halves for ref in half]:
            at = pl.ds(start, ref.shape[0])
            first = column % ref.shape[1]
            keys[group, at, :HD] = ref[:, pl.ds(first, HD)]
            values[group, at, :HD] = ref[:, pl.ds(first + HD, HD)]
            start += ref.shape[0]
        keys[group, :total_keys, HD:] = extra[...]
        values[group, :total_keys, HD:] = jnp.ones((total_keys, HD), jnp.bfloat16)

    def lane_of(heads):
        return lax.broadcasted_iota(jnp.int32, (heads * tokens, HD), 1)

    def query_rows(first, heads):
        at = part * groups * PER_GROUP + first
        columns = [pl.ds(pl.multiple_of((at + head) * HD, HD), HD) for head in range(heads)]
        return jnp.concatenate([q_ref[:, column] for column in columns], axis=0)

    def scores_of(query, group, start, is_span):
        made = lax.dot_general(
            query,
            keys[group, pl.ds(start, chunk), :],
            (((1,), (1,)), ((), ())),
            preferred_element_type=jnp.float32,
        )
        if start == 0 and is_span:
            rows = query.shape[0]
            causal = lax.broadcasted_iota(jnp.int32, (rows, tokens), 1) <= (
                lax.broadcasted_iota(jnp.int32, (rows, tokens), 0) % tokens
            )
            own = jnp.where(causal, made[:, :tokens], MASKED)
            made = jnp.concatenate([own, made[:, tokens:]], axis=1)
        return made

    def give(first, heads, result):
        kept = tokens // head_size
        for head in range(heads):
            column = pl.ds((first + head) * HD, HD)
            one = result[head * tokens : (head + 1) * tokens]
            if head_size == 2:
                low, high = one[:kept], one[kept:]
                outs[0][:, column] = jnp.where(my_head == 0, low, high)
                outs[1][:, column] = jnp.where(my_head == 0, high, low)
            else:
                outs[0][:, column] = one[:kept]
                outs[1][:, column] = one[kept:]

    halves, extra_ref = key_sets[-1]
    total_keys = key_count(halves)
    longest = [None] * groups

    def begin(group):
        fill(group, halves, extra_ref)
        if first_phase:
            key = keys[group, :total_keys, :HD].astype(jnp.float32)
            squares = jnp.sum(key * key, axis=1, keepdims=True)
            longest[group] = jnp.max(squares, axis=0, keepdims=True)

    def weigh(index):
        group, first, heads = blocks[index]
        rows = pl.ds(first * tokens, heads * tokens)
        query = query_rows(first, heads)
        if first_phase:
            wide = query.astype(jnp.float32)
            bound = jnp.sqrt(jnp.sum(wide * wide, axis=1, keepdims=True) * longest[group])
            shift = jnp.ceil(bound * (1.0 / SHIFT_STEP)) * SHIFT_STEP
            lane = lane_of(heads)
            extra = jnp.where(lane == 0, 1.0, jnp.where(lane == 1, -shift, 0.0))
            extra = extra.astype(jnp.bfloat16)
            state_extra[rows, :] = extra
        else:
            extra = state_extra[pl.ds((part * groups * PER_GROUP + first) * tokens, heads * tokens), :]
        query = jnp.concatenate([query, extra], axis=1)
        for start in range(0, total_keys, chunk):
            made = scores_of(query, group, start, first_phase)
            weights[index % 2][: heads * tokens, pl.ds(start, chunk)] = jnp.exp2(
                made * EXP2_SCALE
            ).astype(jnp.bfloat16)

    def finish(index, extremes):
        group, first, heads = blocks[index]
        summed = jnp.dot(
            weights[index % 2][: heads * tokens, :total_keys],
            values[group, :total_keys, :],
            preferred_element_type=jnp.float32,
        )
        if first_phase:
            state_sum[pl.ds(first * tokens, heads * tokens), :] = summed
            return extremes
        old = pl.ds((part * groups * PER_GROUP + first) * tokens, heads * tokens)
        summed = summed + state_sum[old, :]
        total = summed[:, HD:]
        give(first, heads, (summed[:, :HD] / total).astype(jnp.bfloat16))
        lowest, highest = extremes
        for head in range(heads):
            one = total[head * tokens : (head + 1) * tokens]
            lowest, highest = jnp.minimum(lowest, one), jnp.maximum(highest, one)
        return lowest, highest

    blocks = []
    for group in range(groups):
        at = group * PER_GROUP
        for heads in HEADS_A_BLOCK:
            blocks.append((group, at, heads))
            at += heads
    begin(0)
    extremes = (jnp.ones((tokens, HD), jnp.float32),) * 2
    for index in range(len(blocks) + 1):
        if index >= 1:
            extremes = finish(index - 1, extremes)
        if index < len(blocks):
            weigh(index)
            if index + 1 < len(blocks) and blocks[index + 1][0] != blocks[index][0]:
                begin(blocks[index + 1][0])
    if first_phase:
        return

    @pl.when((jnp.min(extremes[0]) < LOWEST_TOTAL) | (jnp.max(extremes[1]) > HIGHEST_TOTAL))
    def exact():
        heads = 4
        block = heads * tokens
        count = groups * PER_GROUP // heads
        for number, (halves, extra_ref) in enumerate(key_sets):
            for group in range(groups):
                fill(group, halves, extra_ref)

            def one_block(index, carry):
                group = index * heads // PER_GROUP
                extra = (lane_of(heads) == 0).astype(jnp.float32).astype(jnp.bfloat16)
                query = jnp.concatenate([query_rows(index * heads, heads), extra], axis=1)
                rows = pl.ds(pl.multiple_of(index * block, block), block)
                if number == 0:
                    top = jnp.full((block, HD), MASKED, jnp.float32)
                    summed = jnp.zeros((block, 2 * HD), jnp.float32)
                else:
                    top = slow_top[rows, :]
                    summed = slow_sum[rows, :]
                best = top
                for start in range(0, key_count(halves), chunk):
                    made = scores_of(query, group, start, number == 0)
                    for at in range(0, chunk, HD):
                        best = jnp.maximum(best, made[:, at : at + HD])
                best = jnp.broadcast_to(jnp.max(best, axis=1, keepdims=True), (block, HD))
                fade = jnp.exp2((top - best) * EXP2_SCALE)
                summed = summed * jnp.concatenate([fade, fade], axis=1)
                for start in range(0, key_count(halves), chunk):
                    made = scores_of(query, group, start, number == 0)
                    parts = [
                        jnp.exp2((made[:, at : at + HD] - best) * EXP2_SCALE)
                        for at in range(0, chunk, HD)
                    ]
                    summed = summed + jnp.dot(
                        jnp.concatenate(parts, axis=1).astype(jnp.bfloat16),
                        values[group, pl.ds(start, chunk), :],
                        preferred_element_type=jnp.float32,
                    )
                slow_top[rows, :] = best
                slow_sum[rows, :] = summed
                return carry

            lax.fori_loop(0, count, one_block, 0)
        for index in range(count):
            rows = pl.ds(index * block, block)
            result = (slow_sum[rows, :HD] / slow_sum[rows, HD:]).astype(jnp.bfloat16)
            give(index * heads, heads, result)


def attend(queries, part, parts, key_sets, spec, state):
    tokens, _, _, head_size = spec[:4]
    total_keys = max(extra.shape[0] for _, _, extra in key_sets)
    columns = queries.shape[1] // parts
    groups = columns // (PER_GROUP * HD)
    block = max(HEADS_A_BLOCK) * tokens
    rows = PER_GROUP * groups * tokens
    pieces = [piece for mine, theirs, extra in key_sets for piece in [extra] + mine + theirs]
    sizes = tuple((len(mine), len(theirs)) for mine, theirs, _ in key_sets)
    operands = queries.size * 2 + sum(piece.size for piece in pieces) * 2 + rows * HD * 12
    scratch = groups * total_keys * HD * 8 + block * total_keys * 4 + rows * HD * 12
    whole = pl.BlockSpec(memory_space=pltpu.VMEM)
    kept = tokens // head_size
    scratch_shapes = [pltpu.VMEM((groups, total_keys, 2 * HD), jnp.bfloat16)] * 2
    scratch_shapes += [pltpu.VMEM((block, total_keys), jnp.bfloat16)] * 2
    if state is None:
        state = ()
        out_shape = [
            jax.ShapeDtypeStruct((rows, 2 * HD), jnp.float32),
            jax.ShapeDtypeStruct((rows, HD), jnp.bfloat16),
        ]
    else:
        out_shape = [
            jax.ShapeDtypeStruct((kept, columns), jnp.bfloat16),
            jax.ShapeDtypeStruct((tokens - kept, columns), jnp.bfloat16),
        ]
        scratch_shapes += [
            pltpu.VMEM((rows, 2 * HD), jnp.float32),
            pltpu.VMEM((rows, HD), jnp.float32),
        ]
    return pl.pallas_call(
        functools.partial(attend_kernel, spec, sizes, part, groups),
        out_shape=out_shape,
        in_specs=[whole] * (1 + len(pieces) + len(state)),
        out_specs=[whole] * 2,
        scratch_shapes=scratch_shapes,
        compiler_params=pltpu.CompilerParams(vmem_limit_bytes=operands + scratch + (8 << 20)),
        cost_estimate=pl.CostEstimate(
            flops=8 * tokens * columns * total_keys,
            bytes_accessed=4 * tokens * columns + 2 * total_keys * columns // PER_GROUP,
            transcendentals=0,
        ),
    )(queries, *pieces, *state)


def pick_kernel(group_size, cache_ref, other_ref, own_ref):
    request = lax.axis_index("seq") // group_size
    other_ref[...] = cache_ref[1 - request]
    own_ref[...] = cache_ref[request]


def pick(cache, group_size):
    whole = pl.BlockSpec(memory_space=pltpu.VMEM)
    return pl.pallas_call(
        functools.partial(pick_kernel, group_size),
        out_shape=[jax.ShapeDtypeStruct(cache.shape[1:], cache.dtype)] * 2,
        in_specs=[whole],
        out_specs=[whole] * 2,
        compiler_params=pltpu.CompilerParams(vmem_limit_bytes=8 << 20),
    )(cache)


def join_kernel(spots, count, *refs):
    parts, (out_ref, done) = refs[len(refs) - 2 - count : -2], refs[-2:]
    side = out_ref.shape[1] // 2
    my_head = lax.axis_index("head")
    copies = []
    for at, (ref, (received, start)) in enumerate(zip(parts, spots)):
        owner = 1 - my_head if received else my_head
        first = pl.multiple_of(owner * side + start, HD)
        copies.append(
            pltpu.make_async_copy(ref, out_ref.at[:, pl.ds(first, ref.shape[1])], done.at[at])
        )
    for copy in copies:
        copy.start()
    for copy in copies:
        copy.wait()


def join(pieces, spots, columns, partial):
    earlier = [] if partial is None else [partial]
    return pl.pallas_call(
        functools.partial(join_kernel, spots, len(pieces)),
        out_shape=jax.ShapeDtypeStruct((pieces[0].shape[0], columns), pieces[0].dtype),
        in_specs=[pl.BlockSpec(memory_space=pl.ANY)] * len(earlier)
        + [pl.BlockSpec(memory_space=pltpu.VMEM)] * len(pieces),
        out_specs=pl.BlockSpec(memory_space=pl.ANY),
        scratch_shapes=[pltpu.SemaphoreType.DMA((len(pieces),))],
        input_output_aliases={0: 0} if earlier else {},
        compiler_params=pltpu.CompilerParams(vmem_limit_bytes=8 << 20),
    )(*earlier, *pieces)


def put_together(kept, received):
    columns = kept[0].shape[1]
    pieces = kept + received
    spots = [(at >= len(kept), at % len(kept) * columns) for at in range(len(pieces))]
    out = join(pieces[:-1], spots[:-1], columns * len(pieces), None)
    return join(pieces[-1:], spots[-1:], columns * len(pieces), out)


def body(span_query, span_kv, prefix_cache, prefix_len, block_owner):
    seq_size = lax.axis_size("seq")
    head_size = lax.axis_size("head")
    group_size = seq_size // REQS
    tokens = span_kv.shape[0]
    page = prefix_cache.shape[1]
    groups = span_kv.shape[1] // (2 * HD)
    parts = 2 if groups % 2 == 0 else 1
    bits = [1 << at for at in range(1, group_size.bit_length() - 1)]
    orders = (bits, bits[::-1])

    stages = len(bits)

    def send(rows, stage):
        return hop(rows, tuple(order[stage] for order in orders))

    def swap_cores(pieces):
        return hop(pieces[0] if len(pieces) == 1 else jnp.concatenate(pieces, axis=0), (1, 1))

    def whole_layout(layout):
        for stage in range(stages):
            layout = layout + shifted(layout, 1 << stage)
        return layout

    span_layout = whole_layout([(0, SPAN_ROWS, tokens)])
    page_layout = whole_layout([(0, OWN_PAGE, page), (0, CROSSED_PAGE, page)])

    other_page, own_page = pick(prefix_cache, group_size)
    crossed = hop(other_page, (group_size, group_size))

    span_early = send(span_kv, stages - 1)
    span_forward = send(span_kv, 0)
    for stage in range(1, stages - 1):
        seen = jnp.concatenate([span_kv, span_forward], axis=0)
        span_forward = jnp.concatenate([span_forward, send(seen, stage)], axis=0)
    span_late = send(span_forward, stages - 1)
    spec = (tokens, page, group_size, head_size, orders)
    span_masks, page_masks = masks(prefix_len, block_owner, (span_layout, page_layout), spec)
    span_forward, span_masks, crossed = together(span_forward, span_masks, crossed)
    pages = [jnp.concatenate([own_page, crossed], axis=0)]
    pages.append(send(pages[0], 0))
    span_early, span_late = together(span_early, span_late)
    pages[1], span_late = together(pages[1], span_late)
    span = [jnp.concatenate([span_kv, span_forward, span_early, span_late], axis=0)]
    span_swapped = [swap_cores(span)]

    span_set = (span, span_swapped, span_masks)
    state = attend(span_query, 0, 1, [span_set], spec, None)

    for stage in range(1, stages - 1):
        pages.append(send(jnp.concatenate(pages, axis=0), stage))
    columns = span_kv.shape[1] // parts
    cuts = [slice(part * columns, (part + 1) * columns) for part in range(parts)]
    held = [jnp.concatenate([piece[:, cut] for piece in pages], axis=0) for cut in cuts]
    arrived = [send(rows, stages - 1) for rows in held]
    results = []
    for part in range(parts):
        if part:
            first_kept, arrived[part] = together(results[-1][0], arrived[part])
            results[-1] = (first_kept, results[-1][1])
        else:
            arrived[part], state = together(arrived[part], state)
        mine = [held[part], arrived[part]]
        page_set = (mine, [swap_cores(mine)], page_masks)
        results.append(attend(span_query, part, parts, [span_set, page_set], spec, state))
    if head_size != 2:
        rows = jnp.concatenate([jnp.concatenate(pair, axis=0) for pair in results], axis=1)
        return lax.all_to_all(rows, "head", split_axis=0, concat_axis=1, tiled=True)
    kept = [pair[0] for pair in results]
    received = [lax.ppermute(pair[1], "head", [(0, 1), (1, 0)]) for pair in results]
    return put_together(kept, received)


def solution(mesh):
    placed = (P("seq", "head"), P("seq", "head"), P("seq", None, "head"), P(), P())
    return jax.shard_map(
        body, mesh=mesh, in_specs=placed, out_specs=P(("seq", "head"), None), check_vma=False
    )
```
